256 devices in a mesh: dx: 16 (over y, x), dy: 16 (over z, core).
Axes of the slice: x: 4, y: 4, z: 8, core: 2. Of those that a mesh axis runs over, the one named last changes fastest.
Arguments:
- volume_fraction: float32 [512, 512, 128], P('dx', 'dy'), may hold values from 0 to 1
- vorticity: float32 [512, 512, 128], P('dx', 'dy'), may hold values from 0.05 to 20
Outputs:
- volume_coeffs: float32 [512, 512, 128], P('dx', 'dy')
- vorticity_coeffs: float32 [512, 512, 128], P('dx', 'dy')
The draws below stay inside these ranges and needn't reach their ends.
All inputs are finite; a program needn't handle non-finite values.
Results may differ from the reference program's by a relative error of at most 0.00012.
Values sent between devices are 32-bit elements; how exact they have to be, the bound alone decides.
A program may use at most 64 MiB of HBM per device.

```python
import math
import jax
import jax.numpy as jnp
from jax import lax

NZ = 128
LEVELS = 3
NX = 512
NY = 512


def block_scale(rng, shape, pieces, least, largest):
    loudness, own = 1.0, jax.random.fold_in(rng, 6)
    for axis_at, shards_of in pieces:
        heights = jnp.exp(jax.random.uniform(jax.random.fold_in(own, axis_at), (shards_of,), jnp.float32, least / len(pieces), largest / len(pieces)))
        loudness = loudness * jnp.repeat(heights, shape[axis_at] // shards_of).reshape([-1 if axis == axis_at else 1 for axis in range(len(shape))])
    return loudness


def setup_inputs(seed: int = 0) -> dict:
    arg_keys = jax.random.split(jax.random.key(seed), 3)
    return {
        "volume_fraction": jnp.clip(1.0 * jax.random.uniform(arg_keys[0], (NX, NY, NZ), jnp.float32) ** block_scale(arg_keys[0], (NX, NY, NZ), ((0, 16), (1, 16)), -0.2, 0.2), 0.0, 1.0),
        "vorticity": jnp.clip(jnp.exp(math.log(20.0) - 5.9914645 * jax.random.uniform(arg_keys[1], (NX, NY, NZ), jnp.float32) ** block_scale(arg_keys[1], (NX, NY, NZ), ((0, 16), (1, 16)), -0.2, 0.2)), 0.05, 20.0),
    }


LIFT_ALPHA = -1.586134342
LIFT_BETA = -0.05298011854
LIFT_GAMMA = 0.8829110762
LIFT_DELTA = 0.4435068522
LIFT_KAPPA = 1.149604398


def split_pairs(field, along):
    count = field.shape[along]
    paired = field.reshape(field.shape[:along] + (count // 2, 2) + field.shape[along + 1:])
    return lax.index_in_dim(paired, 0, along + 1, False), lax.index_in_dim(paired, 1, along + 1, False)


def join_pairs(even_part, odd_part, along):
    joined = jnp.stack([even_part, odd_part], along + 1)
    shape = list(even_part.shape)
    shape[along] = shape[along] * 2
    return joined.reshape(tuple(shape))


def lift_core(even_part, odd_part, next_fn, prev_fn):
    odd_part = odd_part + LIFT_ALPHA * (even_part + next_fn(even_part))
    even_part = even_part + LIFT_BETA * (prev_fn(odd_part) + odd_part)
    odd_part = odd_part + LIFT_GAMMA * (even_part + next_fn(even_part))
    even_part = even_part + LIFT_DELTA * (prev_fn(odd_part) + odd_part)
    return even_part / LIFT_KAPPA, odd_part * LIFT_KAPPA


def lift_line(field, along, periodic):
    even_part, odd_part = split_pairs(field, along)
    pairs = even_part.shape[along]
    if periodic:
        def next_fn(values):
            return jnp.roll(values, -1, along)

        def prev_fn(values):
            return jnp.roll(values, 1, along)
    else:
        def next_fn(values):
            return jnp.concatenate([lax.slice_in_dim(values, 1, pairs, axis=along), lax.slice_in_dim(values, pairs - 1, pairs, axis=along)], along)

        def prev_fn(values):
            return jnp.concatenate([lax.slice_in_dim(values, 0, 1, axis=along), lax.slice_in_dim(values, 0, pairs - 1, axis=along)], along)
    low, high = lift_core(even_part, odd_part, next_fn, prev_fn)
    return join_pairs(low, high, along)


def one_level(field):
    field = lift_line(field, 2, False)
    field = lift_line(field, 0, True)
    return lift_line(field, 1, True)


def transform(field, level):
    result = one_level(field)
    if level + 1 < LEVELS:
        shape = result.shape
        blocks = result.reshape(shape[0] // 2, 2, shape[1] // 2, 2, shape[2] // 2, 2)
        inner = transform(blocks[:, 0, :, 0, :, 0], level + 1)
        result = blocks.at[:, 0, :, 0, :, 0].set(inner).reshape(shape)
    return result


def reference(volume_fraction, vorticity):
    return transform(volume_fraction, 0), transform(vorticity, 0)
```

```python
import jax
import jax.numpy as jnp
import numpy as np
from jax import lax
from jax.experimental import pallas as pl
from jax.experimental.pallas import tpu as pltpu
from jax.sharding import PartitionSpec as P

LEVELS = 3
LIFT_ALPHA = -1.586134342
LIFT_BETA = -0.05298011854
LIFT_GAMMA = 0.8829110762
LIFT_DELTA = 0.4435068522
LIFT_KAPPA = 1.149604398
MESH = pl.DeviceIdType.MESH
N = 32
NZ = 128
EDGE_ROWS = 208
CORNER_ROWS = 48


def lift_matrix(count, periodic):
    eye = np.eye(count)
    even, odd = eye[0::2], eye[1::2]
    if periodic:
        following = lambda t: np.roll(t, -1, 0)
        before = lambda t: np.roll(t, 1, 0)
    else:
        following = lambda t: np.concatenate([t[1:], t[-1:]])
        before = lambda t: np.concatenate([t[:1], t[:-1]])
    odd = odd + LIFT_ALPHA * (even + following(even))
    even = even + LIFT_BETA * (before(odd) + odd)
    odd = odd + LIFT_GAMMA * (even + following(even))
    even = even + LIFT_DELTA * (before(odd) + odd)
    out = np.zeros((count, count))
    out[0::2], out[1::2] = even / LIFT_KAPPA, odd * LIFT_KAPPA
    return out


def factor(matrix, rank):
    u, s, vt = np.linalg.svd(matrix)
    assert s[rank:].max() < 1e-12
    return u[:, :rank] * s[:rank], vt[:rank]


def axis_operators():
    found, current = [], np.eye(5 * N)
    for level, (up, down) in enumerate(((2, 2), (3, 3), (4, 3))):
        full = lift_matrix(current.shape[0], True) @ current
        size = N >> level
        rows = full[2 * size : 3 * size]
        gain_left, send_up = factor(rows[:, N : 2 * N], up)
        gain_right, send_down = factor(rows[:, 3 * N : 4 * N], down)
        found.append((rows[:, 2 * N : 3 * N], send_up, send_down, gain_left, gain_right))
        current = full[0::2]
    return found


def depth_operators():
    one = lift_matrix(NZ, False)
    two = lift_matrix(NZ // 2, False) @ one[0::2]
    three = lift_matrix(NZ // 4, False) @ two[0::2]
    return one, two, three


OPS = axis_operators()


def padded(matrix, rows):
    return np.concatenate([matrix, np.zeros((rows - matrix.shape[0],) + matrix.shape[1:])])


def blocks(matrix, count):
    return np.kron(np.eye(count), matrix)


def batched(matrix):
    rows, cols = matrix.shape
    out = np.zeros((rows, 8, 8, cols))
    for i in range(8):
        out[:, i, i, :] = matrix
    return out.reshape(rows * 8, 8 * cols)


def corner_matrix(up, down, count, rows):
    out = np.zeros((4, rows, 2 * count, N))
    for corner in range(4):
        for jy in range(count):
            for jx, line in enumerate((up, down)[corner // 2]):
                out[corner, count * jy + jx, count * (corner % 2) + jy] = line
    return out.reshape(4 * rows, 2 * count * N)


def gain_matrix(level, states):
    _, _, _, left, right = OPS[level]
    size = N >> level
    left4 = np.zeros((size, 4))
    right4 = np.zeros((size, 4))
    left4[:, : left.shape[1]] = left
    right4[:, : right.shape[1]] = right
    eye = np.eye(size)
    parts = []
    for gain in (left4, right4):
        parts.append(np.einsum("xj,yv->xyjv", gain[:, :states], eye).reshape(size * size, -1))
    for gain in (left4, right4):
        parts.append(np.einsum("yj,xv->xyjv", gain[:, :states], eye).reshape(size * size, -1))
    for corner in range(4):
        gx = (left4, right4)[corner // 2]
        gy = (left4, right4)[corner % 2]
        parts.append(np.einsum("xi,yj->xyji", gx, gy).reshape(size * size, 16))
    out = np.concatenate(parts, 1)
    return np.pad(out, ((0, 0), (0, 256 - out.shape[1])))


def halves(matrix):
    high = np.asarray(matrix, jnp.bfloat16)
    low = np.asarray(matrix - high.astype(np.float64), jnp.bfloat16)
    return high, low


def wide(matrix):
    return np.pad(matrix, ((0, 0), (0, 256 - matrix.shape[1])))


def tables():
    one, two, three = depth_operators()
    depth = np.zeros((2, NZ, 256))
    for f in range(2):
        depth[f, :, 64 * f : 64 * f + 64] = two.T
        depth[f, :, 128 + 32 * f : 160 + 32 * f] = three.T
    own1, up1, down1, _, _ = OPS[0]
    own2, up2, down2, _, _ = OPS[1]
    own3, up3, down3, _, _ = OPS[2]
    ext2 = np.concatenate([own2, padded(up2, 4), padded(down2, 4)])
    ext3 = np.concatenate([own3, up3, padded(down3, 4)])
    spread2 = np.zeros((2, 64, 2, NZ))
    spread3 = np.zeros((4, 32, 2, NZ))
    for f in range(2):
        for i in range(64):
            spread2[f, i, f, 2 * i] = 1
        for i in range(32):
            spread3[f, i, f, 4 * i] = 1
    pairs = {}
    pairs["z1"] = one.T
    pairs["x1"] = blocks(own1, 4)
    pairs["c1"] = corner_matrix(up1, down1, 2, 8)
    pairs["z23"] = depth.reshape(256, 256)
    pairs["s1"] = batched(np.concatenate([up1, down1]))
    pairs["b2"] = batched(ext2)
    pairs["n2"] = blocks(own2, 8)
    pairs["c2"] = corner_matrix(up2, down2, 4, 16)
    pairs["b3"] = batched(ext3)
    pairs["n3"] = blocks(own3, 8)
    pairs["c3"] = corner_matrix(up3, down3, 4, 16)
    pairs["m2"] = gain_matrix(1, 3)
    pairs["m3"] = gain_matrix(2, 4)
    packed, where, at = [], {}, 0

    def put(name, array):
        nonlocal at
        where[name] = (at, array.shape[0])
        packed.append(array)
        at += array.shape[0]

    for name, matrix in pairs.items():
        high, low = halves(matrix)
        if matrix.shape[1] == 128:
            put(name, np.concatenate([high, low], 1))
        else:
            put(name + "h", high)
            put(name + "l", low)
    high, low = halves(blocks(own1, 2))
    put("u1", wide(np.concatenate([high, high, low], 1)))
    put("p2", np.asarray(spread2.reshape(128, 256), jnp.bfloat16))
    put("p3", np.asarray(spread3.reshape(128, 256), jnp.bfloat16))
    return np.concatenate(packed), where


TABLE, WHERE = tables()


def split(value):
    high = value.astype(jnp.bfloat16)
    return high, (value - high.astype(jnp.float32)).astype(jnp.bfloat16)


def dot(a, b):
    return jnp.dot(a, b, preferred_element_type=jnp.float32)


def column(gain, first):
    row = lax.broadcasted_iota(jnp.int32, (8, NZ), 0)
    out = jnp.zeros((8, NZ), jnp.float32)
    for i in range(8):
        if abs(gain[first + i]) > 1e-13:
            out = jnp.where(row == i, jnp.float32(gain[first + i]), out)
    return out


def lift_own(lines):
    pairs = N // 2
    even = lines[0::2]
    odd = lines[1::2]
    zero = jnp.zeros_like(even[0])
    odd = [LIFT_ALPHA * even[0]] + [odd[i] + LIFT_ALPHA * (even[i] + (even[i + 1] if i + 1 < pairs else zero)) for i in range(pairs)]
    even = [LIFT_BETA * odd[0]] + [even[i] + LIFT_BETA * (odd[i] + odd[i + 1]) for i in range(pairs)] + [LIFT_BETA * odd[pairs]]
    odd = [odd[i] + LIFT_GAMMA * (even[i] + even[i + 1]) for i in range(pairs + 1)]
    out = []
    for i in range(pairs):
        out.append((even[i + 1] + LIFT_DELTA * (odd[i] + odd[i + 1])) * (1.0 / LIFT_KAPPA))
        out.append(odd[i + 1] * LIFT_KAPPA)
    return out


def kernel(nx, ny, v0_ref, v1_ref, table_ref, out0_ref, out1_ref, fields, table, w1h, w1l, w2h, w2l, w3h, w3l, sides, states1, lines, states2, states3, level2, level3, send_edge, send_corner, got_edge, got_corner, in_sem, send_sem, recv_sem):
    ix, iy = lax.axis_index("dx"), lax.axis_index("dy")
    right, left = lax.rem(ix + 1, nx), lax.rem(ix + nx - 1, nx)
    above, below = lax.rem(iy + 1, ny), lax.rem(iy + ny - 1, ny)
    edge_to = [(right, iy), (left, iy), (ix, above), (ix, below)]
    corner_to = [(right, above), (right, below), (left, above), (left, below)]

    loads = [
        pltpu.make_async_copy(v0_ref, fields.at[0], in_sem.at[0]),
        pltpu.make_async_copy(v1_ref, fields.at[1], in_sem.at[1]),
        pltpu.make_async_copy(table_ref, table, in_sem.at[2]),
    ]
    for load in loads:
        load.start()
    barrier = pltpu.get_barrier_semaphore()
    for there in corner_to + edge_to:
        pl.semaphore_signal(barrier, inc=1, device_id=there, device_id_type=MESH)
    for load in loads:
        load.wait()

    def part(name):
        at, rows = WHERE[name]
        return table[at : at + rows, :]

    def both(name):
        if name in WHERE:
            return part(name)[:, :128], part(name)[:, 128:]
        return part(name + "h"), part(name + "l")

    def times(name, pair):
        (ah, al), (bh, bl) = both(name), pair
        return dot(ah, bh) + dot(ah, bl) + dot(al, bh)

    def timed(pair, name):
        (ah, al), (bh, bl) = pair, both(name)
        return dot(ah, bh) + dot(al, bh) + dot(ah, bl)

    for b in range(4):
        v0 = split(fields[0, 8 * b : 8 * b + 8].reshape(256, NZ))
        v1 = split(fields[1, 8 * b : 8 * b + 8].reshape(256, NZ))
        w1 = jnp.concatenate([timed(v0, "z1"), timed(v1, "z1")], 1)
        v01 = [jnp.concatenate([p, q], 1) for p, q in zip(v0, v1)]
        w23 = timed(v01, "z23")
        rows = slice(256 * b, 256 * b + 256)
        w1h[rows, :], w1l[rows, :] = split(w1)
        high, low = split(w23)
        w2h[rows, :], w3h[rows, :] = high[:, :128], high[:, 128:]
        w2l[rows, :], w3l[rows, :] = low[:, :128], low[:, 128:]
        if b == 0:
            for j in range(2):
                sides[2 + j] = sum(float(OPS[0][2][j, i]) * w1[32 * i : 32 * i + 32] for i in range(3))
        if b == 3:
            for j in range(2):
                sides[j] = sum(float(OPS[0][1][j, 28 + i]) * w1[128 + 32 * i : 160 + 32 * i] for i in range(4))

    for b in range(4):
        rows = slice(256 * b, 256 * b + 256)
        here = slice(8 * b, 8 * b + 8)
        states1[:, here, :] = times("s1", (w1h[rows, :], w1l[rows, :])).reshape(4, 8, 256)
        states2[:, here, :] = times("b2", (w2h[rows, :], w2l[rows, :])).reshape(24, 8, NZ)
        states3[:, here, :] = times("b3", (w3h[rows, :], w3l[rows, :])).reshape(16, 8, NZ)

    def put_edges1(first, value):
        for k in range(2):
            for f in range(2):
                send_edge[first + k, 64 * f : 64 * f + 64, :] = value[64 * k : 64 * k + 64, 128 * f : 128 * f + 128]

    lines1 = split(states1[...].reshape(128, 256))
    put_edges1(0, times("x1", split(sides[...].reshape(128, 256))))
    put_edges1(2, times("x1", lines1))
    corners1 = times("c1", lines1)
    for c in range(4):
        for f in range(2):
            send_corner[c, 8 * f : 8 * f + 8, :] = corners1[8 * c : 8 * c + 8, 128 * f : 128 * f + 128]

    for c in range(2):
        value = times("b2", split(states2[8 * c : 8 * c + 8].reshape(256, NZ))).reshape(24, 8, NZ)
        level2[:, 8 * c : 8 * c + 8, :] = value[:16]
        for k in range(2):
            for j in range(3):
                send_edge[k, 128 + 16 * j + 8 * c : 136 + 16 * j + 8 * c, :] = value[16 + 4 * k + j]
    lines2 = split(states2[16:24].reshape(256, NZ))
    value = times("n2", lines2)
    for k in range(2):
        send_edge[2 + k, 128:176, :] = value[64 * k : 64 * k + 48]
    value = times("c2", lines2)
    for c in range(4):
        send_corner[c, 16:32, :] = value[16 * c : 16 * c + 16]
    value = times("b3", split(states3[0:8].reshape(256, NZ))).reshape(16, 8, NZ)
    level3[...] = value[:8]
    for k in range(2):
        send_edge[k, 176:208, :] = value[8 + 4 * k : 12 + 4 * k].reshape(32, NZ)
    lines3 = split(states3[8:16].reshape(256, NZ))
    value = times("n3", lines3)
    for k in range(2):
        send_edge[2 + k, 176:208, :] = value[32 * k : 32 * k + 32]
    value = times("c3", lines3)
    for c in range(4):
        send_corner[c, 32:48, :] = value[16 * c : 16 * c + 16]

    pl.semaphore_wait(barrier, 8)
    copies = []
    for c in range(4):
        copies.append(pltpu.make_async_remote_copy(src_ref=send_corner.at[c], dst_ref=got_corner.at[c], send_sem=send_sem.at[c], recv_sem=recv_sem.at[c], device_id=corner_to[c], device_id_type=MESH))
    for k in range(4):
        copies.append(pltpu.make_async_remote_copy(src_ref=send_edge.at[k], dst_ref=got_edge.at[k], send_sem=send_sem.at[4 + k], recv_sem=recv_sem.at[4 + k], device_id=edge_to[k], device_id_type=MESH))
    for copy in copies:
        copy.start()

    outs = (out0_ref, out1_ref)
    own = part("u1")[:, :192]
    for p in range(16):
        rows = slice(64 * p, 64 * p + 64)
        high = w1h[rows, :]
        value = dot(own, jnp.concatenate([high, w1l[rows, :], high], 0))
        lines[2 * p] = value[:32]
        lines[2 * p + 1] = value[32:]
    for f in range(2):
        for t in range(4):
            value = lift_own([lines[i, 8 * t : 8 * t + 8, 128 * f : 128 * f + 128] for i in range(N)])
            for i in range(N):
                outs[f][i, 8 * t : 8 * t + 8, :] = value[i]

    for copy in copies:
        copy.wait()

    parts2 = [got_edge[k, 128:176, :] for k in range(4)] + [got_corner[c, 16:32, :] for c in range(4)]
    value2 = times("m2", split(jnp.concatenate(parts2, 0))) + level2[...].reshape(256, NZ)
    parts3 = [got_edge[k, 176:208, :] for k in range(4)] + [got_corner[c, 32:48, :] for c in range(4)]
    parts3.append(jnp.zeros((64, NZ), jnp.float32))
    value3 = times("m3", split(jnp.concatenate(parts3, 0))) + level3[...].reshape(64, NZ)
    high, low = split(value2)
    value2 = dot(high, part("p2")) + dot(low, part("p2"))
    high, low = split(value3)
    value3 = dot(high, part("p3")) + dot(low, part("p3"))

    gains = (OPS[0][3], OPS[0][4])
    for f in range(2):
        for k, xs in enumerate(((0, 1, 2), (28, 29, 30, 31))):
            for x in xs:
                outs[f][x] += sum(float(gains[k][x, j]) * got_edge[k, 64 * f + 32 * j : 64 * f + 32 * j + 32, :] for j in range(2))
        for k in range(2):
            for j in range(2):
                for side, first in enumerate((0, 24)):
                    at = 64 * f + 32 * j + first
                    corner = 2 * side + k
                    more = [column(gains[side][:, i], first) * got_corner[corner, 8 * f + 2 * j + i : 8 * f + 2 * j + i + 1, :] for i in range(2)]
                    got_edge[2 + k, at : at + 8, :] += more[0] + more[1]
        for k, first in enumerate((0, 24)):
            cols = [column(gains[k][:, j], first) for j in range(2)]
            for x in range(N):
                outs[f][x, first : first + 8, :] += sum(cols[j] * got_edge[2 + k, 64 * f + 32 * j + x : 64 * f + 32 * j + x + 1, :] for j in range(2))

    lane = lax.broadcasted_iota(jnp.int32, (16, NZ), 1)
    for f in range(2):
        for x in range(16):
            old = outs[f][2 * x, pl.ds(0, 16, stride=2), :]
            outs[f][2 * x, pl.ds(0, 16, stride=2), :] = jnp.where(lane % 2 == 0, value2[16 * x : 16 * x + 16, 128 * f : 128 * f + 128], old)
        for x in range(8):
            old = outs[f][4 * x, pl.ds(0, 8, stride=4), :]
            outs[f][4 * x, pl.ds(0, 8, stride=4), :] = jnp.where(lane[:8] % 4 == 0, value3[8 * x : 8 * x + 8, 128 * f : 128 * f + 128], old)


def solution(mesh):
    nx, ny = mesh.shape["dx"], mesh.shape["dy"]

    def body(volume_fraction, vorticity):
        block = jax.ShapeDtypeStruct((N, N, NZ), jnp.float32)
        f32, bf16 = jnp.float32, jnp.bfloat16
        return pl.pallas_call(
            lambda *refs: kernel(nx, ny, *refs),
            out_shape=(block, block),
            in_specs=[pl.BlockSpec(memory_space=pl.ANY)] * 3,
            out_specs=(pl.BlockSpec(memory_space=pltpu.VMEM),) * 2,
            scratch_shapes=[
                pltpu.VMEM((2, N, N, NZ), f32),
                pltpu.VMEM(TABLE.shape, bf16),
                pltpu.VMEM((1024, 256), bf16),
                pltpu.VMEM((1024, 256), bf16),
                pltpu.VMEM((1024, NZ), bf16),
                pltpu.VMEM((1024, NZ), bf16),
                pltpu.VMEM((1024, NZ), bf16),
                pltpu.VMEM((1024, NZ), bf16),
                pltpu.VMEM((4, N, 256), f32),
                pltpu.VMEM((4, N, 256), f32),
                pltpu.VMEM((N, N, 256), f32),
                pltpu.VMEM((24, N, NZ), f32),
                pltpu.VMEM((16, N, NZ), f32),
                pltpu.VMEM((16, 16, NZ), f32),
                pltpu.VMEM((8, 8, NZ), f32),
                pltpu.VMEM((4, EDGE_ROWS, NZ), f32),
                pltpu.VMEM((4, CORNER_ROWS, NZ), f32),
                pltpu.VMEM((4, EDGE_ROWS, NZ), f32),
                pltpu.VMEM((4, CORNER_ROWS, NZ), f32),
                pltpu.SemaphoreType.DMA((3,)),
                pltpu.SemaphoreType.DMA((8,)),
                pltpu.SemaphoreType.DMA((8,)),
            ],
            compiler_params=pltpu.CompilerParams(
                collective_id=0, has_side_effects=True, vmem_limit_bytes=32 * 1024 * 1024
            ),
        )(volume_fraction, vorticity, jnp.asarray(TABLE))

    placed = P("dx", "dy", None)
    return jax.shard_map(
        body, mesh=mesh, in_specs=(placed, placed), out_specs=(placed, placed), check_vma=False
    )
```

```python
import jax
import jax.numpy as jnp
import numpy as np
from jax import lax
from jax.experimental import pallas as pl
from jax.experimental.pallas import tpu as pltpu
from jax.sharding import PartitionSpec as P

LEVELS = 3
LIFT_ALPHA = -1.586134342
LIFT_BETA = -0.05298011854
LIFT_GAMMA = 0.8829110762
LIFT_DELTA = 0.4435068522
LIFT_KAPPA = 1.149604398
MESH = pl.DeviceIdType.MESH
N = 32
NZ = 128
EDGE_ROWS = 208
CORNER_ROWS = 48


def lift_matrix(count, periodic):
    eye = np.eye(count)
    even, odd = eye[0::2], eye[1::2]
    if periodic:
        following = lambda t: np.roll(t, -1, 0)
        before = lambda t: np.roll(t, 1, 0)
    else:
        following = lambda t: np.concatenate([t[1:], t[-1:]])
        before = lambda t: np.concatenate([t[:1], t[:-1]])
    odd = odd + LIFT_ALPHA * (even + following(even))
    even = even + LIFT_BETA * (before(odd) + odd)
    odd = odd + LIFT_GAMMA * (even + following(even))
    even = even + LIFT_DELTA * (before(odd) + odd)
    out = np.zeros((count, count))
    out[0::2], out[1::2] = even / LIFT_KAPPA, odd * LIFT_KAPPA
    return out


def factor(matrix, rank):
    u, s, vt = np.linalg.svd(matrix)
    assert s[rank:].max() < 1e-12
    return u[:, :rank] * s[:rank], vt[:rank]


def axis_operators():
    found, current = [], np.eye(5 * N)
    for level, (up, down) in enumerate(((2, 2), (3, 3), (4, 3))):
        full = lift_matrix(current.shape[0], True) @ current
        size = N >> level
        rows = full[2 * size : 3 * size]
        gain_left, send_up = factor(rows[:, N : 2 * N], up)
        gain_right, send_down = factor(rows[:, 3 * N : 4 * N], down)
        found.append((rows[:, 2 * N : 3 * N], send_up, send_down, gain_left, gain_right))
        current = full[0::2]
    return found


def depth_operators():
    one = lift_matrix(NZ, False)
    two = lift_matrix(NZ // 2, False) @ one[0::2]
    three = lift_matrix(NZ // 4, False) @ two[0::2]
    return one, two, three


OPS = axis_operators()


def padded(matrix, rows):
    return np.concatenate([matrix, np.zeros((rows - matrix.shape[0],) + matrix.shape[1:])])


def blocks(matrix, count):
    return np.kron(np.eye(count), matrix)


def batched(matrix):
    rows, cols = matrix.shape
    out = np.zeros((rows, 8, 8, cols))
    for i in range(8):
        out[:, i, i, :] = matrix
    return out.reshape(rows * 8, 8 * cols)


def corner_matrix(up, down, count, rows):
    out = np.zeros((4, rows, 2 * count, N))
    for corner in range(4):
        for jy in range(count):
            for jx, line in enumerate((up, down)[corner // 2]):
                out[corner, count * jy + jx, count * (corner % 2) + jy] = line
    return out.reshape(4 * rows, 2 * count * N)


def gain_matrix(level, states):
    _, _, _, left, right = OPS[level]
    size = N >> level
    left4 = np.zeros((size, 4))
    right4 = np.zeros((size, 4))
    left4[:, : left.shape[1]] = left
    right4[:, : right.shape[1]] = right
    eye = np.eye(size)
    parts = []
    for gain in (left4, right4):
        parts.append(np.einsum("xj,yv->xyjv", gain[:, :states], eye).reshape(size * size, -1))
    for gain in (left4, right4):
        parts.append(np.einsum("yj,xv->xyjv", gain[:, :states], eye).reshape(size * size, -1))
    for corner in range(4):
        gx = (left4, right4)[corner // 2]
        gy = (left4, right4)[corner % 2]
        parts.append(np.einsum("xi,yj->xyji", gx, gy).reshape(size * size, 16))
    out = np.concatenate(parts, 1)
    return np.pad(out, ((0, 0), (0, 256 - out.shape[1])))


def halves(matrix):
    high = np.asarray(matrix, jnp.bfloat16)
    low = np.asarray(matrix - high.astype(np.float64), jnp.bfloat16)
    return high, low


def wide(matrix):
    return np.pad(matrix, ((0, 0), (0, 256 - matrix.shape[1])))


def tables():
    one, two, three = depth_operators()
    depth = np.zeros((2, NZ, 256))
    for f in range(2):
        depth[f, :, 64 * f : 64 * f + 64] = two.T
        depth[f, :, 128 + 32 * f : 160 + 32 * f] = three.T
    own1, up1, down1, _, _ = OPS[0]
    own2, up2, down2, _, _ = OPS[1]
    own3, up3, down3, _, _ = OPS[2]
    ext2 = np.concatenate([own2, padded(up2, 4), padded(down2, 4)])
    ext3 = np.concatenate([own3, up3, padded(down3, 4)])
    spread2 = np.zeros((2, 64, 2, NZ))
    spread3 = np.zeros((4, 32, 2, NZ))
    for f in range(2):
        for i in range(64):
            spread2[f, i, f, 2 * i] = 1
        for i in range(32):
            spread3[f, i, f, 4 * i] = 1
    pairs = {}
    pairs["z1"] = one.T
    pairs["x1"] = blocks(own1, 4)
    pairs["c1"] = corner_matrix(up1, down1, 2, 8)
    pairs["z23"] = depth.reshape(256, 256)
    pairs["s1"] = batched(np.concatenate([up1, down1]))
    pairs["b2"] = batched(ext2)
    pairs["n2"] = blocks(own2, 8)
    pairs["c2"] = corner_matrix(up2, down2, 4, 16)
    pairs["b3"] = batched(ext3)
    pairs["n3"] = blocks(own3, 8)
    pairs["c3"] = corner_matrix(up3, down3, 4, 16)
    pairs["m2"] = gain_matrix(1, 3)
    pairs["m3"] = gain_matrix(2, 4)
    groups = (("z1", "z23"), ("x1", "c1", "s1", "b2", "n2", "c2", "b3", "n3", "c3", "u1"), ("m2", "m3", "p2", "p3"))
    packed, where, at = [[], [], []], {}, [0, 0, 0]

    def put(name, array):
        group = next(i for i, names in enumerate(groups) if name in names or name[:-1] in names)
        where[name] = (group, at[group], array.shape[0])
        packed[group].append(array)
        at[group] += array.shape[0]

    for name, matrix in pairs.items():
        high, low = halves(matrix)
        if matrix.shape[1] == 128:
            put(name, np.concatenate([high, low], 1))
        else:
            put(name + "h", high)
            put(name + "l", low)
    high, low = halves(blocks(own1, 2))
    put("u1", wide(np.concatenate([high, high, low], 1)))
    put("p2", np.asarray(spread2.reshape(128, 256), jnp.bfloat16))
    put("p3", np.asarray(spread3.reshape(128, 256), jnp.bfloat16))
    return [np.concatenate(group) for group in packed], where


TABLES, WHERE = tables()


def split(value):
    high = value.astype(jnp.bfloat16)
    return high, (value - high.astype(jnp.float32)).astype(jnp.bfloat16)


def dot(a, b):
    return jnp.dot(a, b, preferred_element_type=jnp.float32)


def column(gain, first):
    row = lax.broadcasted_iota(jnp.int32, (8, NZ), 0)
    out = jnp.zeros((8, NZ), jnp.float32)
    for i in range(8):
        if abs(gain[first + i]) > 1e-13:
            out = jnp.where(row == i, jnp.float32(gain[first + i]), out)
    return out


def lift_own(lines):
    pairs = N // 2
    even = lines[0::2]
    odd = lines[1::2]
    zero = jnp.zeros_like(even[0])
    odd = [LIFT_ALPHA * even[0]] + [odd[i] + LIFT_ALPHA * (even[i] + (even[i + 1] if i + 1 < pairs else zero)) for i in range(pairs)]
    even = [LIFT_BETA * odd[0]] + [even[i] + LIFT_BETA * (odd[i] + odd[i + 1]) for i in range(pairs)] + [LIFT_BETA * odd[pairs]]
    odd = [odd[i] + LIFT_GAMMA * (even[i] + even[i + 1]) for i in range(pairs + 1)]
    out = []
    for i in range(pairs):
        out.append((even[i + 1] + LIFT_DELTA * (odd[i] + odd[i + 1])) * (1.0 / LIFT_KAPPA))
        out.append(odd[i + 1] * LIFT_KAPPA)
    return out


def reader(*refs):
    def part(name):
        group, at, rows = WHERE[name]
        return refs[group][at : at + rows, :]

    def both(name):
        if name in WHERE:
            return part(name)[:, :128], part(name)[:, 128:]
        return part(name + "h"), part(name + "l")

    def times(name, pair):
        (ah, al), (bh, bl) = both(name), pair
        return dot(ah, bh) + dot(ah, bl) + dot(al, bh)

    def timed(pair, name):
        (ah, al), (bh, bl) = pair, both(name)
        return dot(ah, bh) + dot(al, bh) + dot(ah, bl)

    return part, times, timed


def exchange(nx, ny, v0_ref, v1_ref, table0_ref, table1_ref, table2_ref, got_edge, got_corner, own1, level2, level3, table2, fields, table0, table1, w1h, w1l, w2h, w2l, w3h, w3l, sides, states1, lines, states2, states3, send_edge, send_corner, in_sem, send_sem, recv_sem):
    ix, iy = lax.axis_index("dx"), lax.axis_index("dy")
    right, left = lax.rem(ix + 1, nx), lax.rem(ix + nx - 1, nx)
    above, below = lax.rem(iy + 1, ny), lax.rem(iy + ny - 1, ny)
    edge_to = [(right, iy), (left, iy), (ix, above), (ix, below)]
    corner_to = [(right, above), (right, below), (left, above), (left, below)]

    loads = [
        pltpu.make_async_copy(v0_ref, fields.at[0], in_sem.at[0]),
        pltpu.make_async_copy(v1_ref, fields.at[1], in_sem.at[1]),
        pltpu.make_async_copy(table0_ref, table0, in_sem.at[2]),
        pltpu.make_async_copy(table1_ref, table1, in_sem.at[3]),
        pltpu.make_async_copy(table2_ref, table2, in_sem.at[4]),
    ]
    for load in loads:
        load.start()
    barrier = pltpu.get_barrier_semaphore()
    for there in corner_to + edge_to:
        pl.semaphore_signal(barrier, inc=1, device_id=there, device_id_type=MESH)
    part, times, timed = reader(table0, table1)
    for load in loads[:3]:
        load.wait()

    for b in range(4):
        v0 = split(fields[0, 8 * b : 8 * b + 8].reshape(256, NZ))
        v1 = split(fields[1, 8 * b : 8 * b + 8].reshape(256, NZ))
        w1 = jnp.concatenate([timed(v0, "z1"), timed(v1, "z1")], 1)
        v01 = [jnp.concatenate([p, q], 1) for p, q in zip(v0, v1)]
        w23 = timed(v01, "z23")
        rows = slice(256 * b, 256 * b + 256)
        w1h[rows, :], w1l[rows, :] = split(w1)
        high, low = split(w23)
        w2h[rows, :], w3h[rows, :] = high[:, :128], high[:, 128:]
        w2l[rows, :], w3l[rows, :] = low[:, :128], low[:, 128:]
        if b == 0:
            for j in range(2):
                sides[2 + j] = sum(float(OPS[0][2][j, i]) * w1[32 * i : 32 * i + 32] for i in range(3))
        if b == 3:
            for j in range(2):
                sides[j] = sum(float(OPS[0][1][j, 28 + i]) * w1[128 + 32 * i : 160 + 32 * i] for i in range(4))

    loads[3].wait()
    for b in range(4):
        rows = slice(256 * b, 256 * b + 256)
        here = slice(8 * b, 8 * b + 8)
        states1[:, here, :] = times("s1", (w1h[rows, :], w1l[rows, :])).reshape(4, 8, 256)
        states2[:, here, :] = times("b2", (w2h[rows, :], w2l[rows, :])).reshape(24, 8, NZ)
        states3[:, here, :] = times("b3", (w3h[rows, :], w3l[rows, :])).reshape(16, 8, NZ)

    def put_edges1(first, value):
        for k in range(2):
            for f in range(2):
                send_edge[first + k, 64 * f : 64 * f + 64, :] = value[64 * k : 64 * k + 64, 128 * f : 128 * f + 128]

    lines1 = split(states1[...].reshape(128, 256))
    put_edges1(0, times("x1", split(sides[...].reshape(128, 256))))
    put_edges1(2, times("x1", lines1))
    corners1 = times("c1", lines1)
    for c in range(4):
        for f in range(2):
            send_corner[c, 8 * f : 8 * f + 8, :] = corners1[8 * c : 8 * c + 8, 128 * f : 128 * f + 128]

    for c in range(2):
        value = times("b2", split(states2[8 * c : 8 * c + 8].reshape(256, NZ))).reshape(24, 8, NZ)
        level2[:, 8 * c : 8 * c + 8, :] = value[:16]
        for k in range(2):
            for j in range(3):
                send_edge[k, 128 + 16 * j + 8 * c : 136 + 16 * j + 8 * c, :] = value[16 + 4 * k + j]
    lines2 = split(states2[16:24].reshape(256, NZ))
    value = times("n2", lines2)
    for k in range(2):
        send_edge[2 + k, 128:176, :] = value[64 * k : 64 * k + 48]
    value = times("c2", lines2)
    for c in range(4):
        send_corner[c, 16:32, :] = value[16 * c : 16 * c + 16]
    value = times("b3", split(states3[0:8].reshape(256, NZ))).reshape(16, 8, NZ)
    level3[...] = value[:8]
    for k in range(2):
        send_edge[k, 176:208, :] = value[8 + 4 * k : 12 + 4 * k].reshape(32, NZ)
    lines3 = split(states3[8:16].reshape(256, NZ))
    value = times("n3", lines3)
    for k in range(2):
        send_edge[2 + k, 176:208, :] = value[32 * k : 32 * k + 32]
    value = times("c3", lines3)
    for c in range(4):
        send_corner[c, 32:48, :] = value[16 * c : 16 * c + 16]

    pl.semaphore_wait(barrier, 8)
    copies = []
    for c in range(4):
        copies.append(pltpu.make_async_remote_copy(src_ref=send_corner.at[c], dst_ref=got_corner.at[c], send_sem=send_sem.at[c], recv_sem=recv_sem.at[c], device_id=corner_to[c], device_id_type=MESH))
    for k in range(4):
        copies.append(pltpu.make_async_remote_copy(src_ref=send_edge.at[k], dst_ref=got_edge.at[k], send_sem=send_sem.at[4 + k], recv_sem=recv_sem.at[4 + k], device_id=edge_to[k], device_id_type=MESH))
    for copy in copies:
        copy.start()

    own = part("u1")[:, :192]
    for p in range(16):
        rows = slice(64 * p, 64 * p + 64)
        high = w1h[rows, :]
        value = dot(own, jnp.concatenate([high, w1l[rows, :], high], 0))
        lines[2 * p] = value[:32]
        lines[2 * p + 1] = value[32:]
    for f in range(2):
        for t in range(4):
            value = lift_own([lines[i, 8 * t : 8 * t + 8, 128 * f : 128 * f + 128] for i in range(N)])
            for i in range(N):
                own1[f, i, 8 * t : 8 * t + 8, :] = value[i]

    loads[4].wait()
    for copy in copies:
        copy.wait()


def finish(got_edge, got_corner, own1, level2, level3, table2, out0_ref, out1_ref, out, lines, out_sem):
    part, times, _ = reader(None, None, table2)

    parts2 = [got_edge[k, 128:176, :] for k in range(4)] + [got_corner[c, 16:32, :] for c in range(4)]
    value2 = times("m2", split(jnp.concatenate(parts2, 0))) + level2[...].reshape(256, NZ)
    parts3 = [got_edge[k, 176:208, :] for k in range(4)] + [got_corner[c, 32:48, :] for c in range(4)]
    parts3.append(jnp.zeros((64, NZ), jnp.float32))
    value3 = times("m3", split(jnp.concatenate(parts3, 0))) + level3[...].reshape(64, NZ)
    high, low = split(value2)
    value2 = dot(high, part("p2")) + dot(low, part("p2"))
    high, low = split(value3)
    value3 = dot(high, part("p3")) + dot(low, part("p3"))

    gains = (OPS[0][3], OPS[0][4])
    lane = lax.broadcasted_iota(jnp.int32, (16, NZ), 1)
    stores = []
    for f in range(2):
        ends = []
        for k in range(2):
            ends.append([])
            for j in range(2):
                at = 64 * f + 32 * j
                rows = [got_edge[2 + k, at + 8 * t : at + 8 * t + 8, :] for t in range(4)]
                for side, t in enumerate((0, 3)):
                    corner = 2 * side + k
                    for i in range(2):
                        rows[t] += column(gains[side][:, i], 8 * t) * got_corner[corner, 8 * f + 2 * j + i : 8 * f + 2 * j + i + 1, :]
                for t in range(4):
                    lines[k, j, 8 * t : 8 * t + 8, :] = rows[t]
        cols = [[column(gains[k][:, j], 24 * k) for j in range(2)] for k in range(2)]
        for x in range(N):
            value = [own1[f, x, 8 * t : 8 * t + 8, :] for t in range(4)]
            for k, xs in enumerate(((0, 1, 2), (28, 29, 30, 31))):
                if x in xs:
                    for j in range(2):
                        for t in range(4):
                            at = 64 * f + 32 * j + 8 * t
                            value[t] += float(gains[k][x, j]) * got_edge[k, at : at + 8, :]
            for k in range(2):
                for j in range(2):
                    value[3 * k] += cols[k][j] * lines[k, j, x : x + 1, :]
            for t in range(4):
                out[f, x, 8 * t : 8 * t + 8, :] = value[t]
            if x % 2 == 0:
                at = 8 * x
                cells = out[f, x, pl.ds(0, 16, stride=2), :]
                out[f, x, pl.ds(0, 16, stride=2), :] = jnp.where(lane % 2 == 0, value2[at : at + 16, 128 * f : 128 * f + 128], cells)
            if x % 4 == 0:
                at = 2 * x
                cells = out[f, x, pl.ds(0, 8, stride=4), :]
                out[f, x, pl.ds(0, 8, stride=4), :] = jnp.where(lane[:8] % 4 == 0, value3[at : at + 8, 128 * f : 128 * f + 128], cells)
            if x % 16 == 15:
                here = pl.ds(x - 15, 16)
                store = pltpu.make_async_copy(out.at[f, here], (out0_ref, out1_ref)[f].at[here], out_sem.at[2 * f + x // 16])
                store.start()
                stores.append(store)
    for store in stores:
        store.wait()


def solution(mesh):
    nx, ny = mesh.shape["dx"], mesh.shape["dy"]
    f32, bf16 = jnp.float32, jnp.bfloat16

    def body(volume_fraction, vorticity):
        inputs = [volume_fraction, vorticity] + [jnp.asarray(table) for table in TABLES]
        inputs = [pltpu.with_memory_space_constraint(value, pltpu.HBM) for value in inputs]
        passed = (
            pltpu.VMEM((4, EDGE_ROWS, NZ), f32),
            pltpu.VMEM((4, CORNER_ROWS, NZ), f32),
            pltpu.VMEM((2, N, N, NZ), f32),
            pltpu.VMEM((16, 16, NZ), f32),
            pltpu.VMEM((8, 8, NZ), f32),
            pltpu.VMEM(TABLES[2].shape, bf16),
        )
        middle = pl.pallas_call(
            lambda *refs: exchange(nx, ny, *refs),
            out_shape=passed,
            in_specs=[pl.BlockSpec(memory_space=pltpu.HBM)] * 5,
            out_specs=(pl.BlockSpec(memory_space=pltpu.VMEM),) * 6,
            scratch_shapes=[
                pltpu.VMEM((2, N, N, NZ), f32),
                pltpu.VMEM(TABLES[0].shape, bf16),
                pltpu.VMEM(TABLES[1].shape, bf16),
                pltpu.VMEM((1024, 256), bf16),
                pltpu.VMEM((1024, 256), bf16),
                pltpu.VMEM((1024, NZ), bf16),
                pltpu.VMEM((1024, NZ), bf16),
                pltpu.VMEM((1024, NZ), bf16),
                pltpu.VMEM((1024, NZ), bf16),
                pltpu.VMEM((4, N, 256), f32),
                pltpu.VMEM((4, N, 256), f32),
                pltpu.VMEM((N, N, 256), f32),
                pltpu.VMEM((24, N, NZ), f32),
                pltpu.VMEM((16, N, NZ), f32),
                pltpu.VMEM((4, EDGE_ROWS, NZ), f32),
                pltpu.VMEM((4, CORNER_ROWS, NZ), f32),
                pltpu.SemaphoreType.DMA((5,)),
                pltpu.SemaphoreType.DMA((8,)),
                pltpu.SemaphoreType.DMA((8,)),
            ],
            compiler_params=pltpu.CompilerParams(
                collective_id=0, has_side_effects=True, vmem_limit_bytes=32 * 1024 * 1024
            ),
        )(*inputs)
        middle = [pltpu.with_memory_space_constraint(value, pltpu.VMEM) for value in middle]
        block = pltpu.HBM((N, N, NZ), f32)
        return pl.pallas_call(
            finish,
            out_shape=(block, block),
            in_specs=[pl.BlockSpec(memory_space=pltpu.VMEM)] * 6,
            out_specs=(pl.BlockSpec(memory_space=pltpu.HBM),) * 2,
            scratch_shapes=[
                pltpu.VMEM((2, N, N, NZ), f32),
                pltpu.VMEM((2, 2, N, NZ), f32),
                pltpu.SemaphoreType.DMA((4,)),
            ],
            compiler_params=pltpu.CompilerParams(vmem_limit_bytes=32 * 1024 * 1024),
        )(*middle)

    placed = P("dx", "dy", None)
    return jax.shard_map(
        body, mesh=mesh, in_specs=(placed, placed), out_specs=(placed, placed), check_vma=False
    )
```

```python
import jax
import jax.numpy as jnp
import numpy as np
from jax import lax
from jax.experimental import pallas as pl
from jax.experimental.pallas import tpu as pltpu
from jax.sharding import PartitionSpec as P

LEVELS = 3
LIFT_ALPHA = -1.586134342
LIFT_BETA = -0.05298011854
LIFT_GAMMA = 0.8829110762
LIFT_DELTA = 0.4435068522
LIFT_KAPPA = 1.149604398
MESH = pl.DeviceIdType.MESH
N = 32
NZ = 128
EDGE_ROWS = 208
CORNER_ROWS = 48


def lift_matrix(count, periodic):
    eye = np.eye(count)
    even, odd = eye[0::2], eye[1::2]
    if periodic:
        following = lambda t: np.roll(t, -1, 0)
        before = lambda t: np.roll(t, 1, 0)
    else:
        following = lambda t: np.concatenate([t[1:], t[-1:]])
        before = lambda t: np.concatenate([t[:1], t[:-1]])
    odd = odd + LIFT_ALPHA * (even + following(even))
    even = even + LIFT_BETA * (before(odd) + odd)
    odd = odd + LIFT_GAMMA * (even + following(even))
    even = even + LIFT_DELTA * (before(odd) + odd)
    out = np.zeros((count, count))
    out[0::2], out[1::2] = even / LIFT_KAPPA, odd * LIFT_KAPPA
    return out


def factor(matrix, rank):
    u, s, vt = np.linalg.svd(matrix)
    assert s[rank:].max() < 1e-12
    return u[:, :rank] * s[:rank], vt[:rank]


def axis_operators():
    found, current = [], np.eye(5 * N)
    for level, (up, down) in enumerate(((2, 2), (3, 3), (4, 3))):
        full = lift_matrix(current.shape[0], True) @ current
        size = N >> level
        rows = full[2 * size : 3 * size]
        gain_left, send_up = factor(rows[:, N : 2 * N], up)
        gain_right, send_down = factor(rows[:, 3 * N : 4 * N], down)
        found.append((rows[:, 2 * N : 3 * N], send_up, send_down, gain_left, gain_right))
        current = full[0::2]
    return found


def depth_operators():
    one = lift_matrix(NZ, False)
    two = lift_matrix(NZ // 2, False) @ one[0::2]
    three = lift_matrix(NZ // 4, False) @ two[0::2]
    return one, two, three


OPS = axis_operators()


def padded(matrix, rows):
    return np.concatenate([matrix, np.zeros((rows - matrix.shape[0],) + matrix.shape[1:])])


def blocks(matrix, count):
    return np.kron(np.eye(count), matrix)


def batched(matrix):
    rows, cols = matrix.shape
    out = np.zeros((rows, 8, 8, cols))
    for i in range(8):
        out[:, i, i, :] = matrix
    return out.reshape(rows * 8, 8 * cols)


def corner_matrix(up, down, stride, rows):
    sent = (up, down)
    total = len(up) + len(down)
    out = np.zeros((4, rows, total, N))
    for corner in range(4):
        sx, sy = corner // 2, corner % 2
        for jy in range(len(sent[sy])):
            for jx, line in enumerate(sent[sx]):
                out[corner, stride * jy + jx, sy * len(up) + jy] = line
    return out.reshape(4 * rows, total * N)


def gain_matrix(level):
    gains = OPS[level][3:]
    size = N >> level
    eye = np.eye(size)
    parts = [np.einsum("xj,yv->xyjv", gain, eye).reshape(size * size, -1) for gain in gains]
    parts += [np.einsum("yj,xv->xyjv", gain, eye).reshape(size * size, -1) for gain in gains]
    four = [np.pad(gain, ((0, 0), (0, 4 - gain.shape[1]))) for gain in gains]
    for corner in range(4):
        parts.append(np.einsum("xi,yj->xyji", four[corner // 2], four[corner % 2]).reshape(size * size, 16))
    return wide(np.concatenate(parts, 1))


def halves(matrix):
    high = np.asarray(matrix, jnp.bfloat16)
    low = np.asarray(matrix - high.astype(np.float64), jnp.bfloat16)
    return high, low


def wide(matrix):
    return np.pad(matrix, ((0, 0), (0, 256 - matrix.shape[1])))


def tables():
    one, two, three = depth_operators()
    depth = np.zeros((2, NZ, 256))
    for f in range(2):
        depth[f, :, 64 * f : 64 * f + 64] = two.T
        depth[f, :, 128 + 32 * f : 160 + 32 * f] = three.T
    own = [ops[0] for ops in OPS]
    up = [ops[1] for ops in OPS]
    down = [ops[2] for ops in OPS]
    sent = [np.concatenate([p, q]) for p, q in zip(up, down)]
    spread2 = np.zeros((2, 64, 2, NZ))
    spread3 = np.zeros((4, 32, 2, NZ))
    for f in range(2):
        for i in range(64):
            spread2[f, i, f, 2 * i] = 1
        for i in range(32):
            spread3[f, i, f, 4 * i] = 1
    groups = [
        {"ya": batched(np.concatenate([sent[0], own[1], sent[1], own[2], sent[2]]))},
        {
            "e2": batched(sent[1]),
            "n2": wide(blocks(own[1], 6)),
            "c2": wide(corner_matrix(up[1], down[1], 4, 16)),
            "e3": batched(sent[2]),
            "n3": wide(blocks(own[2], 7)),
            "c3": wide(corner_matrix(up[2], down[2], 4, 16)),
            "c1": corner_matrix(up[0], down[0], 2, 8),
            "z1": one.T,
            "z23": depth.reshape(256, 256),
        },
        {"o2": batched(own[1]), "o3": batched(own[2]), "x1": blocks(own[0], 4)},
        {"m2": gain_matrix(1), "m3": gain_matrix(2)},
    ]
    packed, where = [], {}
    for group, pairs in enumerate(groups):
        arrays = []

        def put(name, array):
            extra = -array.shape[0] % 16
            where[name] = (group, sum(len(other) for other in arrays), array.shape[0] + extra)
            arrays.append(np.pad(array, ((0, extra), (0, 0))))

        for name, matrix in pairs.items():
            high, low = halves(matrix)
            if matrix.shape[1] == 128:
                put(name, np.concatenate([high, low], 1))
            else:
                put(name + "h", high)
                put(name + "l", low)
        if group == 2:
            high, low = halves(blocks(own[0], 2))
            put("u1", wide(np.concatenate([high, high, low], 1)))
        if group == 3:
            put("p2", np.asarray(spread2.reshape(128, 256), jnp.bfloat16))
            put("p3", np.asarray(spread3.reshape(128, 256), jnp.bfloat16))
        packed.append(np.concatenate(arrays))
    return packed, where


TABLES, WHERE = tables()


def split(value):
    high = value.astype(jnp.bfloat16)
    return high, (value - high.astype(jnp.float32)).astype(jnp.bfloat16)


def dot(a, b):
    return jnp.dot(a, b, preferred_element_type=jnp.float32)


def column(gain, first):
    row = lax.broadcasted_iota(jnp.int32, (8, NZ), 0)
    out = jnp.zeros((8, NZ), jnp.float32)
    for i in range(8):
        if abs(gain[first + i]) > 1e-13:
            out = jnp.where(row == i, jnp.float32(gain[first + i]), out)
    return out


def lift_own(lines):
    pairs = N // 2
    even = lines[0::2]
    odd = lines[1::2]
    zero = jnp.zeros_like(even[0])
    odd = [LIFT_ALPHA * even[0]] + [odd[i] + LIFT_ALPHA * (even[i] + (even[i + 1] if i + 1 < pairs else zero)) for i in range(pairs)]
    even = [LIFT_BETA * odd[0]] + [even[i] + LIFT_BETA * (odd[i] + odd[i + 1]) for i in range(pairs)] + [LIFT_BETA * odd[pairs]]
    odd = [odd[i] + LIFT_GAMMA * (even[i] + even[i + 1]) for i in range(pairs + 1)]
    out = []
    for i in range(pairs):
        out.append((even[i + 1] + LIFT_DELTA * (odd[i] + odd[i + 1])) * (1.0 / LIFT_KAPPA))
        out.append(odd[i + 1] * LIFT_KAPPA)
    return out


def both_of(part, name):
    if name in WHERE:
        return part(name)[:, :128], part(name)[:, 128:]
    return part(name + "h"), part(name + "l")


def reader(*refs):
    def part(name):
        group, at, rows = WHERE[name]
        return refs[group][at : at + rows, :]

    def times(name, pair):
        (ah, al), (bh, bl) = both_of(part, name), pair
        return dot(ah, bh) + dot(ah, bl) + dot(al, bh)

    def timed(pair, name):
        (ah, al), (bh, bl) = pair, both_of(part, name)
        return dot(ah, bh) + dot(al, bh) + dot(ah, bl)

    return part, times, timed


def exchange(nx, ny, v0_ref, v1_ref, table0_ref, table1_ref, table2_ref, table3_ref, own1, got_edge, got_corner, level2, level3, table3, fields, table0, table1, table2, rawh, rawl, states1, states2, states3, lines, send_side, got_side, send_edge, send_corner, relays, in_sem, send_sem, recv_sem):
    ix, iy = lax.axis_index("dx"), lax.axis_index("dy")
    right, left = lax.rem(ix + 1, nx), lax.rem(ix + nx - 1, nx)
    above, below = lax.rem(iy + 1, ny), lax.rem(iy + ny - 1, ny)
    edge_to = [(right, iy), (left, iy), (ix, above), (ix, below)]
    corner_to = [(right, above), (right, below), (left, above), (left, below)]


    def rank(tx, ty):
        return 3 * tx + 2 * ty + 20 * lax.div(2 * ty, ny)

    earlier = [rank(tx, ty) < rank(ix, iy) for tx, ty in corner_to]
    barrier = pltpu.get_barrier_semaphore()
    for there, first in zip(corner_to, earlier):

        @pl.when(jnp.logical_not(first))
        def _():
            pl.semaphore_signal(barrier, inc=1, device_id=there, device_id_type=MESH)

    first_y, last_y = iy == 0, iy == ny - 1
    relayed = [jnp.logical_not(earlier[c] | first_y if c % 2 else earlier[c]) for c in range(4)]
    for k in (3, 1, 0):
        pl.semaphore_signal(barrier, inc=1, device_id=edge_to[k], device_id_type=MESH)

    @pl.when(jnp.logical_not(last_y))
    def _():
        pl.semaphore_signal(barrier, inc=1, device_id=edge_to[2], device_id_type=MESH)

    loads = []
    for i, (source, target) in enumerate(((table0_ref, table0), (v0_ref, fields.at[0]), (v1_ref, fields.at[1]), (table1_ref, table1), (table2_ref, table2), (table3_ref, table3))):
        loads.append(pltpu.make_async_copy(source, target, in_sem.at[i]))
        loads[-1].start()
    part, times, timed = reader(table0, table1, table2)

    def copy_to(at, source, target, there):
        return pltpu.make_async_remote_copy(src_ref=source, dst_ref=target, send_sem=send_sem.at[at], recv_sem=recv_sem.at[at], device_id=there, device_id_type=MESH)

    for load in loads[:3]:
        load.wait()
    for f in range(2):
        for j in range(2):
            at = slice(64 * f + 32 * j, 64 * f + 32 * j + 32)
            send_side[0, at, :] = sum(float(OPS[0][1][j, 28 + i]) * fields[f, 28 + i] for i in range(4))
            send_side[1, at, :] = sum(float(OPS[0][2][j, i]) * fields[f, i] for i in range(3))
    for b in range(4):
        here = slice(8 * b, 8 * b + 8)
        raw = split(jnp.concatenate([fields[f, here].reshape(256, NZ) for f in range(2)], 1))
        rawh[256 * b : 256 * b + 256, :], rawl[256 * b : 256 * b + 256, :] = raw
        value = times("ya", raw).reshape(42, 8, 256)
        states1[:, here, :] = value[:4]
        states2[:, here, :] = value[4:26]
        states3[:, here, :] = value[26:41]
    for k in range(2):
        for f in range(2):
            send_side[2 + k, 64 * f : 64 * f + 64, :] = states1[2 * k : 2 * k + 2, :, 128 * f : 128 * f + 128].reshape(64, NZ)
    loads[3].wait()

    def relay(below):
        for k in range(2):
            pl.semaphore_signal(relays.at[2 - 2 * k + below], inc=1, device_id=edge_to[k], device_id_type=MESH)

    pl.semaphore_wait(barrier, 4 - first_y.astype(jnp.int32) + sum(first.astype(jnp.int32) for first in earlier))

    @pl.when(last_y)
    def _():
        pl.semaphore_signal(relays.at[4], inc=1, device_id=edge_to[2], device_id_type=MESH)

    relay(0)
    pl.when(jnp.logical_not(first_y))(lambda: relay(1))
    sides = [copy_to(8 + k, send_side.at[k], got_side.at[k], edge_to[k]) for k in range(4)]
    for k in range(3):
        sides[k].start()
    pl.when(jnp.logical_not(first_y))(sides[3].start)

    value = [times("e2", split(states2[8 * c : 8 * c + 8].reshape(256, 256))) for c in range(2)]
    rows2 = [value[c][8 * j : 8 * j + 8] for j in range(6) for c in range(2)]
    lines2 = jnp.concatenate([states2[16:22].reshape(192, 256), jnp.zeros((64, 256), jnp.float32)], 0)
    lines2 = split(lines2)
    rows2 += [times("n2", lines2), times("c2", lines2)]
    rows3 = [times("e3", split(states3[0:8].reshape(256, 256)))[:56]]
    lines3 = jnp.concatenate([states3[8:15].reshape(224, 256), jnp.zeros((32, 256), jnp.float32)], 0)
    lines3 = split(lines3)
    rows3 += [times("n3", lines3)[:56], times("c3", lines3)]
    corners1 = times("c1", split(states1[...].reshape(128, 256)))
    zh, zl = both_of(part, "z23")

    def deep(value, half):
        high, low = split(value)
        at = slice(128 * half, 128 * half + 128)
        return dot(high, zh[:, at]) + dot(low, zh[:, at]) + dot(high, zl[:, at])

    value = deep(jnp.concatenate(rows2, 0), 0)
    for k in range(2):
        send_edge[k, 0:48, :] = value[48 * k : 48 * k + 48]
        send_edge[2 + k, 0:48, :] = value[96 + 48 * k : 144 + 48 * k]
    for c in range(4):
        send_corner[c, 16:32, :] = value[192 + 16 * c : 208 + 16 * c]
    value = deep(jnp.concatenate(rows3, 0), 1)
    for k, first in enumerate((0, 32)):
        for axis in range(2):
            count = 32 - 8 * k
            at = 56 * axis + first
            send_edge[2 * axis + k, 48 : 48 + count, :] = value[at : at + count]
    send_edge[1, 72:80, :] = jnp.zeros((8, NZ), jnp.float32)
    send_edge[3, 72:80, :] = jnp.zeros((8, NZ), jnp.float32)
    for c in range(4):
        send_corner[c, 32:48, :] = value[112 + 16 * c : 128 + 16 * c]
    value = timed(split(jnp.concatenate([corners1[:, :128], corners1[:, 128:]], 0)), "z1")
    for c in range(4):
        for f in range(2):
            send_corner[c, 8 * f : 8 * f + 8, :] = value[32 * f + 8 * c : 32 * f + 8 * c + 8]
    copies = [pltpu.make_async_remote_copy(src_ref=send_corner.at[c], dst_ref=got_corner.at[c], send_sem=send_sem.at[c], recv_sem=recv_sem.at[c], device_id=corner_to[c], device_id_type=MESH) for c in range(4)]
    for c in range(4):
        pl.when(earlier[c])(copies[c].start)
    copies += [copy_to(4 + k, send_edge.at[k], got_edge.at[k], edge_to[k]) for k in range(4)]
    for k in range(3):
        copies[4 + k].start()
    pl.when(jnp.logical_not(first_y))(copies[7].start)

    loads[4].wait()
    value = [times("o2", split(states2[8 * c : 8 * c + 8].reshape(256, 256))) for c in range(2)]
    value = deep(jnp.concatenate([value[c][8 * x : 8 * x + 8] for x in range(16) for c in range(2)], 0), 0)
    level2[...] = value
    level3[...] = deep(times("o3", split(states3[0:8].reshape(256, 256))), 1)
    def wait_and_send(c):
        pl.semaphore_wait(relays.at[c], 1)
        copies[c].start()

    for c in (0, 1):
        pl.when(relayed[c])(lambda: wait_and_send(c))

    @pl.when(first_y)
    def _():
        pl.semaphore_wait(relays.at[4], 1)
        relay(1)
        copies[7].start()
        sides[3].start()
        copies[1].start()
        copies[3].start()

    for c in (2, 3):
        pl.when(relayed[c])(lambda: wait_and_send(c))

    own = part("u1")[:, :192]
    for b in range(4):
        rows = slice(256 * b, 256 * b + 256)
        high, low = rawh[rows, :], rawl[rows, :]
        high, low = split(jnp.concatenate([timed((high[:, at : at + 128], low[:, at : at + 128]), "z1") for at in (0, 128)], 1))
        for p in range(4):
            at = slice(64 * p, 64 * p + 64)
            lines[4 * b + p] = dot(own, jnp.concatenate([high[at], low[at], high[at]], 0))
    for f in range(2):
        for t in range(4):
            value = lift_own([lines[i // 2, 32 * (i % 2) + 8 * t : 32 * (i % 2) + 8 * t + 8, 128 * f : 128 * f + 128] for i in range(N)])
            for i in range(N):
                own1[f, i, 8 * t : 8 * t + 8, :] = value[i]

    for copy in sides:
        copy.wait()
    gains = (OPS[0][3], OPS[0][4])
    both = []
    for axis in range(2):
        value = [got_side[2 * axis + k, 64 * f : 64 * f + 64, :] for f in range(2) for k in range(2)]
        value = jnp.concatenate([jnp.concatenate(value[:2], 0), jnp.concatenate(value[2:], 0)], 1)
        value = times("x1", split(value))
        both.append(timed(split(jnp.concatenate([value[:, :128], value[:, 128:]], 0)), "z1"))
    got_side[0], got_side[1] = both[1][:128], both[1][128:]
    for f in range(2):
        for k, xs in enumerate(((0, 1, 2), (28, 29, 30, 31))):
            for x in xs:
                own1[f, x] += sum(float(gains[k][x, j]) * both[0][128 * f + 64 * k + 32 * j : 128 * f + 64 * k + 32 * j + 32] for j in range(2))
        for k in range(2):
            cols = [column(gains[k][:, j], 24 * k) for j in range(2)]
            for x in range(N):
                own1[f, x, 24 * k : 24 * k + 8, :] += sum(cols[j] * got_side[f, 64 * k + 32 * j + x : 64 * k + 32 * j + x + 1, :] for j in range(2))

    loads[5].wait()
    for c in range(4):
        pl.when(jnp.logical_not(relayed[c]))(lambda: pl.semaphore_wait(relays.at[c], 1))
    for copy in copies:
        copy.wait()


def finish(own1, got_edge, got_corner, level2, level3, table3, out0_ref, out1_ref, even, odd, out_sem):
    part, times, _ = reader(None, None, None, table3)
    outs = (out0_ref, out1_ref)
    stores = []

    def store(at, source, target):
        stores.append(pltpu.make_async_copy(source, target, out_sem.at[at]))
        stores[-1].start()

    for f in range(2):
        store(f, own1.at[f, pl.ds(1, 13), 1], outs[f].at[pl.ds(1, 13), 1])

    parts2 = [got_edge[k, 0:48, :] for k in range(4)] + [got_corner[c, 16:32, :] for c in range(4)]
    value2 = times("m2", split(jnp.concatenate(parts2, 0))) + level2[...]
    parts3 = [got_edge[k, 48 : 80 - 8 * (k % 2), :] for k in range(4)] + [got_corner[c, 32:48, :] for c in range(4)]
    parts3.append(jnp.zeros((80, NZ), jnp.float32))
    value3 = times("m3", split(jnp.concatenate(parts3, 0))) + level3[...]
    high, low = split(value2)
    value2 = dot(high, part("p2")) + dot(low, part("p2"))
    high, low = split(value3)
    value3 = dot(high, part("p3")) + dot(low, part("p3"))

    gains = (OPS[0][3], OPS[0][4])
    lane = lax.broadcasted_iota(jnp.int32, (16, NZ), 1)
    cols = [[column(gains[k][:, j], 24 * k) for j in range(2)] for k in range(2)]
    for f in range(2):

        def cornered(x):
            value = [own1[f, x // 2, x % 2, 8 * t : 8 * t + 8, :] for t in range(4)]
            for side, xs in enumerate(((0, 1, 2), (28, 29, 30, 31))):
                if x in xs:
                    for k in range(2):
                        for j in range(2):
                            row = sum(float(gains[side][x, i]) * got_corner[2 * side + k, 8 * f + 2 * j + i : 8 * f + 2 * j + i + 1, :] for i in range(2))
                            value[3 * k] += cols[k][j] * row
            return jnp.concatenate(value, 0)

        for i, x in enumerate((1, 29, 31)):
            odd[f, i] = cornered(x)
        store(2 + f, odd.at[f, 0], outs[f].at[0, 1])
        store(4 + f, odd.at[f, pl.ds(1, 2)], outs[f].at[pl.ds(14, 2), 1])
    for f in range(2):
        for p in range(16):
            even[f, p] = cornered(2 * p)
            cells = even[f, p, pl.ds(0, 16, stride=2), :]
            even[f, p, pl.ds(0, 16, stride=2), :] = jnp.where(lane % 2 == 0, value2[16 * p : 16 * p + 16, 128 * f : 128 * f + 128], cells)
            if p % 2 == 0:
                cells = even[f, p, pl.ds(0, 8, stride=4), :]
                even[f, p, pl.ds(0, 8, stride=4), :] = jnp.where(lane[:8] % 4 == 0, value3[4 * p : 4 * p + 8, 128 * f : 128 * f + 128], cells)
            if p % 8 == 7:
                here = pl.ds(p - 7, 8)
                store(6 + 2 * f + p // 8, even.at[f, here], outs[f].at[here, 0])
    for copy in stores:
        copy.wait()


def solution(mesh):
    nx, ny = mesh.shape["dx"], mesh.shape["dy"]
    f32, bf16 = jnp.float32, jnp.bfloat16

    def body(volume_fraction, vorticity):
        inputs = [volume_fraction, vorticity] + [jnp.asarray(table) for table in TABLES]
        inputs = [pltpu.with_memory_space_constraint(value, pltpu.HBM) for value in inputs]
        passed = (
            pltpu.VMEM((2, N, N, NZ), f32),
            pltpu.VMEM((4, 80, NZ), f32),
            pltpu.VMEM((4, 48, NZ), f32),
            pltpu.VMEM((256, NZ), f32),
            pltpu.VMEM((64, NZ), f32),
            pltpu.VMEM(TABLES[3].shape, bf16),
        )
        middle = pl.pallas_call(
            lambda *refs: exchange(nx, ny, *refs),
            out_shape=passed,
            in_specs=[pl.BlockSpec(memory_space=pltpu.HBM)] * 6,
            out_specs=(pl.BlockSpec(memory_space=pltpu.VMEM),) * 6,
            scratch_shapes=[
                pltpu.VMEM((2, N, N, NZ), f32),
                pltpu.VMEM(TABLES[0].shape, bf16),
                pltpu.VMEM(TABLES[1].shape, bf16),
                pltpu.VMEM(TABLES[2].shape, bf16),
                pltpu.VMEM((1024, 256), bf16),
                pltpu.VMEM((1024, 256), bf16),
                pltpu.VMEM((4, N, 256), f32),
                pltpu.VMEM((22, N, 256), f32),
                pltpu.VMEM((15, N, 256), f32),
                pltpu.VMEM((16, 64, 256), f32),
                pltpu.VMEM((4, 128, NZ), f32),
                pltpu.VMEM((4, 128, NZ), f32),
                pltpu.VMEM((4, 80, NZ), f32),
                pltpu.VMEM((4, 48, NZ), f32),
                pltpu.SemaphoreType.REGULAR((5,)),
                pltpu.SemaphoreType.DMA((6,)),
                pltpu.SemaphoreType.DMA((12,)),
                pltpu.SemaphoreType.DMA((12,)),
            ],
            compiler_params=pltpu.CompilerParams(
                collective_id=0, has_side_effects=True, vmem_limit_bytes=32 * 1024 * 1024
            ),
        )(*inputs)
        middle = [middle[0].reshape(2, 16, 2, N, NZ)] + list(middle[1:])
        middle = [pltpu.with_memory_space_constraint(value, pltpu.VMEM) for value in middle]
        block = pltpu.HBM((16, 2, N, NZ), f32)
        outs = pl.pallas_call(
            finish,
            out_shape=(block, block),
            in_specs=[pl.BlockSpec(memory_space=pltpu.VMEM)] * 6,
            out_specs=(pl.BlockSpec(memory_space=pltpu.HBM),) * 2,
            scratch_shapes=[
                pltpu.VMEM((2, 16, N, NZ), f32),
                pltpu.VMEM((2, 3, N, NZ), f32),
                pltpu.SemaphoreType.DMA((10,)),
            ],
            compiler_params=pltpu.CompilerParams(vmem_limit_bytes=32 * 1024 * 1024),
        )(*middle)
        return tuple(out.reshape(N, N, NZ) for out in outs)

    placed = P("dx", "dy", None)
    return jax.shard_map(
        body, mesh=mesh, in_specs=(placed, placed), out_specs=(placed, placed), check_vma=False
    )
```

```python
import jax
import jax.numpy as jnp
import numpy as np
from jax import lax
from jax.experimental import pallas as pl
from jax.experimental.pallas import tpu as pltpu
from jax.sharding import PartitionSpec as P

LEVELS = 3
LIFT_ALPHA = -1.586134342
LIFT_BETA = -0.05298011854
LIFT_GAMMA = 0.8829110762
LIFT_DELTA = 0.4435068522
LIFT_KAPPA = 1.149604398
MESH = pl.DeviceIdType.MESH
N = 32
NZ = 128
EDGE_ROWS = 208
CORNER_ROWS = 48


def lift_matrix(count, periodic):
    eye = np.eye(count)
    even, odd = eye[0::2], eye[1::2]
    if periodic:
        following = lambda t: np.roll(t, -1, 0)
        before = lambda t: np.roll(t, 1, 0)
    else:
        following = lambda t: np.concatenate([t[1:], t[-1:]])
        before = lambda t: np.concatenate([t[:1], t[:-1]])
    odd = odd + LIFT_ALPHA * (even + following(even))
    even = even + LIFT_BETA * (before(odd) + odd)
    odd = odd + LIFT_GAMMA * (even + following(even))
    even = even + LIFT_DELTA * (before(odd) + odd)
    out = np.zeros((count, count))
    out[0::2], out[1::2] = even / LIFT_KAPPA, odd * LIFT_KAPPA
    return out


def factor(matrix, rank):
    u, s, vt = np.linalg.svd(matrix)
    assert s[rank:].max() < 1e-12
    return u[:, :rank] * s[:rank], vt[:rank]


def axis_operators():
    found, current = [], np.eye(5 * N)
    for level, (up, down) in enumerate(((2, 2), (3, 3), (4, 3))):
        full = lift_matrix(current.shape[0], True) @ current
        size = N >> level
        rows = full[2 * size : 3 * size]
        gain_left, send_up = factor(rows[:, N : 2 * N], up)
        gain_right, send_down = factor(rows[:, 3 * N : 4 * N], down)
        found.append((rows[:, 2 * N : 3 * N], send_up, send_down, gain_left, gain_right))
        current = full[0::2]
    return found


def depth_operators():
    one = lift_matrix(NZ, False)
    two = lift_matrix(NZ // 2, False) @ one[0::2]
    three = lift_matrix(NZ // 4, False) @ two[0::2]
    return one, two, three


OPS = axis_operators()


def padded(matrix, rows):
    return np.concatenate([matrix, np.zeros((rows - matrix.shape[0],) + matrix.shape[1:])])


def blocks(matrix, count):
    return np.kron(np.eye(count), matrix)


def batched(matrix):
    rows, cols = matrix.shape
    out = np.zeros((rows, 8, 8, cols))
    for i in range(8):
        out[:, i, i, :] = matrix
    return out.reshape(rows * 8, 8 * cols)


def corner_matrix(up, down, stride, rows):
    sent = (up, down)
    total = len(up) + len(down)
    out = np.zeros((4, rows, total, N))
    for corner in range(4):
        sx, sy = corner // 2, corner % 2
        for jy in range(len(sent[sy])):
            for jx, line in enumerate(sent[sx]):
                out[corner, stride * jy + jx, sy * len(up) + jy] = line
        if rows == 8:
            out[corner, 4:] = out[corner, :4]
    return out.reshape(4 * rows, total * N)


def gain_matrix(level):
    gains = OPS[level][3:]
    size = N >> level
    eye = np.eye(size)
    if level == 2:
        gains = [np.pad(gain, ((0, 0), (0, 4 - gain.shape[1]))) for gain in gains]
    parts = [np.einsum("xj,yv->xyjv", gain, eye).reshape(size * size, -1) for gain in gains]
    parts += [np.einsum("yj,xv->xyjv", gain, eye).reshape(size * size, -1) for gain in gains]
    four = [np.pad(gain, ((0, 0), (0, 4 - gain.shape[1]))) for gain in gains]
    for corner in range(4):
        parts.append(np.einsum("xi,yj->xyji", four[corner // 2], four[corner % 2]).reshape(size * size, 16))
    if level == 2:
        for i, width in enumerate([8] * 4 + [1] * 4):
            states = parts[i].reshape(size * size, -1, 2, width)
            parts[i] = np.concatenate([states[:, :, half].reshape(size * size, -1) for half in range(2)])
        out = np.concatenate(parts, 1)
        return np.pad(out, ((0, 0), (0, 128 - out.shape[1])))
    return wide(np.concatenate(parts, 1))


def halves(matrix):
    high = np.asarray(matrix, jnp.bfloat16)
    low = np.asarray(matrix - high.astype(np.float64), jnp.bfloat16)
    return high, low


def wide(matrix):
    return np.pad(matrix, ((0, 0), (0, 256 - matrix.shape[1])))


def tables():
    one, two, three = depth_operators()
    depth = np.zeros((2, NZ, 256))
    for f in range(2):
        depth[f, :, 64 * f : 64 * f + 64] = two.T
        for half in (128, 192):
            depth[f, :, half + 32 * f : half + 32 * f + 32] = three.T
    own = [ops[0] for ops in OPS]
    up = [ops[1] for ops in OPS]
    down = [ops[2] for ops in OPS]
    sent = [np.concatenate([p, q]) for p, q in zip(up, down)]
    spread2 = np.zeros((2, 64, 2, NZ))
    spread3 = np.zeros((4, 32, 2, NZ))
    for f in range(2):
        for i in range(64):
            spread2[f, i, f, 2 * i] = 1
        for i in range(32):
            spread3[f, i, f, 4 * i] = spread3[2 + f, i, f, 4 * i] = 1
    groups = [
        {"ya": batched(np.concatenate([sent[0], own[1], sent[1], own[2], sent[2]]))},
        {
            "c1": corner_matrix(up[0], down[0], 2, 8),
            "c23": np.concatenate([wide(corner_matrix(up[1], down[1], 4, 16)), wide(corner_matrix(up[2], down[2], 4, 16))]),
            "z1": one.T,
            "z23": depth.reshape(256, 256),
        },
        {
            "e2": batched(sent[1]),
            "e3": batched(sent[2]),
            "n23": np.concatenate([wide(blocks(own[1], 6)), wide(blocks(own[2], 7))]),
        },
        {"o2": batched(own[1]), "o3": batched(own[2]), "x1": blocks(own[0], 4)},
        {"m2": gain_matrix(1), "m3": gain_matrix(2)},
    ]
    packed, where = [], {}
    for group, pairs in enumerate(groups):
        arrays = []

        def put(name, array):
            extra = -array.shape[0] % 16
            where[name] = (group, sum(len(other) for other in arrays), array.shape[0] + extra)
            arrays.append(np.pad(array, ((0, extra), (0, 0))))

        for name, matrix in pairs.items():
            high, low = halves(matrix)
            if matrix.shape[1] == 128:
                put(name, np.concatenate([high, low], 1))
            else:
                put(name + "h", high)
                put(name + "l", low)
        if group == 3:
            high, low = halves(blocks(own[0], 2))
            put("u1", wide(np.concatenate([high, high, low], 1)))
        if group == 4:
            put("p2", np.asarray(spread2.reshape(128, 256), jnp.bfloat16))
            put("p3", np.asarray(spread3.reshape(128, 256), jnp.bfloat16))
        packed.append(np.concatenate(arrays))
    return packed, where


TABLES, WHERE = tables()


def split(value):
    high = value.astype(jnp.bfloat16)
    return high, (value - high.astype(jnp.float32)).astype(jnp.bfloat16)


def dot(a, b):
    return jnp.dot(a, b, preferred_element_type=jnp.float32)


def column(gain, first):
    row = lax.broadcasted_iota(jnp.int32, (8, NZ), 0)
    out = jnp.zeros((8, NZ), jnp.float32)
    for i in range(8):
        if abs(gain[first + i]) > 1e-13:
            out = jnp.where(row == i, jnp.float32(gain[first + i]), out)
    return out


def lift_own(lines):
    pairs = N // 2
    even = lines[0::2]
    odd = lines[1::2]
    zero = jnp.zeros_like(even[0])
    odd = [LIFT_ALPHA * even[0]] + [odd[i] + LIFT_ALPHA * (even[i] + (even[i + 1] if i + 1 < pairs else zero)) for i in range(pairs)]
    even = [LIFT_BETA * odd[0]] + [even[i] + LIFT_BETA * (odd[i] + odd[i + 1]) for i in range(pairs)] + [LIFT_BETA * odd[pairs]]
    odd = [odd[i] + LIFT_GAMMA * (even[i] + even[i + 1]) for i in range(pairs + 1)]
    out = []
    for i in range(pairs):
        out.append((even[i + 1] + LIFT_DELTA * (odd[i] + odd[i + 1])) * (1.0 / LIFT_KAPPA))
        out.append(odd[i + 1] * LIFT_KAPPA)
    return out


def both_of(part, name):
    if name in WHERE:
        return part(name)[:, :128], part(name)[:, 128:]
    return part(name + "h"), part(name + "l")


def reader(*refs):
    def part(name):
        group, at, rows = WHERE[name]
        return refs[group][at : at + rows, :]

    def times(name, pair):
        (ah, al), (bh, bl) = both_of(part, name), pair
        return dot(jnp.concatenate([ah, ah, al], 1), jnp.concatenate([bh, bl, bh], 0))

    def timed(pair, name):
        (ah, al), (bh, bl) = pair, both_of(part, name)
        return dot(jnp.concatenate([ah, al, ah], 1), jnp.concatenate([bh, bh, bl], 0))

    return part, times, timed


def exchange(nx, ny, v0_ref, v1_ref, table0_ref, table1_ref, table2_ref, table3_ref, table4_ref, own1, got_edge, got_corner, level2, level3, table4, fields, table0, table1, table2, table3, rawh, rawl, states1, states2, states3, lines, send_side, got_side, send_edge, send_corner, relays, in_sem, send_sem, recv_sem):
    loads = []

    def load(source, target):
        loads.append(pltpu.make_async_copy(source, target, in_sem.at[len(loads)]))
        loads[-1].start()

    load(table0_ref, table0)
    for b in range(2):
        for f, ref in enumerate((v0_ref, v1_ref)):
            load(ref.at[pl.ds(16 * b, 16)], fields.at[f, pl.ds(16 * b, 16)])
    load(table1_ref, table1)
    ix, iy = lax.axis_index("dx"), lax.axis_index("dy")
    right, left = lax.rem(ix + 1, nx), lax.rem(ix + nx - 1, nx)
    above, below = lax.rem(iy + 1, ny), lax.rem(iy + ny - 1, ny)
    edge_to = [(right, iy), (left, iy), (ix, above), (ix, below)]
    corner_to = [(right, above), (right, below), (left, above), (left, below)]


    def rank(tx, ty):
        return 3 * tx + 2 * ty + 20 * lax.div(2 * ty, ny)

    earlier = [rank(tx, ty) < rank(ix, iy) for tx, ty in corner_to]
    barrier = pltpu.get_barrier_semaphore()
    for there, first in zip(corner_to, earlier):

        @pl.when(jnp.logical_not(first))
        def _():
            pl.semaphore_signal(barrier, inc=1, device_id=there, device_id_type=MESH)

    first_x, last_x, first_y, last_y = ix == 0, ix == nx - 1, iy == 0, iy == ny - 1
    inner_x, inner_y = jnp.logical_not(first_x), jnp.logical_not(first_y)
    relayed = [jnp.logical_not(e) for e in (earlier[0], earlier[1] | first_y, earlier[2], earlier[3] | first_y)]
    for k, say in ((3, None), (1, None), (2, jnp.logical_not(last_y)), (0, jnp.logical_not(last_x))):

        def signal():
            pl.semaphore_signal(barrier, inc=1, device_id=edge_to[k], device_id_type=MESH)

        signal() if say is None else pl.when(say)(signal)

    part, times, timed = reader(table0, table1, table2, table3)

    def copy_to(at, source, target, there):
        return pltpu.make_async_remote_copy(src_ref=source, dst_ref=target, send_sem=send_sem.at[at], recv_sem=recv_sem.at[at], device_id=there, device_id_type=MESH)

    loads[0].wait()
    for b in range(4):
        here = slice(8 * b, 8 * b + 8)
        if b % 2 == 0:
            loads[2 * (b // 2) + 1].wait()
            loads[2 * (b // 2) + 2].wait()
        raw = split(jnp.concatenate([fields[f, here].reshape(256, NZ) for f in range(2)], 1))
        rawh[256 * b : 256 * b + 256, :], rawl[256 * b : 256 * b + 256, :] = raw
        value = times("ya", raw).reshape(42, 8, 256)
        states1[:, here, :] = value[:4]
        states2[:, here, :] = value[4:26]
        states3[:, here, :] = value[26:41]
    for f in range(2):
        for j in range(2):
            at = slice(64 * f + 32 * j, 64 * f + 32 * j + 32)
            send_side[0, at, :] = sum(float(OPS[0][1][j, 28 + i]) * fields[f, 28 + i] for i in range(4))
            send_side[1, at, :] = sum(float(OPS[0][2][j, i]) * fields[f, i] for i in range(3))
    for k in range(2):
        for f in range(2):
            send_side[2 + k, 64 * f : 64 * f + 64, :] = states1[2 * k : 2 * k + 2, :, 128 * f : 128 * f + 128].reshape(64, NZ)
    for source, target in ((table2_ref, table2), (table3_ref, table3), (table4_ref, table4)):
        load(source, target)
    def answer(at, k):
        pl.semaphore_signal(relays.at[at], inc=1, device_id=edge_to[k], device_id_type=MESH)

    def relay(below, k):
        answer(2 - 2 * k + below, k)

    pl.semaphore_wait(barrier, 2 + inner_x.astype(jnp.int32) + inner_y.astype(jnp.int32) + sum(first.astype(jnp.int32) for first in earlier))
    pl.when(last_y)(lambda: answer(4, 2))
    pl.when(last_x)(lambda: answer(5, 0))

    @pl.when(last_x & last_y)
    def _():
        pl.semaphore_signal(relays.at[6], inc=1, device_id=corner_to[0], device_id_type=MESH)

    relay(0, 0)
    pl.when(inner_x)(lambda: relay(0, 1))
    pl.when(inner_y)(lambda: relay(1, 0))
    pl.when(inner_x & inner_y)(lambda: relay(1, 1))
    sides = [copy_to(8 + k, send_side.at[k], got_side.at[k], edge_to[k]) for k in range(4)]

    def start_inner(group):
        group[0].start()
        group[2].start()
        pl.when(inner_x)(group[1].start)
        pl.when(inner_y)(group[3].start)

    start_inner(sides)

    loads[5].wait()
    zh, zl = both_of(part, "z23")

    def deep(value, half):
        return deep_of(split(value), half)

    def deep_of(pair, half):
        high, low = pair
        at = slice(128 * half, 128 * half + 128)
        return dot(jnp.concatenate([high, low, high], 1), jnp.concatenate([zh[:, at], zh[:, at], zl[:, at]], 0))

    corners1 = times("c1", split(states1[...].reshape(128, 256)))
    lines2 = split(states2[16:22].reshape(192, 256))
    lines3 = split(states3[8:15].reshape(224, 256))
    deep2 = jnp.concatenate([deep_of(lines2, 0), jnp.zeros((64, NZ), jnp.float32)], 0)
    deep3 = jnp.concatenate([deep_of(lines3, 1), jnp.zeros((32, NZ), jnp.float32)], 0)
    both = split(jnp.concatenate([deep2, deep3], 1))
    corners1 = timed(split(jnp.concatenate([corners1[:, :128], corners1[:, 128:]], 0)), "z1")
    value = times("c23", both)
    corners2, corners3 = value[:64, :128], value[64:, 128:]
    along_y = both
    row = lax.broadcasted_iota(jnp.int32, (8, NZ), 0)
    lane = lax.broadcasted_iota(jnp.int32, (8, NZ), 1)

    def beside(value, at, apart, step):
        if step == 8:
            return jnp.where(lane < 64, value[at : at + 8], value[at + apart : at + apart + 8])
        pairs = value[at : at + 16].reshape(8, 2, NZ)
        return jnp.where(lane < 64, pairs[:, 0], pairs[:, 1])

    for c in range(4):
        send_corner[c, 0:8, :] = jnp.where(row < 4, corners1[8 * c : 8 * c + 8], corners1[32 + 8 * c : 40 + 8 * c])
        send_corner[c, 8:24, :] = corners2[16 * c : 16 * c + 16]
        send_corner[c, 24:32, :] = beside(corners3, 16 * c, 1, 1)
    copies = [copy_to(c, send_corner.at[c], got_corner.at[c], corner_to[c]) for c in range(4)]
    for c in range(4):
        pl.when(earlier[c])(copies[c].start)
    loads[6].wait()
    value = [times("e2", split(states2[8 * c : 8 * c + 8].reshape(256, 256))) for c in range(2)]
    rows2 = [value[c][8 * j : 8 * j + 8] for j in range(6) for c in range(2)]
    rows3 = times("e3", split(states3[0:8].reshape(256, 256)))[:56]
    sides_y = times("n23", along_y)
    value = deep(jnp.concatenate(rows2, 0), 0)
    for k in range(2):
        send_edge[k, 0:48, :] = value[48 * k : 48 * k + 48]
        send_edge[2 + k, 0:48, :] = sides_y[48 * k : 48 * k + 48, :128]
    value = jnp.concatenate([deep(rows3, 1), sides_y[96:152, 128:]], 0)
    for axis in range(2):
        at = 56 * axis
        send_edge[2 * axis, 48:56, :] = beside(value, at, 8, 8)
        send_edge[2 * axis, 56:64, :] = beside(value, at + 16, 8, 8)
        send_edge[2 * axis + 1, 48:56, :] = beside(value, at + 32, 8, 8)
        send_edge[2 * axis + 1, 56:64, :] = jnp.where(lane < 64, value[at + 48 : at + 56], 0.0)
    edges = [copy_to(4 + k, send_edge.at[k], got_edge.at[k], edge_to[k]) for k in range(4)]
    start_inner(edges)

    loads[7].wait()
    value = [times("o2", split(states2[8 * c : 8 * c + 8].reshape(256, 256))) for c in range(2)]
    value = deep(jnp.concatenate([value[c][8 * x : 8 * x + 8] for x in range(16) for c in range(2)], 0), 0)
    level2[...] = value
    value = deep(times("o3", split(states3[0:8].reshape(256, 256))), 1)
    level3[...] = jnp.where(lax.broadcasted_iota(jnp.int32, (64, NZ), 1) < 64, value, 0.0)
    own = part("u1")[:, :192]
    for b in range(4):
        rows = slice(256 * b, 256 * b + 256)
        high, low = rawh[rows, :], rawl[rows, :]
        high, low = split(jnp.concatenate([timed((high[:, at : at + 128], low[:, at : at + 128]), "z1") for at in (0, 128)], 1))
        for p in range(4):
            at = slice(64 * p, 64 * p + 64)
            lines[4 * b + p] = dot(own, jnp.concatenate([high[at], low[at], high[at]], 0))
    for f in range(2):
        for t in range(4):
            value = lift_own([lines[i // 2, 32 * (i % 2) + 8 * t : 32 * (i % 2) + 8 * t + 8, 128 * f : 128 * f + 128] for i in range(N)])
            for i in range(N):
                own1[f, i, 8 * t : 8 * t + 8, :] = value[i]

    def wait_and_send(c):
        pl.semaphore_wait(relays.at[c], 1)
        copies[c].start()

    for c in (0, 1):
        pl.when(relayed[c])(lambda: wait_and_send(c))

    @pl.when(first_x)
    def _():
        pl.semaphore_wait(relays.at[5], 1)
        relay(0, 1)
        pl.when(inner_y)(lambda: relay(1, 1))
        edges[1].start()
        sides[1].start()

    pl.when(relayed[2])(lambda: wait_and_send(2))

    @pl.when(first_y)
    def _():
        pl.semaphore_wait(relays.at[4], 1)
        relay(1, 0)
        relay(1, 1)
        edges[3].start()
        sides[3].start()
        copies[1].start()
        pl.when(inner_x)(copies[3].start)

    pl.when(relayed[3])(lambda: wait_and_send(3))

    @pl.when(first_x & first_y)
    def _():
        pl.semaphore_wait(relays.at[6], 1)
        copies[3].start()

    for copy in sides:
        copy.wait()
    gains = (OPS[0][3], OPS[0][4])
    both = []
    for axis in range(2):
        value = [got_side[2 * axis + k, 64 * f : 64 * f + 64, :] for f in range(2) for k in range(2)]
        value = jnp.concatenate([jnp.concatenate(value[:2], 0), jnp.concatenate(value[2:], 0)], 1)
        value = times("x1", split(value))
        both.append(timed(split(jnp.concatenate([value[:, :128], value[:, 128:]], 0)), "z1"))
    got_side[0], got_side[1] = both[1][:128], both[1][128:]
    for f in range(2):
        for k, xs in enumerate(((0, 1, 2), (28, 29, 30, 31))):
            for x in xs:
                own1[f, x] += sum(float(gains[k][x, j]) * both[0][128 * f + 64 * k + 32 * j : 128 * f + 64 * k + 32 * j + 32] for j in range(2))
        for k in range(2):
            cols = [column(gains[k][:, j], 24 * k) for j in range(2)]
            for x in range(N):
                own1[f, x, 24 * k : 24 * k + 8, :] += sum(cols[j] * got_side[f, 64 * k + 32 * j + x : 64 * k + 32 * j + x + 1, :] for j in range(2))

    loads[8].wait()
    for c in range(4):
        pl.when(jnp.logical_not(relayed[c]))(lambda: pl.semaphore_wait(relays.at[c], 1))
    for copy in copies + edges:
        copy.wait()


def finish(own1, got_edge, got_corner, level2, level3, table4, out0_ref, out1_ref, even, odd, out_sem):
    part, times, _ = reader(None, None, None, None, table4)
    outs = (out0_ref, out1_ref)
    stores = []

    def store(at, source, target):
        stores.append(pltpu.make_async_copy(source, target, out_sem.at[at]))
        stores[-1].start()

    for f in range(2):
        store(f, own1.at[f, pl.ds(1, 13), 1], outs[f].at[pl.ds(1, 13), 1])

    parts2 = [got_edge[k, 0:48, :] for k in range(4)] + [got_corner[c, 8:24, :] for c in range(4)]
    value2 = times("m2", split(jnp.concatenate(parts2, 0))) + level2[...]
    parts3 = [got_edge[k, 48:64, :] for k in range(4)] + [got_corner[c, 24:32, :] for c in range(4)]
    parts3.append(jnp.zeros((32, NZ), jnp.float32))
    value3 = times("m3", split(jnp.concatenate(parts3, 0)))
    value3 = jnp.where(lax.broadcasted_iota(jnp.int32, (64, NZ), 1) < 64, value3[:64], value3[64:]) + level3[...]
    high, low = split(value2)
    value2 = dot(jnp.concatenate([high, low], 1), jnp.concatenate([part("p2")] * 2, 0))
    high, low = split(value3)
    value3 = dot(jnp.concatenate([high, low], 1), jnp.concatenate([part("p3")] * 2, 0))

    gains = (OPS[0][3], OPS[0][4])
    lane = lax.broadcasted_iota(jnp.int32, (16, NZ), 1)
    cols = [[column(gains[k][:, j], 24 * k) for j in range(2)] for k in range(2)]
    for f in range(2):

        def cornered(x):
            value = [own1[f, x // 2, x % 2, 8 * t : 8 * t + 8, :] for t in range(4)]
            for side, xs in enumerate(((0, 1, 2), (28, 29, 30, 31))):
                if x in xs:
                    for k in range(2):
                        for j in range(2):
                            row = sum(float(gains[side][x, i]) * got_corner[2 * side + k, 4 * f + 2 * j + i : 4 * f + 2 * j + i + 1, :] for i in range(2))
                            value[3 * k] += cols[k][j] * row
            return jnp.concatenate(value, 0)

        for i, x in enumerate((1, 29, 31)):
            odd[f, i] = cornered(x)
        store(2 + f, odd.at[f, 0], outs[f].at[0, 1])
        store(4 + f, odd.at[f, pl.ds(1, 2)], outs[f].at[pl.ds(14, 2), 1])
    for f in range(2):
        for p in range(16):
            even[f, p] = cornered(2 * p)
            cells = even[f, p, pl.ds(0, 16, stride=2), :]
            even[f, p, pl.ds(0, 16, stride=2), :] = jnp.where(lane % 2 == 0, value2[16 * p : 16 * p + 16, 128 * f : 128 * f + 128], cells)
            if p % 2 == 0:
                cells = even[f, p, pl.ds(0, 8, stride=4), :]
                even[f, p, pl.ds(0, 8, stride=4), :] = jnp.where(lane[:8] % 4 == 0, value3[4 * p : 4 * p + 8, 128 * f : 128 * f + 128], cells)
            if p % 8 == 7:
                here = pl.ds(p - 7, 8)
                store(6 + 2 * f + p // 8, even.at[f, here], outs[f].at[here, 0])
    for copy in stores:
        copy.wait()


def solution(mesh):
    nx, ny = mesh.shape["dx"], mesh.shape["dy"]
    f32, bf16 = jnp.float32, jnp.bfloat16

    def body(volume_fraction, vorticity):
        inputs = [volume_fraction, vorticity] + [jnp.asarray(table) for table in TABLES]
        inputs = [pltpu.with_memory_space_constraint(value, pltpu.HBM) for value in inputs]
        passed = (
            pltpu.VMEM((2, N, N, NZ), f32),
            pltpu.VMEM((4, 64, NZ), f32),
            pltpu.VMEM((4, 32, NZ), f32),
            pltpu.VMEM((256, NZ), f32),
            pltpu.VMEM((64, NZ), f32),
            pltpu.VMEM(TABLES[4].shape, bf16),
        )
        middle = pl.pallas_call(
            lambda *refs: exchange(nx, ny, *refs),
            out_shape=passed,
            in_specs=[pl.BlockSpec(memory_space=pltpu.HBM)] * 7,
            out_specs=(pl.BlockSpec(memory_space=pltpu.VMEM),) * 6,
            scratch_shapes=[
                pltpu.VMEM((2, N, N, NZ), f32),
                pltpu.VMEM(TABLES[0].shape, bf16),
                pltpu.VMEM(TABLES[1].shape, bf16),
                pltpu.VMEM(TABLES[2].shape, bf16),
                pltpu.VMEM(TABLES[3].shape, bf16),
                pltpu.VMEM((1024, 256), bf16),
                pltpu.VMEM((1024, 256), bf16),
                pltpu.VMEM((4, N, 256), f32),
                pltpu.VMEM((22, N, 256), f32),
                pltpu.VMEM((15, N, 256), f32),
                pltpu.VMEM((16, 64, 256), f32),
                pltpu.VMEM((4, 128, NZ), f32),
                pltpu.VMEM((4, 128, NZ), f32),
                pltpu.VMEM((4, 64, NZ), f32),
                pltpu.VMEM((4, 32, NZ), f32),
                pltpu.SemaphoreType.REGULAR((7,)),
                pltpu.SemaphoreType.DMA((13,)),
                pltpu.SemaphoreType.DMA((12,)),
                pltpu.SemaphoreType.DMA((12,)),
            ],
            compiler_params=pltpu.CompilerParams(
                collective_id=0, has_side_effects=True, vmem_limit_bytes=32 * 1024 * 1024
            ),
        )(*inputs)
        middle = [middle[0].reshape(2, 16, 2, N, NZ)] + list(middle[1:])
        middle = [pltpu.with_memory_space_constraint(value, pltpu.VMEM) for value in middle]
        block = pltpu.HBM((16, 2, N, NZ), f32)
        outs = pl.pallas_call(
            finish,
            out_shape=(block, block),
            in_specs=[pl.BlockSpec(memory_space=pltpu.VMEM)] * 6,
            out_specs=(pl.BlockSpec(memory_space=pltpu.HBM),) * 2,
            scratch_shapes=[
                pltpu.VMEM((2, 16, N, NZ), f32),
                pltpu.VMEM((2, 3, N, NZ), f32),
                pltpu.SemaphoreType.DMA((10,)),
            ],
            compiler_params=pltpu.CompilerParams(vmem_limit_bytes=32 * 1024 * 1024),
        )(*middle)
        return tuple(out.reshape(N, N, NZ) for out in outs)

    placed = P("dx", "dy", None)
    return jax.shard_map(
        body, mesh=mesh, in_specs=(placed, placed), out_specs=(placed, placed), check_vma=False
    )
```

```python
import jax
import jax.numpy as jnp
import numpy as np
from jax import lax
from jax.experimental import pallas as pl
from jax.experimental.pallas import tpu as pltpu
from jax.sharding import PartitionSpec as P

LEVELS = 3
LIFT_ALPHA = -1.586134342
LIFT_BETA = -0.05298011854
LIFT_GAMMA = 0.8829110762
LIFT_DELTA = 0.4435068522
LIFT_KAPPA = 1.149604398
MESH = pl.DeviceIdType.MESH
N = 32
NZ = 128
EDGE_ROWS = 208
CORNER_ROWS = 48


def lift_matrix(count, periodic):
    eye = np.eye(count)
    even, odd = eye[0::2], eye[1::2]
    if periodic:
        following = lambda t: np.roll(t, -1, 0)
        before = lambda t: np.roll(t, 1, 0)
    else:
        following = lambda t: np.concatenate([t[1:], t[-1:]])
        before = lambda t: np.concatenate([t[:1], t[:-1]])
    odd = odd + LIFT_ALPHA * (even + following(even))
    even = even + LIFT_BETA * (before(odd) + odd)
    odd = odd + LIFT_GAMMA * (even + following(even))
    even = even + LIFT_DELTA * (before(odd) + odd)
    out = np.zeros((count, count))
    out[0::2], out[1::2] = even / LIFT_KAPPA, odd * LIFT_KAPPA
    return out


def factor(matrix, rank):
    u, s, vt = np.linalg.svd(matrix)
    assert s[rank:].max() < 1e-12
    return u[:, :rank] * s[:rank], vt[:rank]


def axis_operators():
    found, current = [], np.eye(5 * N)
    for level, (up, down) in enumerate(((2, 2), (3, 3), (4, 3))):
        full = lift_matrix(current.shape[0], True) @ current
        size = N >> level
        rows = full[2 * size : 3 * size]
        gain_left, send_up = factor(rows[:, N : 2 * N], up)
        gain_right, send_down = factor(rows[:, 3 * N : 4 * N], down)
        found.append((rows[:, 2 * N : 3 * N], send_up, send_down, gain_left, gain_right))
        current = full[0::2]
    return found


def depth_operators():
    one = lift_matrix(NZ, False)
    two = lift_matrix(NZ // 2, False) @ one[0::2]
    three = lift_matrix(NZ // 4, False) @ two[0::2]
    return one, two, three


OPS = axis_operators()


def padded(matrix, rows):
    return np.concatenate([matrix, np.zeros((rows - matrix.shape[0],) + matrix.shape[1:])])


def blocks(matrix, count):
    return np.kron(np.eye(count), matrix)


def batched(matrix):
    rows, cols = matrix.shape
    out = np.zeros((rows, 8, 8, cols))
    for i in range(8):
        out[:, i, i, :] = matrix
    return out.reshape(rows * 8, 8 * cols)


def corner_matrix(up, down, stride, rows, split_lanes=False):
    sent = (up, down)
    total = len(up) + len(down)
    out = np.zeros((4, rows, total, N))
    for corner in range(4):
        sx, sy = corner // 2, corner % 2
        for jy in range(len(sent[sy])):
            for jx, line in enumerate(sent[sx]):
                at = 8 * (jx % 2) + 2 * jy + jx // 2 if split_lanes else stride * jy + jx
                out[corner, at, sy * len(up) + jy] = line
        if rows == 8:
            out[corner, 4:] = out[corner, :4]
    return out.reshape(4 * rows, total * N)


def gain_matrix(level):
    gains = OPS[level][3:]
    size = N >> level
    eye = np.eye(size)
    if level == 2:
        gains = [np.pad(gain, ((0, 0), (0, 4 - gain.shape[1]))) for gain in gains]
    parts = [np.einsum("xj,yv->xyjv", gain, eye).reshape(size * size, -1) for gain in gains]
    parts += [np.einsum("yj,xv->xyjv", gain, eye).reshape(size * size, -1) for gain in gains]
    four = [np.pad(gain, ((0, 0), (0, 4 - gain.shape[1]))) for gain in gains]
    for corner in range(4):
        parts.append(np.einsum("xi,yj->xyji", four[corner // 2], four[corner % 2]).reshape(size * size, 16))
    if level == 2:
        for i, width in enumerate([8] * 4 + [1] * 4):
            states = parts[i].reshape(size * size, -1, 2, width)
            parts[i] = np.concatenate([states[:, :, half].reshape(size * size, -1) for half in range(2)])
        out = np.concatenate(parts, 1)
        return np.pad(out, ((0, 0), (0, 128 - out.shape[1])))
    return wide(np.concatenate(parts, 1))


def halves(matrix):
    high = np.asarray(matrix, jnp.bfloat16)
    low = np.asarray(matrix - high.astype(np.float64), jnp.bfloat16)
    return high, low


def wide(matrix):
    return np.pad(matrix, ((0, 0), (0, 256 - matrix.shape[1])))


def tables():
    one, two, three = depth_operators()
    depth = np.zeros((2, NZ, 256))
    for f in range(2):
        depth[f, :, 64 * f : 64 * f + 64] = two.T
        for half in (128, 192):
            depth[f, :, half + 32 * f : half + 32 * f + 32] = three.T
    own = [ops[0] for ops in OPS]
    up = [ops[1] for ops in OPS]
    down = [ops[2] for ops in OPS]
    sent = [np.concatenate([p, q]) for p, q in zip(up, down)]
    spread2 = np.zeros((2, 64, 2, NZ))
    spread3 = np.zeros((4, 32, 2, NZ))
    for f in range(2):
        for i in range(64):
            spread2[f, i, f, 2 * i] = 1
        for i in range(32):
            spread3[f, i, f, 4 * i] = spread3[2 + f, i, f, 4 * i] = 1
    groups = [
        {"ys": batched(np.concatenate(sent))},
        {
            "c1": corner_matrix(up[0], down[0], 2, 8),
            "c23": np.concatenate([wide(corner_matrix(up[1], down[1], 4, 16)), wide(corner_matrix(up[2], down[2], 4, 16, True))]),
            "z1": one.T,
            "z23": depth.reshape(256, 256),
        },
        {
            "yo": batched(np.concatenate(own[1:])),
            "e2": batched(sent[1]),
            "e3": batched(sent[2]),
            "n23": np.concatenate([wide(blocks(own[1], 6)), wide(blocks(own[2], 7))]),
        },
        {"o2": batched(own[1]), "o3": batched(own[2]), "x1": blocks(own[0], 4)},
        {"m2": gain_matrix(1), "m3": gain_matrix(2)},
    ]
    packed, where = [], {}
    for group, pairs in enumerate(groups):
        arrays = []

        def put(name, array):
            extra = -array.shape[0] % 16
            where[name] = (group, sum(len(other) for other in arrays), array.shape[0] + extra)
            arrays.append(np.pad(array, ((0, extra), (0, 0))))

        for name, matrix in pairs.items():
            high, low = halves(matrix)
            if name == "ys":
                put(name, np.concatenate([np.pad(half, ((0, 8), (0, 0))) for half in (high, low)]))
            elif matrix.shape[1] == 128:
                put(name, np.concatenate([high, low], 1))
            else:
                put(name + "h", high)
                put(name + "l", low)
        if group == 3:
            high, low = halves(blocks(own[0], 2))
            put("u1", wide(np.concatenate([high, high, low], 1)))
        if group == 4:
            put("p2", np.asarray(spread2.reshape(128, 256), jnp.bfloat16))
            put("p3", np.asarray(spread3.reshape(128, 256), jnp.bfloat16))
        packed.append(np.concatenate(arrays))
    return packed, where


TABLES, WHERE = tables()


def split(value):
    high = value.astype(jnp.bfloat16)
    return high, (value - high.astype(jnp.float32)).astype(jnp.bfloat16)


def dot(a, b):
    return jnp.dot(a, b, preferred_element_type=jnp.float32)


def column(gain, first):
    row = lax.broadcasted_iota(jnp.int32, (8, NZ), 0)
    out = jnp.zeros((8, NZ), jnp.float32)
    for i in range(8):
        if abs(gain[first + i]) > 1e-13:
            out = jnp.where(row == i, jnp.float32(gain[first + i]), out)
    return out


def lift_own(lines):
    pairs = N // 2
    even = lines[0::2]
    odd = lines[1::2]
    zero = jnp.zeros_like(even[0])
    odd = [LIFT_ALPHA * even[0]] + [odd[i] + LIFT_ALPHA * (even[i] + (even[i + 1] if i + 1 < pairs else zero)) for i in range(pairs)]
    even = [LIFT_BETA * odd[0]] + [even[i] + LIFT_BETA * (odd[i] + odd[i + 1]) for i in range(pairs)] + [LIFT_BETA * odd[pairs]]
    odd = [odd[i] + LIFT_GAMMA * (even[i] + even[i + 1]) for i in range(pairs + 1)]
    out = []
    for i in range(pairs):
        out.append((even[i + 1] + LIFT_DELTA * (odd[i] + odd[i + 1])) * (1.0 / LIFT_KAPPA))
        out.append(odd[i + 1] * LIFT_KAPPA)
    return out


def both_of(part, name):
    if name in WHERE:
        return part(name)[:, :128], part(name)[:, 128:]
    return part(name + "h"), part(name + "l")


def reader(*refs):
    def part(name):
        group, at, rows = WHERE[name]
        return refs[group][at : at + rows, :]

    def times(name, pair):
        (ah, al), (bh, bl) = both_of(part, name), pair
        value = dot(jnp.concatenate([ah, al], 0), bh)
        return value[: ah.shape[0]] + value[ah.shape[0] :] + dot(ah, bl)

    def timed(pair, name):
        (ah, al), (bh, bl) = pair, both_of(part, name)
        value = dot(jnp.concatenate([ah, al], 0), bh)
        return value[: ah.shape[0]] + value[ah.shape[0] :] + dot(ah, bl)

    return part, times, timed


def exchange(nx, ny, v0_ref, v1_ref, table0_ref, table1_ref, table2_ref, table3_ref, table4_ref, own1, got_edge, got_corner, level2, level3, table4, fields, table0, table1, table2, table3, rawh, rawl, states1, states2, states3, lines, send_side, got_side, send_edge, send_corner, relays, in_sem, send_sem, recv_sem):
    loads = []

    def load(source, target):
        loads.append(pltpu.make_async_copy(source, target, in_sem.at[len(loads)]))
        loads[-1].start()

    load(table0_ref, table0)
    for b in range(2):
        for f, ref in enumerate((v0_ref, v1_ref)):
            load(ref.at[pl.ds(16 * b, 16)], fields.at[f, pl.ds(16 * b, 16)])
    load(table1_ref, table1)
    ix, iy = lax.axis_index("dx"), lax.axis_index("dy")
    right, left = lax.rem(ix + 1, nx), lax.rem(ix + nx - 1, nx)
    above, below = lax.rem(iy + 1, ny), lax.rem(iy + ny - 1, ny)
    edge_to = [(right, iy), (left, iy), (ix, above), (ix, below)]
    corner_to = [(right, above), (right, below), (left, above), (left, below)]


    def rank(tx, ty):
        return 3 * tx + 2 * ty + 20 * lax.div(2 * ty, ny)

    earlier = [rank(tx, ty) < rank(ix, iy) for tx, ty in corner_to]
    barrier = pltpu.get_barrier_semaphore()
    for there, first in zip(corner_to, earlier):

        @pl.when(jnp.logical_not(first))
        def _():
            pl.semaphore_signal(barrier, inc=1, device_id=there, device_id_type=MESH)

    first_x, last_x, first_y, last_y = ix == 0, ix == nx - 1, iy == 0, iy == ny - 1
    inner_x, inner_y = jnp.logical_not(first_x), jnp.logical_not(first_y)
    relayed = [jnp.logical_not(e) for e in (earlier[0], earlier[1] | first_y, earlier[2], earlier[3] | first_y)]
    for k, say in ((3, None), (1, None), (2, jnp.logical_not(last_y)), (0, jnp.logical_not(last_x))):

        def signal():
            pl.semaphore_signal(barrier, inc=1, device_id=edge_to[k], device_id_type=MESH)

        signal() if say is None else pl.when(say)(signal)

    part, times, timed = reader(table0, table1, table2, table3)

    def copy_to(at, source, target, there):
        return pltpu.make_async_remote_copy(src_ref=source, dst_ref=target, send_sem=send_sem.at[at], recv_sem=recv_sem.at[at], device_id=there, device_id_type=MESH)

    loads[0].wait()
    for b in range(4):
        here = slice(8 * b, 8 * b + 8)
        if b % 2 == 0:
            loads[2 * (b // 2) + 1].wait()
            loads[2 * (b // 2) + 2].wait()
        raw = split(jnp.concatenate([fields[f, here].reshape(256, NZ) for f in range(2)], 1))
        rawh[256 * b : 256 * b + 256, :], rawl[256 * b : 256 * b + 256, :] = raw
        value = dot(part("ys"), raw[0])
        value = (value[:144] + value[144:] + dot(part("ys")[:144], raw[1])).reshape(18, 8, 256)
        states1[:, here, :] = value[:4]
        states2[16:22, here, :] = value[4:10]
        states3[8:15, here, :] = value[10:17]
    for f in range(2):
        for j in range(2):
            at = slice(64 * f + 32 * j, 64 * f + 32 * j + 32)
            send_side[0, at, :] = sum(float(OPS[0][1][j, 28 + i]) * fields[f, 28 + i] for i in range(4))
            send_side[1, at, :] = sum(float(OPS[0][2][j, i]) * fields[f, i] for i in range(3))
    for k in range(2):
        for f in range(2):
            send_side[2 + k, 64 * f : 64 * f + 64, :] = states1[2 * k : 2 * k + 2, :, 128 * f : 128 * f + 128].reshape(64, NZ)
    for source, target in ((table2_ref, table2), (table3_ref, table3), (table4_ref, table4)):
        load(source, target)
    def answer(at, k):
        pl.semaphore_signal(relays.at[at], inc=1, device_id=edge_to[k], device_id_type=MESH)

    def relay(below, k):
        answer(2 - 2 * k + below, k)

    pl.semaphore_wait(barrier, 2 + inner_x.astype(jnp.int32) + inner_y.astype(jnp.int32) + sum(first.astype(jnp.int32) for first in earlier))
    pl.when(last_y)(lambda: answer(4, 2))
    pl.when(last_x)(lambda: answer(5, 0))

    @pl.when(last_x & last_y)
    def _():
        pl.semaphore_signal(relays.at[6], inc=1, device_id=corner_to[0], device_id_type=MESH)

    relay(0, 0)
    pl.when(inner_x)(lambda: relay(0, 1))
    pl.when(inner_y)(lambda: relay(1, 0))
    pl.when(inner_x & inner_y)(lambda: relay(1, 1))
    sides = [copy_to(8 + k, send_side.at[k], got_side.at[k], edge_to[k]) for k in range(4)]

    def start_inner(group):
        group[0].start()
        group[2].start()
        pl.when(inner_x)(group[1].start)
        pl.when(inner_y)(group[3].start)

    start_inner(sides)

    loads[5].wait()
    zh, zl = both_of(part, "z23")

    def deep(value, half):
        return deep_of(split(value), half)

    def deep_of(pair, half):
        high, low = pair
        at = slice(128 * half, 128 * half + 128)
        value = dot(jnp.concatenate([high, low], 0), zh[:, at])
        return value[: high.shape[0]] + value[high.shape[0] :] + dot(high, zl[:, at])

    corners1 = times("c1", split(states1[...].reshape(128, 256)))
    lines2 = split(states2[16:22].reshape(192, 256))
    lines3 = split(states3[8:15].reshape(224, 256))
    deep2 = jnp.concatenate([deep_of(lines2, 0), jnp.zeros((64, NZ), jnp.float32)], 0)
    deep3 = jnp.concatenate([deep_of(lines3, 1), jnp.zeros((32, NZ), jnp.float32)], 0)
    both = split(jnp.concatenate([deep2, deep3], 1))
    corners1 = timed(split(jnp.concatenate([corners1[:, :128], corners1[:, 128:]], 0)), "z1")
    value = times("c23", both)
    corners2, corners3 = value[:64, :128], value[64:, 128:]
    along_y = both
    row = lax.broadcasted_iota(jnp.int32, (8, NZ), 0)
    lane = lax.broadcasted_iota(jnp.int32, (8, NZ), 1)

    def beside(value, at):
        return jnp.where(lane < 64, value[at : at + 8], value[at + 8 : at + 16])

    for c in range(4):
        send_corner[c, 0:8, :] = jnp.where(row < 4, corners1[8 * c : 8 * c + 8], corners1[32 + 8 * c : 40 + 8 * c])
        send_corner[c, 8:24, :] = corners2[16 * c : 16 * c + 16]
        send_corner[c, 24:32, :] = beside(corners3, 16 * c)
    copies = [copy_to(c, send_corner.at[c], got_corner.at[c], corner_to[c]) for c in range(4)]
    for c in range(4):
        pl.when(earlier[c])(copies[c].start)
    loads[6].wait()
    for b in range(4):
        here = slice(8 * b, 8 * b + 8)
        raw = rawh[256 * b : 256 * b + 256, :], rawl[256 * b : 256 * b + 256, :]
        value = times("yo", raw).reshape(24, 8, 256)
        states2[0:16, here, :] = value[:16]
        states3[0:8, here, :] = value[16:]
    value = [times("e2", split(states2[8 * c : 8 * c + 8].reshape(256, 256))) for c in range(2)]
    rows2 = [value[c][8 * j : 8 * j + 8] for j in range(6) for c in range(2)]
    rows3 = times("e3", split(states3[0:8].reshape(256, 256)))[:56]
    sides_y = times("n23", along_y)
    value = deep(jnp.concatenate(rows2, 0), 0)
    for k in range(2):
        send_edge[k, 0:48, :] = value[48 * k : 48 * k + 48]
        send_edge[2 + k, 0:48, :] = sides_y[48 * k : 48 * k + 48, :128]
    value = jnp.concatenate([deep(rows3, 1), sides_y[96:152, 128:]], 0)
    for axis in range(2):
        at = 56 * axis
        send_edge[2 * axis, 48:56, :] = beside(value, at)
        send_edge[2 * axis, 56:64, :] = beside(value, at + 16)
        send_edge[2 * axis + 1, 48:56, :] = beside(value, at + 32)
        send_edge[2 * axis + 1, 56:64, :] = jnp.where(lane < 64, value[at + 48 : at + 56], 0.0)
    edges = [copy_to(4 + k, send_edge.at[k], got_edge.at[k], edge_to[k]) for k in range(4)]
    start_inner(edges)

    loads[7].wait()
    value = [times("o2", split(states2[8 * c : 8 * c + 8].reshape(256, 256))) for c in range(2)]
    value = deep(jnp.concatenate([value[c][8 * x : 8 * x + 8] for x in range(16) for c in range(2)], 0), 0)
    level2[...] = value
    value = deep(times("o3", split(states3[0:8].reshape(256, 256))), 1)
    level3[...] = jnp.where(lax.broadcasted_iota(jnp.int32, (64, NZ), 1) < 64, value, 0.0)
    own = part("u1")[:, :192]
    for b in range(4):
        rows = slice(256 * b, 256 * b + 256)
        high, low = rawh[rows, :], rawl[rows, :]
        high, low = split(jnp.concatenate([timed((high[:, at : at + 128], low[:, at : at + 128]), "z1") for at in (0, 128)], 1))
        for p in range(4):
            at = slice(64 * p, 64 * p + 64)
            lines[4 * b + p] = dot(own, jnp.concatenate([high[at], low[at], high[at]], 0))
    for f in range(2):
        for t in range(4):
            value = lift_own([lines[i // 2, 32 * (i % 2) + 8 * t : 32 * (i % 2) + 8 * t + 8, 128 * f : 128 * f + 128] for i in range(N)])
            for i in range(N):
                own1[f, i, 8 * t : 8 * t + 8, :] = value[i]

    def wait_and_send(c):
        pl.semaphore_wait(relays.at[c], 1)
        copies[c].start()

    for c in (0, 1):
        pl.when(relayed[c])(lambda: wait_and_send(c))

    @pl.when(first_x)
    def _():
        pl.semaphore_wait(relays.at[5], 1)
        relay(0, 1)
        pl.when(inner_y)(lambda: relay(1, 1))
        edges[1].start()
        sides[1].start()

    pl.when(relayed[2])(lambda: wait_and_send(2))

    @pl.when(first_y)
    def _():
        pl.semaphore_wait(relays.at[4], 1)
        relay(1, 0)
        relay(1, 1)
        edges[3].start()
        sides[3].start()
        copies[1].start()
        pl.when(inner_x)(copies[3].start)

    pl.when(relayed[3])(lambda: wait_and_send(3))

    @pl.when(first_x & first_y)
    def _():
        pl.semaphore_wait(relays.at[6], 1)
        copies[3].start()

    for copy in sides:
        copy.wait()
    gains = (OPS[0][3], OPS[0][4])
    both = []
    for axis in range(2):
        value = [got_side[2 * axis + k, 64 * f : 64 * f + 64, :] for f in range(2) for k in range(2)]
        value = jnp.concatenate([jnp.concatenate(value[:2], 0), jnp.concatenate(value[2:], 0)], 1)
        value = times("x1", split(value))
        both.append(timed(split(jnp.concatenate([value[:, :128], value[:, 128:]], 0)), "z1"))
    got_side[0], got_side[1] = both[1][:128], both[1][128:]
    for f in range(2):
        for k, xs in enumerate(((0, 1, 2), (28, 29, 30, 31))):
            for x in xs:
                own1[f, x] += sum(float(gains[k][x, j]) * both[0][128 * f + 64 * k + 32 * j : 128 * f + 64 * k + 32 * j + 32] for j in range(2))
        for k in range(2):
            cols = [column(gains[k][:, j], 24 * k) for j in range(2)]
            for x in range(N):
                own1[f, x, 24 * k : 24 * k + 8, :] += sum(cols[j] * got_side[f, 64 * k + 32 * j + x : 64 * k + 32 * j + x + 1, :] for j in range(2))

    loads[8].wait()
    for c in range(4):
        pl.when(jnp.logical_not(relayed[c]))(lambda: pl.semaphore_wait(relays.at[c], 1))
    for copy in copies + edges:
        copy.wait()


def finish(own1, got_edge, got_corner, level2, level3, table4, out0_ref, out1_ref, even, odd, out_sem):
    part, times, _ = reader(None, None, None, None, table4)
    outs = (out0_ref, out1_ref)
    stores = []

    def store(at, source, target):
        stores.append(pltpu.make_async_copy(source, target, out_sem.at[at]))
        stores[-1].start()

    for f in range(2):
        store(f, own1.at[f, pl.ds(1, 13), 1], outs[f].at[pl.ds(1, 13), 1])

    parts2 = [got_edge[k, 0:48, :] for k in range(4)] + [got_corner[c, 8:24, :] for c in range(4)]
    value2 = times("m2", split(jnp.concatenate(parts2, 0))) + level2[...]
    parts3 = [got_edge[k, 48:64, :] for k in range(4)] + [got_corner[c, 24:32, :] for c in range(4)]
    parts3.append(jnp.zeros((32, NZ), jnp.float32))
    value3 = times("m3", split(jnp.concatenate(parts3, 0)))
    value3 = jnp.where(lax.broadcasted_iota(jnp.int32, (64, NZ), 1) < 64, value3[:64], value3[64:]) + level3[...]
    high, low = split(value2)
    value2 = dot(jnp.concatenate([high, low], 1), jnp.concatenate([part("p2")] * 2, 0))
    high, low = split(value3)
    value3 = dot(jnp.concatenate([high, low], 1), jnp.concatenate([part("p3")] * 2, 0))

    gains = (OPS[0][3], OPS[0][4])
    lane = lax.broadcasted_iota(jnp.int32, (16, NZ), 1)
    cols = [[column(gains[k][:, j], 24 * k) for j in range(2)] for k in range(2)]
    for f in range(2):

        def cornered(x):
            value = [own1[f, x // 2, x % 2, 8 * t : 8 * t + 8, :] for t in range(4)]
            for side, xs in enumerate(((0, 1, 2), (28, 29, 30, 31))):
                if x in xs:
                    for k in range(2):
                        for j in range(2):
                            row = sum(float(gains[side][x, i]) * got_corner[2 * side + k, 4 * f + 2 * j + i : 4 * f + 2 * j + i + 1, :] for i in range(2))
                            value[3 * k] += cols[k][j] * row
            return jnp.concatenate(value, 0)

        for i, x in enumerate((1, 29, 31)):
            odd[f, i] = cornered(x)
        store(2 + f, odd.at[f, 0], outs[f].at[0, 1])
        store(4 + f, odd.at[f, pl.ds(1, 2)], outs[f].at[pl.ds(14, 2), 1])
    for f in range(2):
        for p in range(16):
            even[f, p] = cornered(2 * p)
            cells = even[f, p, pl.ds(0, 16, stride=2), :]
            even[f, p, pl.ds(0, 16, stride=2), :] = jnp.where(lane % 2 == 0, value2[16 * p : 16 * p + 16, 128 * f : 128 * f + 128], cells)
            if p % 2 == 0:
                cells = even[f, p, pl.ds(0, 8, stride=4), :]
                even[f, p, pl.ds(0, 8, stride=4), :] = jnp.where(lane[:8] % 4 == 0, value3[4 * p : 4 * p + 8, 128 * f : 128 * f + 128], cells)
            if p % 8 == 7:
                here = pl.ds(p - 7, 8)
                store(6 + 2 * f + p // 8, even.at[f, here], outs[f].at[here, 0])
    for copy in stores:
        copy.wait()


def solution(mesh):
    nx, ny = mesh.shape["dx"], mesh.shape["dy"]
    f32, bf16 = jnp.float32, jnp.bfloat16

    def body(volume_fraction, vorticity):
        inputs = [volume_fraction, vorticity] + [jnp.asarray(table) for table in TABLES]
        inputs = [pltpu.with_memory_space_constraint(value, pltpu.HBM) for value in inputs]
        passed = (
            pltpu.VMEM((2, N, N, NZ), f32),
            pltpu.VMEM((4, 64, NZ), f32),
            pltpu.VMEM((4, 32, NZ), f32),
            pltpu.VMEM((256, NZ), f32),
            pltpu.VMEM((64, NZ), f32),
            pltpu.VMEM(TABLES[4].shape, bf16),
        )
        middle = pl.pallas_call(
            lambda *refs: exchange(nx, ny, *refs),
            out_shape=passed,
            in_specs=[pl.BlockSpec(memory_space=pltpu.HBM)] * 7,
            out_specs=(pl.BlockSpec(memory_space=pltpu.VMEM),) * 6,
            scratch_shapes=[
                pltpu.VMEM((2, N, N, NZ), f32),
                pltpu.VMEM(TABLES[0].shape, bf16),
                pltpu.VMEM(TABLES[1].shape, bf16),
                pltpu.VMEM(TABLES[2].shape, bf16),
                pltpu.VMEM(TABLES[3].shape, bf16),
                pltpu.VMEM((1024, 256), bf16),
                pltpu.VMEM((1024, 256), bf16),
                pltpu.VMEM((4, N, 256), f32),
                pltpu.VMEM((22, N, 256), f32),
                pltpu.VMEM((15, N, 256), f32),
                pltpu.VMEM((16, 64, 256), f32),
                pltpu.VMEM((4, 128, NZ), f32),
                pltpu.VMEM((4, 128, NZ), f32),
                pltpu.VMEM((4, 64, NZ), f32),
                pltpu.VMEM((4, 32, NZ), f32),
                pltpu.SemaphoreType.REGULAR((7,)),
                pltpu.SemaphoreType.DMA((13,)),
                pltpu.SemaphoreType.DMA((12,)),
                pltpu.SemaphoreType.DMA((12,)),
            ],
            compiler_params=pltpu.CompilerParams(
                collective_id=0, has_side_effects=True, vmem_limit_bytes=32 * 1024 * 1024
            ),
        )(*inputs)
        middle = [middle[0].reshape(2, 16, 2, N, NZ)] + list(middle[1:])
        middle = [pltpu.with_memory_space_constraint(value, pltpu.VMEM) for value in middle]
        block = pltpu.HBM((16, 2, N, NZ), f32)
        outs = pl.pallas_call(
            finish,
            out_shape=(block, block),
            in_specs=[pl.BlockSpec(memory_space=pltpu.VMEM)] * 6,
            out_specs=(pl.BlockSpec(memory_space=pltpu.HBM),) * 2,
            scratch_shapes=[
                pltpu.VMEM((2, 16, N, NZ), f32),
                pltpu.VMEM((2, 3, N, NZ), f32),
                pltpu.SemaphoreType.DMA((10,)),
            ],
            compiler_params=pltpu.CompilerParams(vmem_limit_bytes=32 * 1024 * 1024),
        )(*middle)
        return tuple(out.reshape(N, N, NZ) for out in outs)

    placed = P("dx", "dy", None)
    return jax.shard_map(
        body, mesh=mesh, in_specs=(placed, placed), out_specs=(placed, placed), check_vma=False
    )
```

```python
import jax
import jax.numpy as jnp
import numpy as np
from jax import lax
from jax.experimental import pallas as pl
from jax.experimental.pallas import tpu as pltpu
from jax.sharding import PartitionSpec as P

LEVELS = 3
LIFT_ALPHA = -1.586134342
LIFT_BETA = -0.05298011854
LIFT_GAMMA = 0.8829110762
LIFT_DELTA = 0.4435068522
LIFT_KAPPA = 1.149604398
MESH = pl.DeviceIdType.MESH
N = 32
NZ = 128
EDGE_ROWS = 208
CORNER_ROWS = 48


def lift_matrix(count, periodic):
    eye = np.eye(count)
    even, odd = eye[0::2], eye[1::2]
    if periodic:
        following = lambda t: np.roll(t, -1, 0)
        before = lambda t: np.roll(t, 1, 0)
    else:
        following = lambda t: np.concatenate([t[1:], t[-1:]])
        before = lambda t: np.concatenate([t[:1], t[:-1]])
    odd = odd + LIFT_ALPHA * (even + following(even))
    even = even + LIFT_BETA * (before(odd) + odd)
    odd = odd + LIFT_GAMMA * (even + following(even))
    even = even + LIFT_DELTA * (before(odd) + odd)
    out = np.zeros((count, count))
    out[0::2], out[1::2] = even / LIFT_KAPPA, odd * LIFT_KAPPA
    return out


def factor(matrix, rank):
    u, s, vt = np.linalg.svd(matrix)
    assert s[rank:].max() < 1e-12
    return u[:, :rank] * s[:rank], vt[:rank]


def axis_operators():
    found, current = [], np.eye(5 * N)
    for level, (up, down) in enumerate(((2, 2), (3, 3), (4, 3))):
        full = lift_matrix(current.shape[0], True) @ current
        size = N >> level
        rows = full[2 * size : 3 * size]
        gain_left, send_up = factor(rows[:, N : 2 * N], up)
        gain_right, send_down = factor(rows[:, 3 * N : 4 * N], down)
        found.append((rows[:, 2 * N : 3 * N], send_up, send_down, gain_left, gain_right))
        current = full[0::2]
    return found


def depth_operators():
    one = lift_matrix(NZ, False)
    two = lift_matrix(NZ // 2, False) @ one[0::2]
    three = lift_matrix(NZ // 4, False) @ two[0::2]
    return one, two, three


OPS = axis_operators()


def padded(matrix, rows):
    return np.concatenate([matrix, np.zeros((rows - matrix.shape[0],) + matrix.shape[1:])])


def blocks(matrix, count):
    return np.kron(np.eye(count), matrix)


def batched(matrix):
    rows, cols = matrix.shape
    out = np.zeros((rows, 8, 8, cols))
    for i in range(8):
        out[:, i, i, :] = matrix
    return out.reshape(rows * 8, 8 * cols)


def corner_matrix(up, down, stride, rows, split_lanes=False):
    sent = (up, down)
    total = len(up) + len(down)
    out = np.zeros((4, rows, total, N))
    for corner in range(4):
        sx, sy = corner // 2, corner % 2
        for jy in range(len(sent[sy])):
            for jx, line in enumerate(sent[sx]):
                at = 8 * (jx % 2) + 2 * jy + jx // 2 if split_lanes else stride * jy + jx
                out[corner, at, sy * len(up) + jy] = line
        if rows == 8:
            out[corner, 4:] = out[corner, :4]
    return out.reshape(4 * rows, total * N)


def gain_matrix(level):
    gains = OPS[level][3:]
    size = N >> level
    eye = np.eye(size)
    if level == 2:
        gains = [np.pad(gain, ((0, 0), (0, 4 - gain.shape[1]))) for gain in gains]
    parts = [np.einsum("xj,yv->xyjv", gain, eye).reshape(size * size, -1) for gain in gains]
    parts += [np.einsum("yj,xv->xyjv", gain, eye).reshape(size * size, -1) for gain in gains]
    four = [np.pad(gain, ((0, 0), (0, 4 - gain.shape[1]))) for gain in gains]
    for corner in range(4):
        parts.append(np.einsum("xi,yj->xyji", four[corner // 2], four[corner % 2]).reshape(size * size, 16))
    if level == 2:
        for i, width in enumerate([8] * 4 + [1] * 4):
            states = parts[i].reshape(size * size, -1, 2, width)
            parts[i] = np.concatenate([states[:, :, half].reshape(size * size, -1) for half in range(2)])
        out = np.concatenate(parts, 1)
        return np.pad(out, ((0, 0), (0, 128 - out.shape[1])))
    return wide(np.concatenate(parts, 1))


def halves(matrix):
    high = np.asarray(matrix, jnp.bfloat16)
    low = np.asarray(matrix - high.astype(np.float64), jnp.bfloat16)
    return high, low


def wide(matrix):
    return np.pad(matrix, ((0, 0), (0, 256 - matrix.shape[1])))


def tables():
    one, two, three = depth_operators()
    depth = np.zeros((2, NZ, 256))
    for f in range(2):
        depth[f, :, 64 * f : 64 * f + 64] = two.T
        for half in (128, 192):
            depth[f, :, half + 32 * f : half + 32 * f + 32] = three.T
    own = [ops[0] for ops in OPS]
    up = [ops[1] for ops in OPS]
    down = [ops[2] for ops in OPS]
    sent = [np.concatenate([p, q]) for p, q in zip(up, down)]
    spread2 = np.zeros((2, 64, 2, NZ))
    spread3 = np.zeros((4, 32, 2, NZ))
    for f in range(2):
        for i in range(64):
            spread2[f, i, f, 2 * i] = 1
        for i in range(32):
            spread3[f, i, f, 4 * i] = spread3[2 + f, i, f, 4 * i] = 1
    groups = [
        {"ys": batched(np.concatenate(sent))},
        {
            "c1": corner_matrix(up[0], down[0], 2, 8),
            "c23": np.concatenate([wide(corner_matrix(up[1], down[1], 4, 16)), wide(corner_matrix(up[2], down[2], 4, 16, True))]),
            "z1": one.T,
            "z23": depth.reshape(256, 256),
        },
        {
            "yo": batched(np.concatenate(own[1:])),
            "e2": batched(sent[1]),
            "e3": batched(sent[2]),
            "n23": np.concatenate([wide(blocks(own[1], 6)), wide(blocks(own[2], 7))]),
        },
        {"o2": batched(own[1]), "o3": batched(own[2]), "x1": blocks(own[0], 4)},
        {"m2": gain_matrix(1), "m3": gain_matrix(2)},
    ]
    packed, where = [], {}
    for group, pairs in enumerate(groups):
        arrays = []

        def put(name, array):
            extra = -array.shape[0] % 16
            where[name] = (group, sum(len(other) for other in arrays), array.shape[0] + extra)
            arrays.append(np.pad(array, ((0, extra), (0, 0))))

        for name, matrix in pairs.items():
            high, low = halves(matrix)
            if name == "ys":
                put(name, np.concatenate([np.pad(half, ((0, 8), (0, 0))) for half in (high, low)]))
            elif matrix.shape[1] == 128:
                put(name, np.concatenate([high, low], 1))
            else:
                put(name + "h", high)
                put(name + "l", low)
        if group == 3:
            high, low = halves(blocks(own[0], 2))
            put("u1", wide(np.concatenate([high, high, low], 1)))
        if group == 4:
            put("p2", np.asarray(spread2.reshape(128, 256), jnp.bfloat16))
            put("p3", np.asarray(spread3.reshape(128, 256), jnp.bfloat16))
        packed.append(np.concatenate(arrays))
    return packed, where


TABLES, WHERE = tables()


def split(value):
    high = value.astype(jnp.bfloat16)
    return high, (value - high.astype(jnp.float32)).astype(jnp.bfloat16)


def dot(a, b):
    return jnp.dot(a, b, preferred_element_type=jnp.float32)


def column(gain, first):
    row = lax.broadcasted_iota(jnp.int32, (8, NZ), 0)
    out = jnp.zeros((8, NZ), jnp.float32)
    for i in range(8):
        if abs(gain[first + i]) > 1e-13:
            out = jnp.where(row == i, jnp.float32(gain[first + i]), out)
    return out


def lift_own(lines):
    pairs = N // 2
    even = lines[0::2]
    odd = lines[1::2]
    zero = jnp.zeros_like(even[0])
    odd = [LIFT_ALPHA * even[0]] + [odd[i] + LIFT_ALPHA * (even[i] + (even[i + 1] if i + 1 < pairs else zero)) for i in range(pairs)]
    even = [LIFT_BETA * odd[0]] + [even[i] + LIFT_BETA * (odd[i] + odd[i + 1]) for i in range(pairs)] + [LIFT_BETA * odd[pairs]]
    odd = [odd[i] + LIFT_GAMMA * (even[i] + even[i + 1]) for i in range(pairs + 1)]
    out = []
    for i in range(pairs):
        out.append((even[i + 1] + LIFT_DELTA * (odd[i] + odd[i + 1])) * (1.0 / LIFT_KAPPA))
        out.append(odd[i + 1] * LIFT_KAPPA)
    return out


def both_of(part, name):
    if name in WHERE:
        return part(name)[:, :128], part(name)[:, 128:]
    return part(name + "h"), part(name + "l")


def reader(*refs):
    def part(name):
        group, at, rows = WHERE[name]
        return refs[group][at : at + rows, :]

    def times(name, pair):
        (ah, al), (bh, bl) = both_of(part, name), pair
        value = dot(jnp.concatenate([ah, al], 0), bh)
        return value[: ah.shape[0]] + value[ah.shape[0] :] + dot(ah, bl)

    def timed(pair, name):
        (ah, al), (bh, bl) = pair, both_of(part, name)
        value = dot(jnp.concatenate([ah, al], 0), bh)
        return value[: ah.shape[0]] + value[ah.shape[0] :] + dot(ah, bl)

    return part, times, timed


def exchange(nx, ny, v0_ref, v1_ref, table0_ref, table1_ref, table2_ref, table3_ref, table4_ref, own1, got_edge, got_corner, level2, level3, table4, fields, table0, table1, table2, table3, rawh, rawl, states1, states2, states3, lines, send_side, got_side, send_edge, send_corner, relays, in_sem, send_sem, recv_sem):
    loads = []

    def load(source, target):
        loads.append(pltpu.make_async_copy(source, target, in_sem.at[len(loads)]))
        loads[-1].start()

    load(table0_ref, table0)
    for b in range(2):
        for f, ref in enumerate((v0_ref, v1_ref)):
            load(ref.at[pl.ds(16 * b, 16)], fields.at[f, pl.ds(16 * b, 16)])
    load(table1_ref, table1)
    ix, iy = lax.axis_index("dx"), lax.axis_index("dy")
    right, left = lax.rem(ix + 1, nx), lax.rem(ix + nx - 1, nx)
    above, below = lax.rem(iy + 1, ny), lax.rem(iy + ny - 1, ny)
    edge_to = [(right, iy), (left, iy), (ix, above), (ix, below)]
    corner_to = [(right, above), (right, below), (left, above), (left, below)]


    def rank(tx, ty):
        return 3 * tx + 2 * ty + 20 * lax.div(2 * ty, ny)

    earlier = [rank(tx, ty) < rank(ix, iy) for tx, ty in corner_to]
    barrier = pltpu.get_barrier_semaphore()
    for there, first in zip(corner_to, earlier):

        @pl.when(jnp.logical_not(first))
        def _():
            pl.semaphore_signal(barrier, inc=1, device_id=there, device_id_type=MESH)

    first_x, last_x, first_y, last_y = ix == 0, ix == nx - 1, iy == 0, iy == ny - 1
    inner_x, inner_y = jnp.logical_not(first_x), jnp.logical_not(first_y)
    relayed = [jnp.logical_not(e) for e in (earlier[0], earlier[1] | first_y, earlier[2], earlier[3] | first_y)]
    for k, say in ((3, None), (1, None), (2, jnp.logical_not(last_y)), (0, jnp.logical_not(last_x))):

        def signal():
            pl.semaphore_signal(barrier, inc=1, device_id=edge_to[k], device_id_type=MESH)

        signal() if say is None else pl.when(say)(signal)

    part, times, timed = reader(table0, table1, table2, table3)

    def copy_to(at, source, target, there):
        return pltpu.make_async_remote_copy(src_ref=source, dst_ref=target, send_sem=send_sem.at[at], recv_sem=recv_sem.at[at], device_id=there, device_id_type=MESH)

    loads[0].wait()
    for b in range(4):
        here = slice(8 * b, 8 * b + 8)
        if b % 2 == 0:
            loads[2 * (b // 2) + 1].wait()
            loads[2 * (b // 2) + 2].wait()
        raw = split(jnp.concatenate([fields[f, here].reshape(256, NZ) for f in range(2)], 1))
        rawh[256 * b : 256 * b + 256, :], rawl[256 * b : 256 * b + 256, :] = raw
        value = dot(part("ys"), raw[0])
        value = (value[:144] + value[144:] + dot(part("ys")[:144], raw[1])).reshape(18, 8, 256)
        states1[:, here, :] = value[:4]
        states2[16:22, here, :] = value[4:10]
        states3[8:15, here, :] = value[10:17]
    for f in range(2):
        for j in range(2):
            at = slice(64 * f + 32 * j, 64 * f + 32 * j + 32)
            send_side[0, at, :] = sum(float(OPS[0][1][j, 28 + i]) * fields[f, 28 + i] for i in range(4))
            send_side[1, at, :] = sum(float(OPS[0][2][j, i]) * fields[f, i] for i in range(3))
    for k in range(2):
        for f in range(2):
            send_side[2 + k, 64 * f : 64 * f + 64, :] = states1[2 * k : 2 * k + 2, :, 128 * f : 128 * f + 128].reshape(64, NZ)
    for source, target in ((table2_ref, table2), (table3_ref, table3), (table4_ref, table4)):
        load(source, target)
    def answer(at, k):
        pl.semaphore_signal(relays.at[at], inc=1, device_id=edge_to[k], device_id_type=MESH)

    def relay(below, k):
        answer(2 - 2 * k + below, k)

    pl.semaphore_wait(barrier, 2 + inner_x.astype(jnp.int32) + inner_y.astype(jnp.int32) + sum(first.astype(jnp.int32) for first in earlier))
    pl.when(last_y)(lambda: answer(4, 2))
    pl.when(last_x)(lambda: answer(5, 0))

    @pl.when(last_x & last_y)
    def _():
        pl.semaphore_signal(relays.at[6], inc=1, device_id=corner_to[0], device_id_type=MESH)

    relay(0, 0)
    pl.when(inner_x)(lambda: relay(0, 1))
    pl.when(inner_y)(lambda: relay(1, 0))
    pl.when(inner_x & inner_y)(lambda: relay(1, 1))
    sides = [copy_to(8 + k, send_side.at[k], got_side.at[k], edge_to[k]) for k in range(4)]

    def start_inner(group):
        group[0].start()
        group[2].start()
        pl.when(inner_x)(group[1].start)
        pl.when(inner_y)(group[3].start)

    start_inner(sides)

    loads[5].wait()
    zh, zl = both_of(part, "z23")

    def deep(value, half):
        return deep_of(split(value), half)

    def deep_of(pair, half):
        high, low = pair
        at = slice(128 * half, 128 * half + 128)
        value = dot(jnp.concatenate([high, low], 0), zh[:, at])
        return value[: high.shape[0]] + value[high.shape[0] :] + dot(high, zl[:, at])

    lines2 = split(states2[16:22].reshape(192, 256))
    lines3 = split(states3[8:15].reshape(224, 256))
    deep2 = jnp.concatenate([deep_of(lines2, 0), jnp.zeros((64, NZ), jnp.float32)], 0)
    deep3 = jnp.concatenate([deep_of(lines3, 1), jnp.zeros((32, NZ), jnp.float32)], 0)
    both = split(jnp.concatenate([deep2, deep3], 1))
    value = times("c23", both)
    corners1 = times("c1", split(states1[...].reshape(128, 256)))
    corners1 = timed(split(jnp.concatenate([corners1[:, :128], corners1[:, 128:]], 0)), "z1")
    corners2, corners3 = value[:64, :128], value[64:, 128:]
    along_y = both
    row = lax.broadcasted_iota(jnp.int32, (8, NZ), 0)
    lane = lax.broadcasted_iota(jnp.int32, (8, NZ), 1)

    def beside(value, at):
        return jnp.where(lane < 64, value[at : at + 8], value[at + 8 : at + 16])

    for c in range(4):
        send_corner[c, 0:8, :] = jnp.where(row < 4, corners1[8 * c : 8 * c + 8], corners1[32 + 8 * c : 40 + 8 * c])
        send_corner[c, 8:24, :] = corners2[16 * c : 16 * c + 16]
        send_corner[c, 24:32, :] = beside(corners3, 16 * c)
    copies = [copy_to(c, send_corner.at[c], got_corner.at[c], corner_to[c]) for c in range(4)]
    for c in range(4):
        pl.when(earlier[c])(copies[c].start)
    loads[6].wait()
    for b in range(4):
        here = slice(8 * b, 8 * b + 8)
        raw = rawh[256 * b : 256 * b + 256, :], rawl[256 * b : 256 * b + 256, :]
        value = times("yo", raw).reshape(24, 8, 256)
        states2[0:16, here, :] = value[:16]
        states3[0:8, here, :] = value[16:]
    value = [times("e2", split(states2[8 * c : 8 * c + 8].reshape(256, 256))) for c in range(2)]
    rows2 = [value[c][8 * j : 8 * j + 8] for j in range(6) for c in range(2)]
    rows3 = times("e3", split(states3[0:8].reshape(256, 256)))[:56]
    sides_y = times("n23", along_y)
    value = deep(jnp.concatenate(rows2, 0), 0)
    for k in range(2):
        send_edge[k, 0:48, :] = value[48 * k : 48 * k + 48]
        send_edge[2 + k, 0:48, :] = sides_y[48 * k : 48 * k + 48, :128]
    value = jnp.concatenate([deep(rows3, 1), sides_y[96:152, 128:]], 0)
    for axis in range(2):
        at = 56 * axis
        send_edge[2 * axis, 48:56, :] = beside(value, at)
        send_edge[2 * axis, 56:64, :] = beside(value, at + 16)
        send_edge[2 * axis + 1, 48:56, :] = beside(value, at + 32)
        send_edge[2 * axis + 1, 56:64, :] = jnp.where(lane < 64, value[at + 48 : at + 56], 0.0)
    edges = [copy_to(4 + k, send_edge.at[k], got_edge.at[k], edge_to[k]) for k in range(4)]
    start_inner(edges)

    loads[7].wait()
    value = [times("o2", split(states2[8 * c : 8 * c + 8].reshape(256, 256))) for c in range(2)]
    value = deep(jnp.concatenate([value[c][8 * x : 8 * x + 8] for x in range(16) for c in range(2)], 0), 0)
    level2[...] = value
    value = deep(times("o3", split(states3[0:8].reshape(256, 256))), 1)
    level3[...] = jnp.where(lax.broadcasted_iota(jnp.int32, (64, NZ), 1) < 64, value, 0.0)
    own = part("u1")[:, :192]
    for b in range(4):
        rows = slice(256 * b, 256 * b + 256)
        high, low = rawh[rows, :], rawl[rows, :]
        high, low = split(jnp.concatenate([timed((high[:, at : at + 128], low[:, at : at + 128]), "z1") for at in (0, 128)], 1))
        for p in range(4):
            at = slice(64 * p, 64 * p + 64)
            lines[4 * b + p] = dot(own, jnp.concatenate([high[at], low[at], high[at]], 0))
    for f in range(2):
        for t in range(4):
            value = lift_own([lines[i // 2, 32 * (i % 2) + 8 * t : 32 * (i % 2) + 8 * t + 8, 128 * f : 128 * f + 128] for i in range(N)])
            for i in range(N):
                own1[f, i, 8 * t : 8 * t + 8, :] = value[i]

    def wait_and_send(c):
        pl.semaphore_wait(relays.at[c], 1)
        copies[c].start()

    for c in (0, 1):
        pl.when(relayed[c])(lambda: wait_and_send(c))

    @pl.when(first_x)
    def _():
        pl.semaphore_wait(relays.at[5], 1)
        relay(0, 1)
        pl.when(inner_y)(lambda: relay(1, 1))
        edges[1].start()
        sides[1].start()

    pl.when(relayed[2])(lambda: wait_and_send(2))

    @pl.when(first_y)
    def _():
        pl.semaphore_wait(relays.at[4], 1)
        relay(1, 0)
        relay(1, 1)
        edges[3].start()
        sides[3].start()
        copies[1].start()
        pl.when(inner_x)(copies[3].start)

    pl.when(relayed[3])(lambda: wait_and_send(3))

    @pl.when(first_x & first_y)
    def _():
        pl.semaphore_wait(relays.at[6], 1)
        copies[3].start()

    for copy in sides:
        copy.wait()
    gains = (OPS[0][3], OPS[0][4])
    both = []
    for axis in range(2):
        value = [got_side[2 * axis + k, 64 * f : 64 * f + 64, :] for f in range(2) for k in range(2)]
        value = jnp.concatenate([jnp.concatenate(value[:2], 0), jnp.concatenate(value[2:], 0)], 1)
        value = times("x1", split(value))
        both.append(timed(split(jnp.concatenate([value[:, :128], value[:, 128:]], 0)), "z1"))
    got_side[0], got_side[1] = both[1][:128], both[1][128:]
    for f in range(2):
        for k, xs in enumerate(((0, 1, 2), (28, 29, 30, 31))):
            for x in xs:
                own1[f, x] += sum(float(gains[k][x, j]) * both[0][128 * f + 64 * k + 32 * j : 128 * f + 64 * k + 32 * j + 32] for j in range(2))
        for k in range(2):
            cols = [column(gains[k][:, j], 24 * k) for j in range(2)]
            for x in range(N):
                own1[f, x, 24 * k : 24 * k + 8, :] += sum(cols[j] * got_side[f, 64 * k + 32 * j + x : 64 * k + 32 * j + x + 1, :] for j in range(2))

    loads[8].wait()
    for c in range(4):
        pl.when(jnp.logical_not(relayed[c]))(lambda: pl.semaphore_wait(relays.at[c], 1))
    for copy in edges:
        copy.wait()
    for copy in copies:
        copy.wait_send()
    for c in (3, 2, 1, 0):
        copies[c].wait_recv()


def finish(own1, got_edge, got_corner, level2, level3, table4, out0_ref, out1_ref, even, odd, out_sem):
    part, times, _ = reader(None, None, None, None, table4)
    outs = (out0_ref, out1_ref)
    stores = []

    def store(at, source, target):
        stores.append(pltpu.make_async_copy(source, target, out_sem.at[at]))
        stores[-1].start()

    for f in range(2):
        store(f, own1.at[f, pl.ds(1, 13), 1], outs[f].at[pl.ds(1, 13), 1])

    parts2 = [got_edge[k, 0:48, :] for k in range(4)] + [got_corner[c, 8:24, :] for c in range(4)]
    value2 = times("m2", split(jnp.concatenate(parts2, 0))) + level2[...]
    parts3 = [got_edge[k, 48:64, :] for k in range(4)] + [got_corner[c, 24:32, :] for c in range(4)]
    parts3.append(jnp.zeros((32, NZ), jnp.float32))
    value3 = times("m3", split(jnp.concatenate(parts3, 0)))
    value3 = jnp.where(lax.broadcasted_iota(jnp.int32, (64, NZ), 1) < 64, value3[:64], value3[64:]) + level3[...]
    high, low = split(value2)
    value2 = dot(jnp.concatenate([high, low], 1), jnp.concatenate([part("p2")] * 2, 0))
    high, low = split(value3)
    value3 = dot(jnp.concatenate([high, low], 1), jnp.concatenate([part("p3")] * 2, 0))

    gains = (OPS[0][3], OPS[0][4])
    lane = lax.broadcasted_iota(jnp.int32, (16, NZ), 1)
    cols = [[column(gains[k][:, j], 24 * k) for j in range(2)] for k in range(2)]
    for f in range(2):

        def cornered(x):
            value = [own1[f, x // 2, x % 2, 8 * t : 8 * t + 8, :] for t in range(4)]
            for side, xs in enumerate(((0, 1, 2), (28, 29, 30, 31))):
                if x in xs:
                    for k in range(2):
                        for j in range(2):
                            row = sum(float(gains[side][x, i]) * got_corner[2 * side + k, 4 * f + 2 * j + i : 4 * f + 2 * j + i + 1, :] for i in range(2))
                            value[3 * k] += cols[k][j] * row
            return jnp.concatenate(value, 0)

        for i, x in enumerate((1, 29, 31)):
            odd[f, i] = cornered(x)
        store(2 + f, odd.at[f, 0], outs[f].at[0, 1])
        store(4 + f, odd.at[f, pl.ds(1, 2)], outs[f].at[pl.ds(14, 2), 1])
    for f in range(2):
        for p in range(16):
            even[f, p] = cornered(2 * p)
            cells = even[f, p, pl.ds(0, 16, stride=2), :]
            even[f, p, pl.ds(0, 16, stride=2), :] = jnp.where(lane % 2 == 0, value2[16 * p : 16 * p + 16, 128 * f : 128 * f + 128], cells)
            if p % 2 == 0:
                cells = even[f, p, pl.ds(0, 8, stride=4), :]
                even[f, p, pl.ds(0, 8, stride=4), :] = jnp.where(lane[:8] % 4 == 0, value3[4 * p : 4 * p + 8, 128 * f : 128 * f + 128], cells)
            if p % 8 == 7:
                here = pl.ds(p - 7, 8)
                store(6 + 2 * f + p // 8, even.at[f, here], outs[f].at[here, 0])
    for copy in stores:
        copy.wait()


def solution(mesh):
    nx, ny = mesh.shape["dx"], mesh.shape["dy"]
    f32, bf16 = jnp.float32, jnp.bfloat16

    def body(volume_fraction, vorticity):
        inputs = [volume_fraction, vorticity] + [jnp.asarray(table) for table in TABLES]
        inputs = [pltpu.with_memory_space_constraint(value, pltpu.HBM) for value in inputs]
        passed = (
            pltpu.VMEM((2, N, N, NZ), f32),
            pltpu.VMEM((4, 64, NZ), f32),
            pltpu.VMEM((4, 32, NZ), f32),
            pltpu.VMEM((256, NZ), f32),
            pltpu.VMEM((64, NZ), f32),
            pltpu.VMEM(TABLES[4].shape, bf16),
        )
        middle = pl.pallas_call(
            lambda *refs: exchange(nx, ny, *refs),
            out_shape=passed,
            in_specs=[pl.BlockSpec(memory_space=pltpu.HBM)] * 7,
            out_specs=(pl.BlockSpec(memory_space=pltpu.VMEM),) * 6,
            scratch_shapes=[
                pltpu.VMEM((2, N, N, NZ), f32),
                pltpu.VMEM(TABLES[0].shape, bf16),
                pltpu.VMEM(TABLES[1].shape, bf16),
                pltpu.VMEM(TABLES[2].shape, bf16),
                pltpu.VMEM(TABLES[3].shape, bf16),
                pltpu.VMEM((1024, 256), bf16),
                pltpu.VMEM((1024, 256), bf16),
                pltpu.VMEM((4, N, 256), f32),
                pltpu.VMEM((22, N, 256), f32),
                pltpu.VMEM((15, N, 256), f32),
                pltpu.VMEM((16, 64, 256), f32),
                pltpu.VMEM((4, 128, NZ), f32),
                pltpu.VMEM((4, 128, NZ), f32),
                pltpu.VMEM((4, 64, NZ), f32),
                pltpu.VMEM((4, 32, NZ), f32),
                pltpu.SemaphoreType.REGULAR((7,)),
                pltpu.SemaphoreType.DMA((13,)),
                pltpu.SemaphoreType.DMA((12,)),
                pltpu.SemaphoreType.DMA((12,)),
            ],
            compiler_params=pltpu.CompilerParams(
                collective_id=0, has_side_effects=True, vmem_limit_bytes=32 * 1024 * 1024
            ),
        )(*inputs)
        middle = [middle[0].reshape(2, 16, 2, N, NZ)] + list(middle[1:])
        middle = [pltpu.with_memory_space_constraint(value, pltpu.VMEM) for value in middle]
        block = pltpu.HBM((16, 2, N, NZ), f32)
        outs = pl.pallas_call(
            finish,
            out_shape=(block, block),
            in_specs=[pl.BlockSpec(memory_space=pltpu.VMEM)] * 6,
            out_specs=(pl.BlockSpec(memory_space=pltpu.HBM),) * 2,
            scratch_shapes=[
                pltpu.VMEM((2, 16, N, NZ), f32),
                pltpu.VMEM((2, 3, N, NZ), f32),
                pltpu.SemaphoreType.DMA((10,)),
            ],
            compiler_params=pltpu.CompilerParams(vmem_limit_bytes=32 * 1024 * 1024),
        )(*middle)
        return tuple(out.reshape(N, N, NZ) for out in outs)

    placed = P("dx", "dy", None)
    return jax.shard_map(
        body, mesh=mesh, in_specs=(placed, placed), out_specs=(placed, placed), check_vma=False
    )
```

```python
import jax
import jax.numpy as jnp
import numpy as np
from jax import lax
from jax.experimental import pallas as pl
from jax.experimental.pallas import tpu as pltpu
from jax.sharding import PartitionSpec as P

LEVELS = 3
LIFT_ALPHA = -1.586134342
LIFT_BETA = -0.05298011854
LIFT_GAMMA = 0.8829110762
LIFT_DELTA = 0.4435068522
LIFT_KAPPA = 1.149604398
MESH = pl.DeviceIdType.MESH
N = 32
NZ = 128
EDGE_ROWS = 208
CORNER_ROWS = 48


def lift_matrix(count, periodic):
    eye = np.eye(count)
    even, odd = eye[0::2], eye[1::2]
    if periodic:
        following = lambda t: np.roll(t, -1, 0)
        before = lambda t: np.roll(t, 1, 0)
    else:
        following = lambda t: np.concatenate([t[1:], t[-1:]])
        before = lambda t: np.concatenate([t[:1], t[:-1]])
    odd = odd + LIFT_ALPHA * (even + following(even))
    even = even + LIFT_BETA * (before(odd) + odd)
    odd = odd + LIFT_GAMMA * (even + following(even))
    even = even + LIFT_DELTA * (before(odd) + odd)
    out = np.zeros((count, count))
    out[0::2], out[1::2] = even / LIFT_KAPPA, odd * LIFT_KAPPA
    return out


def factor(matrix, rank):
    u, s, vt = np.linalg.svd(matrix)
    assert s[rank:].max() < 1e-12
    return u[:, :rank] * s[:rank], vt[:rank]


def axis_operators():
    found, current = [], np.eye(5 * N)
    for level, (up, down) in enumerate(((2, 2), (3, 3), (4, 3))):
        full = lift_matrix(current.shape[0], True) @ current
        size = N >> level
        rows = full[2 * size : 3 * size]
        gain_left, send_up = factor(rows[:, N : 2 * N], up)
        gain_right, send_down = factor(rows[:, 3 * N : 4 * N], down)
        found.append((rows[:, 2 * N : 3 * N], send_up, send_down, gain_left, gain_right))
        current = full[0::2]
    return found


def depth_operators():
    one = lift_matrix(NZ, False)
    two = lift_matrix(NZ // 2, False) @ one[0::2]
    three = lift_matrix(NZ // 4, False) @ two[0::2]
    return one, two, three


OPS = axis_operators()


def padded(matrix, rows):
    return np.concatenate([matrix, np.zeros((rows - matrix.shape[0],) + matrix.shape[1:])])


def blocks(matrix, count):
    return np.kron(np.eye(count), matrix)


def batched(matrix):
    rows, cols = matrix.shape
    out = np.zeros((rows, 8, 8, cols))
    for i in range(8):
        out[:, i, i, :] = matrix
    return out.reshape(rows * 8, 8 * cols)


def corner_matrix(up, down, stride, rows, split_lanes=False):
    sent = (up, down)
    total = len(up) + len(down)
    out = np.zeros((4, rows, total, N))
    for corner in range(4):
        sx, sy = corner // 2, corner % 2
        for jy in range(len(sent[sy])):
            for jx, line in enumerate(sent[sx]):
                at = 8 * (jx % 2) + 2 * jy + jx // 2 if split_lanes else stride * jy + jx
                out[corner, at, sy * len(up) + jy] = line
        if rows == 8:
            out[corner, 4:] = out[corner, :4]
    return out.reshape(4 * rows, total * N)


def gain_matrix(level):
    gains = OPS[level][3:]
    size = N >> level
    eye = np.eye(size)
    if level == 2:
        gains = [np.pad(gain, ((0, 0), (0, 4 - gain.shape[1]))) for gain in gains]
    parts = [np.einsum("xj,yv->xyjv", gain, eye).reshape(size * size, -1) for gain in gains]
    parts += [np.einsum("yj,xv->xyjv", gain, eye).reshape(size * size, -1) for gain in gains]
    four = [np.pad(gain, ((0, 0), (0, 4 - gain.shape[1]))) for gain in gains]
    for corner in range(4):
        parts.append(np.einsum("xi,yj->xyji", four[corner // 2], four[corner % 2]).reshape(size * size, 16))
    if level == 2:
        for i, width in enumerate([8] * 4 + [1] * 4):
            states = parts[i].reshape(size * size, -1, 2, width)
            parts[i] = np.concatenate([states[:, :, half].reshape(size * size, -1) for half in range(2)])
        out = np.concatenate(parts, 1)
        return np.pad(out, ((0, 0), (0, 128 - out.shape[1])))
    return wide(np.concatenate(parts, 1))


def halves(matrix):
    high = np.asarray(matrix, jnp.bfloat16)
    low = np.asarray(matrix - high.astype(np.float64), jnp.bfloat16)
    return high, low


def wide(matrix):
    return np.pad(matrix, ((0, 0), (0, 256 - matrix.shape[1])))


def tables():
    one, two, three = depth_operators()
    depth = np.zeros((2, NZ, 256))
    for f in range(2):
        depth[f, :, 64 * f : 64 * f + 64] = two.T
        for half in (128, 192):
            depth[f, :, half + 32 * f : half + 32 * f + 32] = three.T
    own = [ops[0] for ops in OPS]
    up = [ops[1] for ops in OPS]
    down = [ops[2] for ops in OPS]
    sent = [np.concatenate([p, q]) for p, q in zip(up, down)]
    spread2 = np.zeros((2, 64, 2, NZ))
    spread3 = np.zeros((4, 32, 2, NZ))
    for f in range(2):
        for i in range(64):
            spread2[f, i, f, 2 * i] = 1
        for i in range(32):
            spread3[f, i, f, 4 * i] = spread3[2 + f, i, f, 4 * i] = 1
    groups = [
        {"ys": batched(np.concatenate(sent))},
        {
            "c1": corner_matrix(up[0], down[0], 2, 8),
            "c23": np.concatenate([wide(corner_matrix(up[1], down[1], 4, 16)), wide(corner_matrix(up[2], down[2], 4, 16, True))]),
            "z1": one.T,
            "z23": depth.reshape(256, 256),
        },
        {
            "yo": batched(np.concatenate(own[1:])),
            "e2": batched(sent[1]),
            "e3": batched(sent[2]),
            "n23": np.concatenate([wide(blocks(own[1], 6)), wide(blocks(own[2], 7))]),
        },
        {"o2": batched(own[1]), "o3": batched(own[2]), "x1": blocks(own[0], 4)},
        {"m2": gain_matrix(1), "m3": gain_matrix(2)},
    ]
    packed, where = [], {}
    for group, pairs in enumerate(groups):
        arrays = []

        def put(name, array):
            extra = -array.shape[0] % 16
            where[name] = (group, sum(len(other) for other in arrays), array.shape[0] + extra)
            arrays.append(np.pad(array, ((0, extra), (0, 0))))

        for name, matrix in pairs.items():
            high, low = halves(matrix)
            if name == "ys":
                put(name, np.concatenate([np.pad(half, ((0, 8), (0, 0))) for half in (high, low)]))
            elif matrix.shape[1] == 128:
                put(name, np.concatenate([high, low], 1))
            else:
                put(name + "h", high)
                put(name + "l", low)
        if group == 3:
            high, low = halves(blocks(own[0], 2))
            put("u1", wide(np.concatenate([high, high, low], 1)))
        if group == 4:
            put("p2", np.asarray(spread2.reshape(128, 256), jnp.bfloat16))
            put("p3", np.asarray(spread3.reshape(128, 256), jnp.bfloat16))
        packed.append(np.concatenate(arrays))
    return packed, where


TABLES, WHERE = tables()


def split(value):
    high = value.astype(jnp.bfloat16)
    return high, (value - high.astype(jnp.float32)).astype(jnp.bfloat16)


def dot(a, b):
    return jnp.dot(a, b, preferred_element_type=jnp.float32)


def column(gain, first):
    row = lax.broadcasted_iota(jnp.int32, (8, NZ), 0)
    out = jnp.zeros((8, NZ), jnp.float32)
    for i in range(8):
        if abs(gain[first + i]) > 1e-13:
            out = jnp.where(row == i, jnp.float32(gain[first + i]), out)
    return out


def lift_own(lines):
    pairs = N // 2
    even = lines[0::2]
    odd = lines[1::2]
    zero = jnp.zeros_like(even[0])
    odd = [LIFT_ALPHA * even[0]] + [odd[i] + LIFT_ALPHA * (even[i] + (even[i + 1] if i + 1 < pairs else zero)) for i in range(pairs)]
    even = [LIFT_BETA * odd[0]] + [even[i] + LIFT_BETA * (odd[i] + odd[i + 1]) for i in range(pairs)] + [LIFT_BETA * odd[pairs]]
    odd = [odd[i] + LIFT_GAMMA * (even[i] + even[i + 1]) for i in range(pairs + 1)]
    out = []
    for i in range(pairs):
        out.append((even[i + 1] + LIFT_DELTA * (odd[i] + odd[i + 1])) * (1.0 / LIFT_KAPPA))
        out.append(odd[i + 1] * LIFT_KAPPA)
    return out


def both_of(part, name):
    if name in WHERE:
        return part(name)[:, :128], part(name)[:, 128:]
    return part(name + "h"), part(name + "l")


def reader(*refs):
    def part(name):
        group, at, rows = WHERE[name]
        return refs[group][at : at + rows, :]

    def times(name, pair):
        (ah, al), (bh, bl) = both_of(part, name), pair
        value = dot(jnp.concatenate([ah, al], 0), bh)
        return value[: ah.shape[0]] + value[ah.shape[0] :] + dot(ah, bl)

    def timed(pair, name):
        (ah, al), (bh, bl) = pair, both_of(part, name)
        value = dot(jnp.concatenate([ah, al], 0), bh)
        return value[: ah.shape[0]] + value[ah.shape[0] :] + dot(ah, bl)

    return part, times, timed


def exchange(nx, ny, v0_ref, v1_ref, table0_ref, table1_ref, table2_ref, table3_ref, table4_ref, own1, got_edge, got_corner, level2, level3, table4, fields, table0, table1, table2, table3, rawh, rawl, states1, states2, states3, lines, send_side, got_side, send_edge, send_corner, relays, in_sem, send_sem, recv_sem):
    loads = []

    def load(source, target):
        loads.append(pltpu.make_async_copy(source, target, in_sem.at[len(loads)]))
        loads[-1].start()

    load(table0_ref, table0)
    for b in range(2):
        for f, ref in enumerate((v0_ref, v1_ref)):
            load(ref.at[pl.ds(16 * b, 16)], fields.at[f, pl.ds(16 * b, 16)])
    load(table1_ref, table1)
    ix, iy = lax.axis_index("dx"), lax.axis_index("dy")
    right, left = lax.rem(ix + 1, nx), lax.rem(ix + nx - 1, nx)
    above, below = lax.rem(iy + 1, ny), lax.rem(iy + ny - 1, ny)
    edge_to = [(right, iy), (left, iy), (ix, above), (ix, below)]
    corner_to = [(right, above), (right, below), (left, above), (left, below)]


    def rank(tx, ty):
        return 3 * tx + 2 * ty + 20 * lax.div(2 * ty, ny)

    earlier = [rank(tx, ty) < rank(ix, iy) for tx, ty in corner_to]
    barrier = pltpu.get_barrier_semaphore()
    for there, first in zip(corner_to, earlier):

        @pl.when(jnp.logical_not(first))
        def _():
            pl.semaphore_signal(barrier, inc=1, device_id=there, device_id_type=MESH)

    first_x, last_x, first_y, last_y = ix == 0, ix == nx - 1, iy == 0, iy == ny - 1
    inner_x, inner_y = jnp.logical_not(first_x), jnp.logical_not(first_y)
    relayed = [jnp.logical_not(e) for e in (earlier[0], earlier[1] | first_y, earlier[2], earlier[3] | first_y)]
    for k, say in ((3, None), (1, None), (2, jnp.logical_not(last_y)), (0, jnp.logical_not(last_x))):

        def signal():
            pl.semaphore_signal(barrier, inc=1, device_id=edge_to[k], device_id_type=MESH)

        signal() if say is None else pl.when(say)(signal)

    part, times, timed = reader(table0, table1, table2, table3)

    def copy_to(at, source, target, there):
        return pltpu.make_async_remote_copy(src_ref=source, dst_ref=target, send_sem=send_sem.at[at], recv_sem=recv_sem.at[at], device_id=there, device_id_type=MESH)

    loads[0].wait()
    for b in range(4):
        here = slice(8 * b, 8 * b + 8)
        if b % 2 == 0:
            loads[2 * (b // 2) + 1].wait()
            loads[2 * (b // 2) + 2].wait()
        raw = split(jnp.concatenate([fields[f, here].reshape(256, NZ) for f in range(2)], 1))
        rawh[256 * b : 256 * b + 256, :], rawl[256 * b : 256 * b + 256, :] = raw
        value = dot(part("ys"), raw[0])
        value = (value[:144] + value[144:] + dot(part("ys")[:144], raw[1])).reshape(18, 8, 256)
        states1[:, here, :] = value[:4]
        states2[16:22, here, :] = value[4:10]
        states3[8:15, here, :] = value[10:17]
    for f in range(2):
        for j in range(2):
            at = slice(64 * f + 32 * j, 64 * f + 32 * j + 32)
            send_side[0, at, :] = sum(float(OPS[0][1][j, 28 + i]) * fields[f, 28 + i] for i in range(4))
            send_side[1, at, :] = sum(float(OPS[0][2][j, i]) * fields[f, i] for i in range(3))
    for k in range(2):
        for f in range(2):
            send_side[2 + k, 64 * f : 64 * f + 64, :] = states1[2 * k : 2 * k + 2, :, 128 * f : 128 * f + 128].reshape(64, NZ)
    for source, target in ((table2_ref, table2), (table3_ref, table3), (table4_ref, table4)):
        load(source, target)
    def answer(at, k):
        pl.semaphore_signal(relays.at[at], inc=1, device_id=edge_to[k], device_id_type=MESH)

    def relay(below, k):
        answer(2 - 2 * k + below, k)

    pl.semaphore_wait(barrier, 2 + inner_x.astype(jnp.int32) + inner_y.astype(jnp.int32) + sum(first.astype(jnp.int32) for first in earlier))
    pl.when(last_y)(lambda: answer(4, 2))
    pl.when(last_x)(lambda: answer(5, 0))

    @pl.when(last_x & last_y)
    def _():
        pl.semaphore_signal(relays.at[6], inc=1, device_id=corner_to[0], device_id_type=MESH)

    relay(0, 0)
    pl.when(inner_x)(lambda: relay(0, 1))
    pl.when(inner_y)(lambda: relay(1, 0))
    pl.when(inner_x & inner_y)(lambda: relay(1, 1))
    sides = [copy_to(8 + k, send_side.at[k], got_side.at[k], edge_to[k]) for k in range(4)]

    def start_inner(group):
        group[0].start()
        group[2].start()
        pl.when(inner_x)(group[1].start)
        pl.when(inner_y)(group[3].start)

    start_inner(sides)

    loads[5].wait()
    zh, zl = both_of(part, "z23")

    def deep(value, half):
        return deep_of(split(value), half)

    def deep_of(pair, half):
        high, low = pair
        at = slice(128 * half, 128 * half + 128)
        value = dot(jnp.concatenate([high, low], 0), zh[:, at])
        return value[: high.shape[0]] + value[high.shape[0] :] + dot(high, zl[:, at])

    high, low = split(jnp.concatenate([states2[16:22].reshape(192, 256), states3[8:15].reshape(224, 256)], 0))
    value = dot(jnp.concatenate([high, low], 0), zh)
    value = value[:416] + value[416:] + dot(high, zl)
    deep2 = jnp.concatenate([value[:192, :128], jnp.zeros((64, NZ), jnp.float32)], 0)
    deep3 = jnp.concatenate([value[192:, 128:], jnp.zeros((32, NZ), jnp.float32)], 0)
    both = split(jnp.concatenate([deep2, deep3], 1))
    value = times("c23", both)
    corners1 = times("c1", split(states1[...].reshape(128, 256)))
    corners1 = timed(split(jnp.concatenate([corners1[:, :128], corners1[:, 128:]], 0)), "z1")
    corners2, corners3 = value[:64, :128], value[64:, 128:]
    along_y = both
    row = lax.broadcasted_iota(jnp.int32, (8, NZ), 0)
    lane = lax.broadcasted_iota(jnp.int32, (8, NZ), 1)

    def beside(value, at):
        return jnp.where(lane < 64, value[at : at + 8], value[at + 8 : at + 16])

    for c in range(4):
        send_corner[c, 0:8, :] = jnp.where(row < 4, corners1[8 * c : 8 * c + 8], corners1[32 + 8 * c : 40 + 8 * c])
        send_corner[c, 8:24, :] = corners2[16 * c : 16 * c + 16]
        send_corner[c, 24:32, :] = beside(corners3, 16 * c)
    copies = [copy_to(c, send_corner.at[c], got_corner.at[c], corner_to[c]) for c in range(4)]
    for c in range(4):
        pl.when(earlier[c])(copies[c].start)
    loads[6].wait()
    for b in range(4):
        here = slice(8 * b, 8 * b + 8)
        raw = rawh[256 * b : 256 * b + 256, :], rawl[256 * b : 256 * b + 256, :]
        value = times("yo", raw).reshape(24, 8, 256)
        states2[0:16, here, :] = value[:16]
        states3[0:8, here, :] = value[16:]
    value = [times("e2", split(states2[8 * c : 8 * c + 8].reshape(256, 256))) for c in range(2)]
    rows2 = [value[c][8 * j : 8 * j + 8] for j in range(6) for c in range(2)]
    rows3 = times("e3", split(states3[0:8].reshape(256, 256)))[:56]
    sides_y = times("n23", along_y)
    value = deep(jnp.concatenate(rows2, 0), 0)
    for k in range(2):
        send_edge[k, 0:48, :] = value[48 * k : 48 * k + 48]
        send_edge[2 + k, 0:48, :] = sides_y[48 * k : 48 * k + 48, :128]
    value = jnp.concatenate([deep(rows3, 1), sides_y[96:152, 128:]], 0)
    for axis in range(2):
        at = 56 * axis
        send_edge[2 * axis, 48:56, :] = beside(value, at)
        send_edge[2 * axis, 56:64, :] = beside(value, at + 16)
        send_edge[2 * axis + 1, 48:56, :] = beside(value, at + 32)
        send_edge[2 * axis + 1, 56:64, :] = jnp.where(lane < 64, value[at + 48 : at + 56], 0.0)
    edges = [copy_to(4 + k, send_edge.at[k], got_edge.at[k], edge_to[k]) for k in range(4)]
    start_inner(edges)

    loads[7].wait()
    value = [times("o2", split(states2[8 * c : 8 * c + 8].reshape(256, 256))) for c in range(2)]
    value = deep(jnp.concatenate([value[c][8 * x : 8 * x + 8] for x in range(16) for c in range(2)], 0), 0)
    level2[...] = value
    value = deep(times("o3", split(states3[0:8].reshape(256, 256))), 1)
    level3[...] = jnp.where(lax.broadcasted_iota(jnp.int32, (64, NZ), 1) < 64, value, 0.0)
    own = part("u1")[:, :192]
    for b in range(4):
        rows = slice(256 * b, 256 * b + 256)
        high, low = rawh[rows, :], rawl[rows, :]
        high, low = split(jnp.concatenate([timed((high[:, at : at + 128], low[:, at : at + 128]), "z1") for at in (0, 128)], 1))
        for p in range(4):
            at = slice(64 * p, 64 * p + 64)
            lines[4 * b + p] = dot(own, jnp.concatenate([high[at], low[at], high[at]], 0))
    for f in range(2):
        for t in range(4):
            value = lift_own([lines[i // 2, 32 * (i % 2) + 8 * t : 32 * (i % 2) + 8 * t + 8, 128 * f : 128 * f + 128] for i in range(N)])
            for i in range(N):
                own1[f, i, 8 * t : 8 * t + 8, :] = value[i]

    def wait_and_send(c):
        pl.semaphore_wait(relays.at[c], 1)
        copies[c].start()

    for c in (0, 1):
        pl.when(relayed[c])(lambda: wait_and_send(c))

    @pl.when(first_x)
    def _():
        pl.semaphore_wait(relays.at[5], 1)
        relay(0, 1)
        pl.when(inner_y)(lambda: relay(1, 1))
        edges[1].start()
        sides[1].start()

    pl.when(relayed[2])(lambda: wait_and_send(2))

    @pl.when(first_y)
    def _():
        pl.semaphore_wait(relays.at[4], 1)
        relay(1, 0)
        relay(1, 1)
        edges[3].start()
        sides[3].start()
        copies[1].start()
        pl.when(inner_x)(copies[3].start)

    pl.when(relayed[3])(lambda: wait_and_send(3))

    @pl.when(first_x & first_y)
    def _():
        pl.semaphore_wait(relays.at[6], 1)
        copies[3].start()

    for copy in sides:
        copy.wait()
    gains = (OPS[0][3], OPS[0][4])
    both = []
    for axis in range(2):
        value = [got_side[2 * axis + k, 64 * f : 64 * f + 64, :] for f in range(2) for k in range(2)]
        value = jnp.concatenate([jnp.concatenate(value[:2], 0), jnp.concatenate(value[2:], 0)], 1)
        value = times("x1", split(value))
        both.append(timed(split(jnp.concatenate([value[:, :128], value[:, 128:]], 0)), "z1"))
    got_side[0], got_side[1] = both[1][:128], both[1][128:]
    for f in range(2):
        for k, xs in enumerate(((0, 1, 2), (28, 29, 30, 31))):
            for x in xs:
                own1[f, x] += sum(float(gains[k][x, j]) * both[0][128 * f + 64 * k + 32 * j : 128 * f + 64 * k + 32 * j + 32] for j in range(2))
        for k in range(2):
            cols = [column(gains[k][:, j], 24 * k) for j in range(2)]
            for x in range(N):
                own1[f, x, 24 * k : 24 * k + 8, :] += sum(cols[j] * got_side[f, 64 * k + 32 * j + x : 64 * k + 32 * j + x + 1, :] for j in range(2))

    loads[8].wait()
    for c in range(4):
        pl.when(jnp.logical_not(relayed[c]))(lambda: pl.semaphore_wait(relays.at[c], 1))
    for copy in edges:
        copy.wait()
    for copy in copies:
        copy.wait_send()
    for c in (3, 2, 1, 0):
        copies[c].wait_recv()


def finish(own1, got_edge, got_corner, level2, level3, table4, out0_ref, out1_ref, even, odd, out_sem):
    part, times, _ = reader(None, None, None, None, table4)
    outs = (out0_ref, out1_ref)
    stores = []

    def store(at, source, target):
        stores.append(pltpu.make_async_copy(source, target, out_sem.at[at]))
        stores[-1].start()

    for f in range(2):
        store(f, own1.at[f, pl.ds(1, 13), 1], outs[f].at[pl.ds(1, 13), 1])

    parts2 = [got_edge[k, 0:48, :] for k in range(4)] + [got_corner[c, 8:24, :] for c in range(4)]
    value2 = times("m2", split(jnp.concatenate(parts2, 0))) + level2[...]
    parts3 = [got_edge[k, 48:64, :] for k in range(4)] + [got_corner[c, 24:32, :] for c in range(4)]
    parts3.append(jnp.zeros((32, NZ), jnp.float32))
    value3 = times("m3", split(jnp.concatenate(parts3, 0)))
    value3 = jnp.where(lax.broadcasted_iota(jnp.int32, (64, NZ), 1) < 64, value3[:64], value3[64:]) + level3[...]
    high, low = split(value2)
    value2 = dot(jnp.concatenate([high, low], 1), jnp.concatenate([part("p2")] * 2, 0))
    high, low = split(value3)
    value3 = dot(jnp.concatenate([high, low], 1), jnp.concatenate([part("p3")] * 2, 0))

    gains = (OPS[0][3], OPS[0][4])
    lane = lax.broadcasted_iota(jnp.int32, (16, NZ), 1)
    cols = [[column(gains[k][:, j], 24 * k) for j in range(2)] for k in range(2)]
    for f in range(2):

        def cornered(x):
            value = [own1[f, x // 2, x % 2, 8 * t : 8 * t + 8, :] for t in range(4)]
            for side, xs in enumerate(((0, 1, 2), (28, 29, 30, 31))):
                if x in xs:
                    for k in range(2):
                        for j in range(2):
                            row = sum(float(gains[side][x, i]) * got_corner[2 * side + k, 4 * f + 2 * j + i : 4 * f + 2 * j + i + 1, :] for i in range(2))
                            value[3 * k] += cols[k][j] * row
            return jnp.concatenate(value, 0)

        for i, x in enumerate((1, 29, 31)):
            odd[f, i] = cornered(x)
        store(2 + f, odd.at[f, 0], outs[f].at[0, 1])
        store(4 + f, odd.at[f, pl.ds(1, 2)], outs[f].at[pl.ds(14, 2), 1])
    for f in range(2):
        for p in range(16):
            even[f, p] = cornered(2 * p)
            cells = even[f, p, pl.ds(0, 16, stride=2), :]
            even[f, p, pl.ds(0, 16, stride=2), :] = jnp.where(lane % 2 == 0, value2[16 * p : 16 * p + 16, 128 * f : 128 * f + 128], cells)
            if p % 2 == 0:
                cells = even[f, p, pl.ds(0, 8, stride=4), :]
                even[f, p, pl.ds(0, 8, stride=4), :] = jnp.where(lane[:8] % 4 == 0, value3[4 * p : 4 * p + 8, 128 * f : 128 * f + 128], cells)
            if p % 8 == 7:
                here = pl.ds(p - 7, 8)
                store(6 + 2 * f + p // 8, even.at[f, here], outs[f].at[here, 0])
    for copy in stores:
        copy.wait()


def solution(mesh):
    nx, ny = mesh.shape["dx"], mesh.shape["dy"]
    f32, bf16 = jnp.float32, jnp.bfloat16

    def body(volume_fraction, vorticity):
        inputs = [volume_fraction, vorticity] + [jnp.asarray(table) for table in TABLES]
        inputs = [pltpu.with_memory_space_constraint(value, pltpu.HBM) for value in inputs]
        passed = (
            pltpu.VMEM((2, N, N, NZ), f32),
            pltpu.VMEM((4, 64, NZ), f32),
            pltpu.VMEM((4, 32, NZ), f32),
            pltpu.VMEM((256, NZ), f32),
            pltpu.VMEM((64, NZ), f32),
            pltpu.VMEM(TABLES[4].shape, bf16),
        )
        middle = pl.pallas_call(
            lambda *refs: exchange(nx, ny, *refs),
            out_shape=passed,
            in_specs=[pl.BlockSpec(memory_space=pltpu.HBM)] * 7,
            out_specs=(pl.BlockSpec(memory_space=pltpu.VMEM),) * 6,
            scratch_shapes=[
                pltpu.VMEM((2, N, N, NZ), f32),
                pltpu.VMEM(TABLES[0].shape, bf16),
                pltpu.VMEM(TABLES[1].shape, bf16),
                pltpu.VMEM(TABLES[2].shape, bf16),
                pltpu.VMEM(TABLES[3].shape, bf16),
                pltpu.VMEM((1024, 256), bf16),
                pltpu.VMEM((1024, 256), bf16),
                pltpu.VMEM((4, N, 256), f32),
                pltpu.VMEM((22, N, 256), f32),
                pltpu.VMEM((15, N, 256), f32),
                pltpu.VMEM((16, 64, 256), f32),
                pltpu.VMEM((4, 128, NZ), f32),
                pltpu.VMEM((4, 128, NZ), f32),
                pltpu.VMEM((4, 64, NZ), f32),
                pltpu.VMEM((4, 32, NZ), f32),
                pltpu.SemaphoreType.REGULAR((7,)),
                pltpu.SemaphoreType.DMA((13,)),
                pltpu.SemaphoreType.DMA((12,)),
                pltpu.SemaphoreType.DMA((12,)),
            ],
            compiler_params=pltpu.CompilerParams(
                collective_id=0, has_side_effects=True, vmem_limit_bytes=32 * 1024 * 1024
            ),
        )(*inputs)
        middle = [middle[0].reshape(2, 16, 2, N, NZ)] + list(middle[1:])
        middle = [pltpu.with_memory_space_constraint(value, pltpu.VMEM) for value in middle]
        block = pltpu.HBM((16, 2, N, NZ), f32)
        outs = pl.pallas_call(
            finish,
            out_shape=(block, block),
            in_specs=[pl.BlockSpec(memory_space=pltpu.VMEM)] * 6,
            out_specs=(pl.BlockSpec(memory_space=pltpu.HBM),) * 2,
            scratch_shapes=[
                pltpu.VMEM((2, 16, N, NZ), f32),
                pltpu.VMEM((2, 3, N, NZ), f32),
                pltpu.SemaphoreType.DMA((10,)),
            ],
            compiler_params=pltpu.CompilerParams(vmem_limit_bytes=32 * 1024 * 1024),
        )(*middle)
        return tuple(out.reshape(N, N, NZ) for out in outs)

    placed = P("dx", "dy", None)
    return jax.shard_map(
        body, mesh=mesh, in_specs=(placed, placed), out_specs=(placed, placed), check_vma=False
    )
```

```python
import jax
import jax.numpy as jnp
import numpy as np
from jax import lax
from jax.experimental import pallas as pl
from jax.experimental.pallas import tpu as pltpu
from jax.sharding import PartitionSpec as P

LEVELS = 3
LIFT_ALPHA = -1.586134342
LIFT_BETA = -0.05298011854
LIFT_GAMMA = 0.8829110762
LIFT_DELTA = 0.4435068522
LIFT_KAPPA = 1.149604398
MESH = pl.DeviceIdType.MESH
N = 32
NZ = 128
EDGE_ROWS = 208
CORNER_ROWS = 48


def lift_matrix(count, periodic):
    eye = np.eye(count)
    even, odd = eye[0::2], eye[1::2]
    if periodic:
        following = lambda t: np.roll(t, -1, 0)
        before = lambda t: np.roll(t, 1, 0)
    else:
        following = lambda t: np.concatenate([t[1:], t[-1:]])
        before = lambda t: np.concatenate([t[:1], t[:-1]])
    odd = odd + LIFT_ALPHA * (even + following(even))
    even = even + LIFT_BETA * (before(odd) + odd)
    odd = odd + LIFT_GAMMA * (even + following(even))
    even = even + LIFT_DELTA * (before(odd) + odd)
    out = np.zeros((count, count))
    out[0::2], out[1::2] = even / LIFT_KAPPA, odd * LIFT_KAPPA
    return out


def factor(matrix, rank):
    u, s, vt = np.linalg.svd(matrix)
    assert s[rank:].max() < 1e-12
    return u[:, :rank] * s[:rank], vt[:rank]


def axis_operators():
    found, current = [], np.eye(5 * N)
    for level, (up, down) in enumerate(((2, 2), (3, 3), (4, 3))):
        full = lift_matrix(current.shape[0], True) @ current
        size = N >> level
        rows = full[2 * size : 3 * size]
        gain_left, send_up = factor(rows[:, N : 2 * N], up)
        gain_right, send_down = factor(rows[:, 3 * N : 4 * N], down)
        found.append((rows[:, 2 * N : 3 * N], send_up, send_down, gain_left, gain_right))
        current = full[0::2]
    return found


def depth_operators():
    one = lift_matrix(NZ, False)
    two = lift_matrix(NZ // 2, False) @ one[0::2]
    three = lift_matrix(NZ // 4, False) @ two[0::2]
    return one, two, three


OPS = axis_operators()


def padded(matrix, rows):
    return np.concatenate([matrix, np.zeros((rows - matrix.shape[0],) + matrix.shape[1:])])


def blocks(matrix, count):
    return np.kron(np.eye(count), matrix)


def batched(matrix):
    rows, cols = matrix.shape
    out = np.zeros((rows, 8, 8, cols))
    for i in range(8):
        out[:, i, i, :] = matrix
    return out.reshape(rows * 8, 8 * cols)


def corner_matrix(up, down, stride, rows, split_lanes=False):
    sent = (up, down)
    total = len(up) + len(down)
    out = np.zeros((4, rows, total, N))
    for corner in range(4):
        sx, sy = corner // 2, corner % 2
        for jy in range(len(sent[sy])):
            for jx, line in enumerate(sent[sx]):
                at = 8 * (jx % 2) + 2 * jy + jx // 2 if split_lanes else stride * jy + jx
                out[corner, at, sy * len(up) + jy] = line
        if rows == 8:
            out[corner, 4:] = out[corner, :4]
    return out.reshape(4 * rows, total * N)


def gain_matrix(level):
    gains = OPS[level][3:]
    size = N >> level
    eye = np.eye(size)
    if level == 2:
        gains = [np.pad(gain, ((0, 0), (0, 4 - gain.shape[1]))) for gain in gains]
    parts = [np.einsum("xj,yv->xyjv", gain, eye).reshape(size * size, -1) for gain in gains]
    parts += [np.einsum("yj,xv->xyjv", gain, eye).reshape(size * size, -1) for gain in gains]
    four = [np.pad(gain, ((0, 0), (0, 4 - gain.shape[1]))) for gain in gains]
    for corner in range(4):
        parts.append(np.einsum("xi,yj->xyji", four[corner // 2], four[corner % 2]).reshape(size * size, 16))
    if level == 2:
        for i, width in enumerate([8] * 4 + [1] * 4):
            states = parts[i].reshape(size * size, -1, 2, width)
            parts[i] = np.concatenate([states[:, :, half].reshape(size * size, -1) for half in range(2)])
        out = np.concatenate(parts, 1)
        return np.pad(out, ((0, 0), (0, 128 - out.shape[1])))
    return wide(np.concatenate(parts, 1))


def halves(matrix):
    high = np.asarray(matrix, jnp.bfloat16)
    low = np.asarray(matrix - high.astype(np.float64), jnp.bfloat16)
    return high, low


def wide(matrix):
    return np.pad(matrix, ((0, 0), (0, 256 - matrix.shape[1])))


def tables():
    one, two, three = depth_operators()
    depth = np.zeros((2, NZ, 256))
    for f in range(2):
        depth[f, :, 64 * f : 64 * f + 64] = two.T
        for half in (128, 192):
            depth[f, :, half + 32 * f : half + 32 * f + 32] = three.T
    own = [ops[0] for ops in OPS]
    up = [ops[1] for ops in OPS]
    down = [ops[2] for ops in OPS]
    sent = [np.concatenate([p, q]) for p, q in zip(up, down)]
    spread2 = np.zeros((2, 64, 2, NZ))
    spread3 = np.zeros((4, 32, 2, NZ))
    for f in range(2):
        for i in range(64):
            spread2[f, i, f, 2 * i] = 1
        for i in range(32):
            spread3[f, i, f, 4 * i] = spread3[2 + f, i, f, 4 * i] = 1
    groups = [
        {"ys": batched(np.concatenate(sent))},
        {
            "c1": corner_matrix(up[0], down[0], 2, 8),
            "c23": np.concatenate([wide(corner_matrix(up[1], down[1], 4, 16)), wide(corner_matrix(up[2], down[2], 4, 16, True))]),
            "z1": one.T,
            "z23": depth.reshape(256, 256),
        },
        {
            "yo": batched(np.concatenate(own[1:])),
            "e2": batched(sent[1]),
            "e3": batched(sent[2]),
            "n23": np.concatenate([wide(blocks(own[1], 6)), wide(blocks(own[2], 7))]),
        },
        {"o2": batched(own[1]), "o3": batched(own[2]), "x1": blocks(own[0], 4)},
        {"m2": gain_matrix(1), "m3": gain_matrix(2)},
    ]
    packed, where = [], {}
    for group, pairs in enumerate(groups):
        arrays = []

        def put(name, array):
            extra = -array.shape[0] % 16
            where[name] = (group, sum(len(other) for other in arrays), array.shape[0] + extra)
            arrays.append(np.pad(array, ((0, extra), (0, 0))))

        for name, matrix in pairs.items():
            high, low = halves(matrix)
            if name == "ys":
                put(name, np.concatenate([np.pad(half, ((0, 8), (0, 0))) for half in (high, low)]))
            elif matrix.shape[1] == 128:
                put(name, np.concatenate([high, low], 1))
            else:
                put(name + "h", high)
                put(name + "l", low)
        if group == 3:
            high, low = halves(blocks(own[0], 2))
            put("u1", wide(np.concatenate([high, high, low], 1)))
        if group == 4:
            put("p2", np.asarray(spread2.reshape(128, 256), jnp.bfloat16))
            put("p3", np.asarray(spread3.reshape(128, 256), jnp.bfloat16))
        packed.append(np.concatenate(arrays))
    return packed, where


TABLES, WHERE = tables()


def split(value):
    high = value.astype(jnp.bfloat16)
    return high, (value - high.astype(jnp.float32)).astype(jnp.bfloat16)


def dot(a, b):
    return jnp.dot(a, b, preferred_element_type=jnp.float32)


def column(gain, first):
    row = lax.broadcasted_iota(jnp.int32, (8, NZ), 0)
    out = jnp.zeros((8, NZ), jnp.float32)
    for i in range(8):
        if abs(gain[first + i]) > 1e-13:
            out = jnp.where(row == i, jnp.float32(gain[first + i]), out)
    return out


def lift_own(lines):
    pairs = N // 2
    even = lines[0::2]
    odd = lines[1::2]
    zero = jnp.zeros_like(even[0])
    odd = [LIFT_ALPHA * even[0]] + [odd[i] + LIFT_ALPHA * (even[i] + (even[i + 1] if i + 1 < pairs else zero)) for i in range(pairs)]
    even = [LIFT_BETA * odd[0]] + [even[i] + LIFT_BETA * (odd[i] + odd[i + 1]) for i in range(pairs)] + [LIFT_BETA * odd[pairs]]
    odd = [odd[i] + LIFT_GAMMA * (even[i] + even[i + 1]) for i in range(pairs + 1)]
    out = []
    for i in range(pairs):
        out.append((even[i + 1] + LIFT_DELTA * (odd[i] + odd[i + 1])) * (1.0 / LIFT_KAPPA))
        out.append(odd[i + 1] * LIFT_KAPPA)
    return out


def both_of(part, name):
    if name in WHERE:
        return part(name)[:, :128], part(name)[:, 128:]
    return part(name + "h"), part(name + "l")


def reader(*refs):
    def part(name):
        group, at, rows = WHERE[name]
        return refs[group][at : at + rows, :]

    def times(name, pair):
        (ah, al), (bh, bl) = both_of(part, name), pair
        value = dot(jnp.concatenate([ah, al], 0), bh)
        return value[: ah.shape[0]] + value[ah.shape[0] :] + dot(ah, bl)

    def timed(pair, name):
        (ah, al), (bh, bl) = pair, both_of(part, name)
        value = dot(jnp.concatenate([ah, al], 0), bh)
        return value[: ah.shape[0]] + value[ah.shape[0] :] + dot(ah, bl)

    return part, times, timed


def exchange(nx, ny, v0_ref, v1_ref, table0_ref, table1_ref, table2_ref, table3_ref, table4_ref, own1, got_edge, got_corner, level2, level3, table4, fields, table0, table1, table2, table3, rawh, rawl, states1, states2, states3, lines, send_side, got_side, send_edge, send_corner, relays, in_sem, send_sem, recv_sem):
    loads = []

    def load(source, target):
        loads.append(pltpu.make_async_copy(source, target, in_sem.at[len(loads)]))
        loads[-1].start()

    load(table0_ref, table0)
    for b in range(2):
        for f, ref in enumerate((v0_ref, v1_ref)):
            load(ref.at[pl.ds(16 * b, 16)], fields.at[f, pl.ds(16 * b, 16)])
    load(table1_ref, table1)
    ix, iy = lax.axis_index("dx"), lax.axis_index("dy")
    right, left = lax.rem(ix + 1, nx), lax.rem(ix + nx - 1, nx)
    above, below = lax.rem(iy + 1, ny), lax.rem(iy + ny - 1, ny)
    edge_to = [(right, iy), (left, iy), (ix, above), (ix, below)]
    corner_to = [(right, above), (right, below), (left, above), (left, below)]


    def rank(tx, ty):
        return 3 * tx + 2 * ty + 20 * lax.div(2 * ty, ny)

    earlier = [rank(tx, ty) < rank(ix, iy) for tx, ty in corner_to]
    barrier = pltpu.get_barrier_semaphore()
    for there, first in zip(corner_to, earlier):

        @pl.when(jnp.logical_not(first))
        def _():
            pl.semaphore_signal(barrier, inc=1, device_id=there, device_id_type=MESH)

    first_x, last_x, first_y, last_y = ix == 0, ix == nx - 1, iy == 0, iy == ny - 1
    inner_x, inner_y = jnp.logical_not(first_x), jnp.logical_not(first_y)
    relayed = [jnp.logical_not(e) for e in (earlier[0], earlier[1] | first_y, earlier[2], earlier[3] | first_y)]
    for k, say in ((3, None), (1, None), (2, jnp.logical_not(last_y)), (0, jnp.logical_not(last_x))):

        def signal():
            pl.semaphore_signal(barrier, inc=1, device_id=edge_to[k], device_id_type=MESH)

        signal() if say is None else pl.when(say)(signal)

    part, times, timed = reader(table0, table1, table2, table3)

    def copy_to(at, source, target, there):
        return pltpu.make_async_remote_copy(src_ref=source, dst_ref=target, send_sem=send_sem.at[at], recv_sem=recv_sem.at[at], device_id=there, device_id_type=MESH)

    loads[0].wait()
    for b in range(4):
        here = slice(8 * b, 8 * b + 8)
        if b % 2 == 0:
            loads[2 * (b // 2) + 1].wait()
            loads[2 * (b // 2) + 2].wait()
        raw = split(jnp.concatenate([fields[f, here].reshape(256, NZ) for f in range(2)], 1))
        rawh[256 * b : 256 * b + 256, :], rawl[256 * b : 256 * b + 256, :] = raw
        value = dot(part("ys"), raw[0])
        value = (value[:144] + value[144:] + dot(part("ys")[:144], raw[1])).reshape(18, 8, 256)
        states1[:, here, :] = value[:4]
        states2[16:22, here, :] = value[4:10]
        states3[8:15, here, :] = value[10:17]
    for f in range(2):
        for j in range(2):
            at = slice(64 * f + 32 * j, 64 * f + 32 * j + 32)
            send_side[0, at, :] = sum(float(OPS[0][1][j, 28 + i]) * fields[f, 28 + i] for i in range(4))
            send_side[1, at, :] = sum(float(OPS[0][2][j, i]) * fields[f, i] for i in range(3))
    for k in range(2):
        for f in range(2):
            send_side[2 + k, 64 * f : 64 * f + 64, :] = states1[2 * k : 2 * k + 2, :, 128 * f : 128 * f + 128].reshape(64, NZ)
    for source, target in ((table2_ref, table2), (table3_ref, table3), (table4_ref, table4)):
        load(source, target)
    def answer(at, k):
        pl.semaphore_signal(relays.at[at], inc=1, device_id=edge_to[k], device_id_type=MESH)

    def relay(below, k):
        answer(2 - 2 * k + below, k)

    pl.semaphore_wait(barrier, 2 + inner_x.astype(jnp.int32) + inner_y.astype(jnp.int32) + sum(first.astype(jnp.int32) for first in earlier))
    pl.when(last_y)(lambda: answer(4, 2))
    pl.when(last_x)(lambda: answer(5, 0))

    @pl.when(last_x & last_y)
    def _():
        pl.semaphore_signal(relays.at[6], inc=1, device_id=corner_to[0], device_id_type=MESH)

    relay(0, 0)
    pl.when(inner_x)(lambda: relay(0, 1))
    pl.when(inner_y)(lambda: relay(1, 0))
    pl.when(inner_x & inner_y)(lambda: relay(1, 1))
    sides = [copy_to(8 + k, send_side.at[k], got_side.at[k], edge_to[k]) for k in range(4)]

    def start_inner(group):
        group[0].start()
        group[2].start()
        pl.when(inner_x)(group[1].start)
        pl.when(inner_y)(group[3].start)

    start_inner(sides)

    loads[5].wait()
    zh, zl = both_of(part, "z23")

    def deep(value, half):
        return deep_of(split(value), half)

    def deep_of(pair, half):
        high, low = pair
        at = slice(128 * half, 128 * half + 128)
        value = dot(jnp.concatenate([high, low], 0), zh[:, at])
        return value[: high.shape[0]] + value[high.shape[0] :] + dot(high, zl[:, at])

    lines2 = split(states2[16:22].reshape(192, 256))
    lines3 = split(states3[8:15].reshape(224, 256))
    deep2 = jnp.concatenate([deep_of(lines2, 0), jnp.zeros((64, NZ), jnp.float32)], 0)
    deep3 = jnp.concatenate([deep_of(lines3, 1), jnp.zeros((32, NZ), jnp.float32)], 0)
    both = split(jnp.concatenate([deep2, deep3], 1))
    value = times("c23", both)
    corners1 = times("c1", split(states1[...].reshape(128, 256)))
    corners1 = timed(split(jnp.concatenate([corners1[:, :128], corners1[:, 128:]], 0)), "z1")
    corners2, corners3 = value[:64, :128], value[64:, 128:]
    along_y = both
    row = lax.broadcasted_iota(jnp.int32, (8, NZ), 0)
    lane = lax.broadcasted_iota(jnp.int32, (8, NZ), 1)

    def beside(value, at):
        return jnp.where(lane < 64, value[at : at + 8], value[at + 8 : at + 16])

    for c in range(4):
        send_corner[c, 0:8, :] = jnp.where(row < 4, corners1[8 * c : 8 * c + 8], corners1[32 + 8 * c : 40 + 8 * c])
        send_corner[c, 8:24, :] = corners2[16 * c : 16 * c + 16]
        send_corner[c, 24:32, :] = beside(corners3, 16 * c)
    copies = [copy_to(c, send_corner.at[c], got_corner.at[c], corner_to[c]) for c in range(4)]
    for c in range(4):
        pl.when(earlier[c])(copies[c].start)
    loads[6].wait()
    for b in range(4):
        here = slice(8 * b, 8 * b + 8)
        raw = rawh[256 * b : 256 * b + 256, :], rawl[256 * b : 256 * b + 256, :]
        value = times("yo", raw).reshape(24, 8, 256)
        states2[0:16, here, :] = value[:16]
        states3[0:8, here, :] = value[16:]
    value = [times("e2", split(states2[8 * c : 8 * c + 8].reshape(256, 256))) for c in range(2)]
    rows2 = [value[c][8 * j : 8 * j + 8] for j in range(6) for c in range(2)]
    rows3 = times("e3", split(states3[0:8].reshape(256, 256)))[:56]
    sides_y = times("n23", along_y)
    value = deep(jnp.concatenate(rows2, 0), 0)
    for k in range(2):
        send_edge[k, 0:48, :] = value[48 * k : 48 * k + 48]
        send_edge[2 + k, 0:48, :] = sides_y[48 * k : 48 * k + 48, :128]
    value = jnp.concatenate([deep(rows3, 1), sides_y[96:152, 128:]], 0)
    for axis in range(2):
        at = 56 * axis
        send_edge[2 * axis, 48:56, :] = beside(value, at)
        send_edge[2 * axis, 56:64, :] = beside(value, at + 16)
        send_edge[2 * axis + 1, 48:56, :] = beside(value, at + 32)
        send_edge[2 * axis + 1, 56:64, :] = jnp.where(lane < 64, value[at + 48 : at + 56], 0.0)
    edges = [copy_to(4 + k, send_edge.at[k], got_edge.at[k], edge_to[k]) for k in range(4)]
    start_inner(edges)

    loads[7].wait()
    value = [times("o2", split(states2[8 * c : 8 * c + 8].reshape(256, 256))) for c in range(2)]
    value = deep(jnp.concatenate([value[c][8 * x : 8 * x + 8] for x in range(16) for c in range(2)], 0), 0)
    level2[...] = value
    value = deep(times("o3", split(states3[0:8].reshape(256, 256))), 1)
    level3[...] = jnp.where(lax.broadcasted_iota(jnp.int32, (64, NZ), 1) < 64, value, 0.0)
    own = part("u1")[:, :192]
    for b in range(4):
        rows = slice(256 * b, 256 * b + 256)
        high, low = rawh[rows, :], rawl[rows, :]
        high, low = split(jnp.concatenate([timed((high[:, at : at + 128], low[:, at : at + 128]), "z1") for at in (0, 128)], 1))
        for p in range(4):
            at = slice(64 * p, 64 * p + 64)
            lines[4 * b + p] = dot(own, jnp.concatenate([high[at], low[at], high[at]], 0))
    for f in range(2):
        for t in range(4):
            value = lift_own([lines[i // 2, 32 * (i % 2) + 8 * t : 32 * (i % 2) + 8 * t + 8, 128 * f : 128 * f + 128] for i in range(N)])
            for i in range(N):
                own1[f, i, 8 * t : 8 * t + 8, :] = value[i]

    def wait_and_send(c):
        pl.semaphore_wait(relays.at[c], 1)
        copies[c].start()

    for c in (0, 1):
        pl.when(relayed[c])(lambda: wait_and_send(c))

    @pl.when(first_x)
    def _():
        pl.semaphore_wait(relays.at[5], 1)
        relay(0, 1)
        pl.when(inner_y)(lambda: relay(1, 1))
        edges[1].start()
        sides[1].start()

    pl.when(relayed[2])(lambda: wait_and_send(2))

    @pl.when(first_y)
    def _():
        pl.semaphore_wait(relays.at[4], 1)
        relay(1, 0)
        relay(1, 1)
        edges[3].start()
        sides[3].start()
        copies[1].start()
        pl.when(inner_x)(copies[3].start)

    pl.when(relayed[3])(lambda: wait_and_send(3))

    @pl.when(first_x & first_y)
    def _():
        pl.semaphore_wait(relays.at[6], 1)
        copies[3].start()

    for copy in sides:
        copy.wait_recv()
    gains = (OPS[0][3], OPS[0][4])
    both = []
    for axis in range(2):
        value = [got_side[2 * axis + k, 64 * f : 64 * f + 64, :] for f in range(2) for k in range(2)]
        value = jnp.concatenate([jnp.concatenate(value[:2], 0), jnp.concatenate(value[2:], 0)], 1)
        value = times("x1", split(value))
        both.append(timed(split(jnp.concatenate([value[:, :128], value[:, 128:]], 0)), "z1"))
    got_side[0], got_side[1] = both[1][:128], both[1][128:]
    for f in range(2):
        for k, xs in enumerate(((0, 1, 2), (28, 29, 30, 31))):
            for x in xs:
                own1[f, x] += sum(float(gains[k][x, j]) * both[0][128 * f + 64 * k + 32 * j : 128 * f + 64 * k + 32 * j + 32] for j in range(2))
        for k in range(2):
            cols = [column(gains[k][:, j], 24 * k) for j in range(2)]
            for x in range(N):
                own1[f, x, 24 * k : 24 * k + 8, :] += sum(cols[j] * got_side[f, 64 * k + 32 * j + x : 64 * k + 32 * j + x + 1, :] for j in range(2))

    loads[8].wait()
    for c in range(4):
        pl.when(jnp.logical_not(relayed[c]))(lambda: pl.semaphore_wait(relays.at[c], 1))
    for copy in edges:
        copy.wait()
    for copy in copies + sides:
        copy.wait_send()
    for c in (3, 2, 1, 0):
        copies[c].wait_recv()


def finish(own1, got_edge, got_corner, level2, level3, table4, out0_ref, out1_ref, even, odd, out_sem):
    part, times, _ = reader(None, None, None, None, table4)
    outs = (out0_ref, out1_ref)
    stores = []

    def store(at, source, target):
        stores.append(pltpu.make_async_copy(source, target, out_sem.at[at]))
        stores[-1].start()

    for f in range(2):
        store(f, own1.at[f, pl.ds(1, 13), 1], outs[f].at[pl.ds(1, 13), 1])

    parts2 = [got_edge[k, 0:48, :] for k in range(4)] + [got_corner[c, 8:24, :] for c in range(4)]
    value2 = times("m2", split(jnp.concatenate(parts2, 0))) + level2[...]
    parts3 = [got_edge[k, 48:64, :] for k in range(4)] + [got_corner[c, 24:32, :] for c in range(4)]
    parts3.append(jnp.zeros((32, NZ), jnp.float32))
    value3 = times("m3", split(jnp.concatenate(parts3, 0)))
    value3 = jnp.where(lax.broadcasted_iota(jnp.int32, (64, NZ), 1) < 64, value3[:64], value3[64:]) + level3[...]
    high, low = split(value2)
    value2 = dot(jnp.concatenate([high, low], 1), jnp.concatenate([part("p2")] * 2, 0))
    high, low = split(value3)
    value3 = dot(jnp.concatenate([high, low], 1), jnp.concatenate([part("p3")] * 2, 0))

    gains = (OPS[0][3], OPS[0][4])
    lane = lax.broadcasted_iota(jnp.int32, (16, NZ), 1)
    cols = [[column(gains[k][:, j], 24 * k) for j in range(2)] for k in range(2)]
    for f in range(2):

        def cornered(x):
            value = [own1[f, x // 2, x % 2, 8 * t : 8 * t + 8, :] for t in range(4)]
            for side, xs in enumerate(((0, 1, 2), (28, 29, 30, 31))):
                if x in xs:
                    for k in range(2):
                        for j in range(2):
                            row = sum(float(gains[side][x, i]) * got_corner[2 * side + k, 4 * f + 2 * j + i : 4 * f + 2 * j + i + 1, :] for i in range(2))
                            value[3 * k] += cols[k][j] * row
            return jnp.concatenate(value, 0)

        for i, x in enumerate((1, 29, 31)):
            odd[f, i] = cornered(x)
        store(2 + f, odd.at[f, 0], outs[f].at[0, 1])
        store(4 + f, odd.at[f, pl.ds(1, 2)], outs[f].at[pl.ds(14, 2), 1])
    for f in range(2):
        for p in range(16):
            even[f, p] = cornered(2 * p)
            cells = even[f, p, pl.ds(0, 16, stride=2), :]
            even[f, p, pl.ds(0, 16, stride=2), :] = jnp.where(lane % 2 == 0, value2[16 * p : 16 * p + 16, 128 * f : 128 * f + 128], cells)
            if p % 2 == 0:
                cells = even[f, p, pl.ds(0, 8, stride=4), :]
                even[f, p, pl.ds(0, 8, stride=4), :] = jnp.where(lane[:8] % 4 == 0, value3[4 * p : 4 * p + 8, 128 * f : 128 * f + 128], cells)
            if p % 8 == 7:
                here = pl.ds(p - 7, 8)
                store(6 + 2 * f + p // 8, even.at[f, here], outs[f].at[here, 0])
    for copy in stores:
        copy.wait()


def solution(mesh):
    nx, ny = mesh.shape["dx"], mesh.shape["dy"]
    f32, bf16 = jnp.float32, jnp.bfloat16

    def body(volume_fraction, vorticity):
        inputs = [volume_fraction, vorticity] + [jnp.asarray(table) for table in TABLES]
        inputs = [pltpu.with_memory_space_constraint(value, pltpu.HBM) for value in inputs]
        passed = (
            pltpu.VMEM((2, N, N, NZ), f32),
            pltpu.VMEM((4, 64, NZ), f32),
            pltpu.VMEM((4, 32, NZ), f32),
            pltpu.VMEM((256, NZ), f32),
            pltpu.VMEM((64, NZ), f32),
            pltpu.VMEM(TABLES[4].shape, bf16),
        )
        middle = pl.pallas_call(
            lambda *refs: exchange(nx, ny, *refs),
            out_shape=passed,
            in_specs=[pl.BlockSpec(memory_space=pltpu.HBM)] * 7,
            out_specs=(pl.BlockSpec(memory_space=pltpu.VMEM),) * 6,
            scratch_shapes=[
                pltpu.VMEM((2, N, N, NZ), f32),
                pltpu.VMEM(TABLES[0].shape, bf16),
                pltpu.VMEM(TABLES[1].shape, bf16),
                pltpu.VMEM(TABLES[2].shape, bf16),
                pltpu.VMEM(TABLES[3].shape, bf16),
                pltpu.VMEM((1024, 256), bf16),
                pltpu.VMEM((1024, 256), bf16),
                pltpu.VMEM((4, N, 256), f32),
                pltpu.VMEM((22, N, 256), f32),
                pltpu.VMEM((15, N, 256), f32),
                pltpu.VMEM((16, 64, 256), f32),
                pltpu.VMEM((4, 128, NZ), f32),
                pltpu.VMEM((4, 128, NZ), f32),
                pltpu.VMEM((4, 64, NZ), f32),
                pltpu.VMEM((4, 32, NZ), f32),
                pltpu.SemaphoreType.REGULAR((7,)),
                pltpu.SemaphoreType.DMA((13,)),
                pltpu.SemaphoreType.DMA((12,)),
                pltpu.SemaphoreType.DMA((12,)),
            ],
            compiler_params=pltpu.CompilerParams(
                collective_id=0, has_side_effects=True, vmem_limit_bytes=32 * 1024 * 1024
            ),
        )(*inputs)
        middle = [middle[0].reshape(2, 16, 2, N, NZ)] + list(middle[1:])
        middle = [pltpu.with_memory_space_constraint(value, pltpu.VMEM) for value in middle]
        block = pltpu.HBM((16, 2, N, NZ), f32)
        outs = pl.pallas_call(
            finish,
            out_shape=(block, block),
            in_specs=[pl.BlockSpec(memory_space=pltpu.VMEM)] * 6,
            out_specs=(pl.BlockSpec(memory_space=pltpu.HBM),) * 2,
            scratch_shapes=[
                pltpu.VMEM((2, 16, N, NZ), f32),
                pltpu.VMEM((2, 3, N, NZ), f32),
                pltpu.SemaphoreType.DMA((10,)),
            ],
            compiler_params=pltpu.CompilerParams(vmem_limit_bytes=32 * 1024 * 1024),
        )(*middle)
        return tuple(out.reshape(N, N, NZ) for out in outs)

    placed = P("dx", "dy", None)
    return jax.shard_map(
        body, mesh=mesh, in_specs=(placed, placed), out_specs=(placed, placed), check_vma=False
    )
```
